32 devices in a mesh: dp: 4 (over y, x), row: 2 (over core), col: 4 (over z).
Axes of the slice: x: 2, y: 2, z: 4, core: 2. Of those that a mesh axis runs over, the one named last changes fastest.
Arguments:
- layer_input: bfloat16 [4096, 2048], P(('dp', 'row'), 'col'), may hold values from -6 to 6
- doc_ids: int32 [4096], P('dp'), may hold values from 0 to 3, as said below
- positions: int32 [4096], P('dp'), may hold values from 0 to 1023, as said below
- w_query: bfloat16 [2048, 2048], P('col', 'row'), may hold values from -0.125 to 0.125
- w_key: bfloat16 [2048, 2048], P('col', 'row'), may hold values from -0.125 to 0.125
- w_value: bfloat16 [2048, 2048], P('col', 'row'), may hold values from -0.125 to 0.125
- w_out: bfloat16 [2048, 2048], P('row', 'col'), may hold values from -0.125 to 0.125
- w_gate: bfloat16 [2048, 8192], P('col', 'row'), may hold values from -0.125 to 0.125
- w_up: bfloat16 [2048, 8192], P('col', 'row'), may hold values from -0.125 to 0.125
- w_down: bfloat16 [8192, 2048], P('row', 'col'), may hold values from -0.0625 to 0.0625
- gain_query: float32 [2048], P(('row', 'col')), may hold values from 0.1 to 1.9
- gain_key: float32 [2048], P(('row', 'col')), may hold values from 0.1 to 1.9
- gain_attn: float32 [2048], P('col'), may hold values from 0.1 to 1.9
- gain_ffn: float32 [2048], P('col'), may hold values from 0.1 to 1.9
- grad_output: bfloat16 [4096, 2048], P(('dp', 'row'), 'col'), may hold values from -6 to 6
Outputs:
- layer_output: bfloat16 [4096, 2048], P(('dp', 'row'), 'col')
- grad_input: float32 [4096, 2048], P(('dp', 'row'), 'col')
- grad_w_query: float32 [2048, 2048], P('col', 'row')
- grad_w_key: float32 [2048, 2048], P('col', 'row')
- grad_w_value: float32 [2048, 2048], P('col', 'row')
- grad_w_out: float32 [2048, 2048], P('row', 'col')
- grad_w_gate: float32 [2048, 8192], P('col', 'row')
- grad_w_up: float32 [2048, 8192], P('col', 'row')
- grad_w_down: float32 [8192, 2048], P('row', 'col')
- grad_gain_query: float32 [2048], P(('row', 'col'))
- grad_gain_key: float32 [2048], P(('row', 'col'))
- grad_gain_attn: float32 [2048], P('col')
- grad_gain_ffn: float32 [2048], P('col')
The draws below stay inside these ranges and needn't reach their ends.
Inputs may be any that keep to these rules, and one draw needn't show every extreme that they name: `doc_ids`: within each group of 1024 consecutive slots the number never falls from slot to slot; a group holds 1 to 4 sequences, and in some group a single sequence fills all 1024 slots. `positions`: each sequence starts at position 0 and the position rises by one from slot to slot within it.
All inputs are finite; a program needn't handle non-finite values.
Results may differ from the reference program's by a relative error of at most 0.019.
Values may be sent and summed in bfloat16 or wider, within the bound.
No kernel may reach another device: no remote copies, remote signals or barrier semaphores. Data moves between devices by JAX's collectives and lax.ppermute only.
A program may use at most 192 MiB of HBM per device.

```python
import jax
import jax.numpy as jnp
from jax import lax

D = 2048
FF = 8192
HEAD = 128
TOK_DP = 1024
HEADS = 16
TOKENS = 4096
N_DP = 4


def sequence_layout(key):
    groups = TOKENS // TOK_DP
    group_index = jnp.arange(groups)
    lonely = jax.random.randint(jax.random.fold_in(key, 101), (), 0, groups)
    crowded = (lonely + 1) % groups
    boundary = jax.random.randint(jax.random.fold_in(key, 102), (groups, 3), 1, TOK_DP)
    switched = jax.random.randint(jax.random.fold_in(key, 103), (groups, 3), 0, 2)
    switched = jnp.where(group_index[:, None] == lonely, 0, switched)
    switched = jnp.where(group_index[:, None] == crowded, 1, switched)
    boundary = jnp.where(switched == 1, boundary, TOK_DP)
    slot_index = jnp.arange(TOK_DP)
    passed = slot_index[None, :, None] >= boundary[:, None, :]
    documents = jnp.sum(passed.astype(jnp.int32), axis=2).astype(jnp.int32)
    openings = jnp.max(jnp.where(passed, boundary[:, None, :], 0), axis=2)
    placed = slot_index[None, :] - openings
    return (documents.reshape(TOKENS).astype(jnp.int32), placed.reshape(TOKENS).astype(jnp.int32))


def draw_doc_ids(key, part):
    layout = sequence_layout(key)
    return layout[0]


def draw_positions(key, part):
    layout = sequence_layout(key)
    return layout[1]


def level_of(stream_key, extent, split, low, high):
    level, own = 1.0, jax.random.fold_in(stream_key, 6)
    for axis_at, blocks in split:
        heights = jnp.exp(jax.random.uniform(jax.random.fold_in(own, axis_at), (blocks,), jnp.float32, low / len(split), high / len(split)))
        level = level * jnp.repeat(heights, extent[axis_at] // blocks).reshape([-1 if axis == axis_at else 1 for axis in range(len(extent))])
    return level


def scatter_about(rng, shape, scale, reach, shards=(), kind=jnp.bfloat16):
    gain = level_of(rng, shape, shards, -0.22, 0.18) if shards else 1.0
    array = jax.random.normal(rng, shape, jnp.float32) * scale * gain
    return jnp.minimum(jnp.maximum(array, -reach), reach).astype(kind)


def setup_inputs(seed: int = 0) -> dict:
    arg_keys = jax.random.split(jax.random.key(seed), 16)
    return {
        "layer_input": scatter_about(arg_keys[0], (TOKENS, D), 1.0, 6.0, ((0, 8), (1, 4))),
        "doc_ids": draw_doc_ids(jax.random.fold_in(arg_keys[15], 71), 0),
        "positions": draw_positions(jax.random.fold_in(arg_keys[15], 71), 0),
        "w_query": scatter_about(arg_keys[3], (D, D), D ** -0.5, 0.125, ((0, 4), (1, 2))),
        "w_key": scatter_about(arg_keys[4], (D, D), D ** -0.5, 0.125, ((0, 4), (1, 2))),
        "w_value": scatter_about(arg_keys[5], (D, D), D ** -0.5, 0.125, ((0, 4), (1, 2))),
        "w_out": scatter_about(arg_keys[6], (D, D), D ** -0.5, 0.125, ((0, 2), (1, 4))),
        "w_gate": scatter_about(arg_keys[7], (D, FF), D ** -0.5, 0.125, ((0, 4), (1, 2))),
        "w_up": scatter_about(arg_keys[8], (D, FF), D ** -0.5, 0.125, ((0, 4), (1, 2))),
        "w_down": scatter_about(arg_keys[9], (FF, D), FF ** -0.5, 0.0625, ((0, 2), (1, 4))),
        "gain_query": jnp.clip(1.0 + 0.18 * jax.random.normal(arg_keys[10], (D,), jnp.float32), 0.1, 1.9),
        "gain_key": jnp.clip(1.0 + 0.18 * jax.random.normal(arg_keys[11], (D,), jnp.float32), 0.1, 1.9),
        "gain_attn": jnp.clip(1.0 + 0.18 * jax.random.normal(arg_keys[12], (D,), jnp.float32), 0.1, 1.9),
        "gain_ffn": jnp.clip(1.0 + 0.18 * jax.random.normal(arg_keys[13], (D,), jnp.float32), 0.1, 1.9),
        "grad_output": scatter_about(arg_keys[14], (TOKENS, D), 1.0, 6.0, ((0, 8), (1, 4))),
    }


EPSILON = 1e-06
ROPE_BASE = 500000.0
MASKED = -1e+30

@jax.custom_vjp
def low(v):
    return lax.optimization_barrier(v.astype(jnp.bfloat16)).astype(jnp.float32)

@jax.custom_vjp
def low_back(v):
    return v

def low_keep(v):
    return (low(v), None)

def low_pass(kept, grad):
    return (grad,)

def back_keep(v):
    return (v, None)

def back_low(kept, grad):
    return (low(grad),)
low.defvjp(low_keep, low_pass)
low_back.defvjp(back_keep, back_low)

def product(left_side, right_side):
    return jnp.dot(left_side, right_side, precision=lax.Precision.HIGHEST, preferred_element_type=jnp.float32)

def inverse_rms(values):
    return lax.rsqrt(lax.optimization_barrier(jnp.mean(values * values, axis=-1, keepdims=True)) + EPSILON)

def rope_tables(positions):
    frequency = ROPE_BASE ** (-(jnp.arange(HEAD // 2, dtype=jnp.float32) * (2.0 / HEAD)))
    angles = positions.astype(jnp.float32)[:, None] * frequency[None, :]
    return (jnp.cos(angles)[:, None, :], jnp.sin(angles)[:, None, :])

def rotate(values, cosine_table, sine_table):
    middle = HEAD // 2
    first_half = values[..., :middle]
    second_half = values[..., middle:]
    return jnp.concatenate([first_half * cosine_table - second_half * sine_table, second_half * cosine_table + first_half * sine_table], axis=-1)

def group_attention(inputs):
    queries, key_rows, value_rows, documents = inputs
    slot_index = jnp.arange(TOK_DP)
    allowed = (documents[:, None] == documents[None, :]) & (slot_index[None, :] <= slot_index[:, None])
    scores = jnp.einsum('qhd,khd->hqk', queries, key_rows, precision=lax.Precision.HIGHEST) * HEAD ** (-0.5)
    scores = low_back(scores)
    scores = jnp.where(allowed[None], scores, MASKED)
    largest = lax.optimization_barrier(jnp.max(scores, axis=-1, keepdims=True))
    weights = jnp.exp(scores - largest)
    chances = low(weights / lax.optimization_barrier(jnp.sum(weights, axis=-1, keepdims=True)))
    return jnp.einsum('hqk,khd->qhd', chances, value_rows, precision=lax.Precision.HIGHEST)

def layer(layer_input, w_query, w_key, w_value, w_out, w_gate, w_up, w_down, gain_query, gain_key, gain_attn, gain_ffn, doc_ids, positions):
    cosine_table, sine_table = rope_tables(positions)
    queries = low_back(product(layer_input, w_query))
    keys_raw = low_back(product(layer_input, w_key))
    values_raw = low(low_back(product(layer_input, w_value)))
    queries = queries * inverse_rms(queries) * gain_query
    keys_raw = keys_raw * inverse_rms(keys_raw) * gain_key
    queries = low(rotate(queries.reshape(TOKENS, HEADS, HEAD), cosine_table, sine_table))
    keys_raw = low(rotate(keys_raw.reshape(TOKENS, HEADS, HEAD), cosine_table, sine_table))
    grouped = (N_DP, TOK_DP, HEADS, HEAD)
    mixture = lax.map(jax.checkpoint(group_attention), (queries.reshape(grouped), keys_raw.reshape(grouped), values_raw.reshape(grouped), doc_ids.reshape(N_DP, TOK_DP)))
    mixture = low(low_back(mixture.reshape(TOKENS, D)))
    attended = low_back(product(mixture, w_out))
    hidden_state = layer_input + attended * inverse_rms(attended) * gain_attn
    state_low = low(hidden_state)
    gate_values = low_back(product(state_low, w_gate))
    up_values = low_back(product(state_low, w_up))
    activated = low(jax.nn.silu(gate_values) * up_values)
    lowered = low_back(product(activated, w_down))
    return hidden_state + lowered * inverse_rms(lowered) * gain_ffn

def reference(layer_input, doc_ids, positions, w_query, w_key, w_value, w_out, w_gate, w_up, w_down, gain_query, gain_key, gain_attn, gain_ffn, grad_output):
    floats = tuple((operand.astype(jnp.float32) for operand in (layer_input, w_query, w_key, w_value, w_out, w_gate, w_up, w_down, gain_query, gain_key, gain_attn, gain_ffn)))

    def forward(*params):
        return layer(*params, doc_ids, positions)
    output, pullback = jax.vjp(forward, *floats)
    grads = pullback(grad_output.astype(jnp.float32))
    return (output.astype(jnp.bfloat16), grads[0], grads[1], grads[2], grads[3], grads[4], grads[5], grads[6], grads[7], grads[8], grads[9], grads[10], grads[11])
```

```python
import functools

import jax
import jax.numpy as jnp
from jax import lax
from jax.experimental import pallas as pl
from jax.experimental.pallas import tpu as pltpu
from jax.sharding import PartitionSpec as P

HEAD = 128
EPSILON = 1e-06
ROPE_BASE = 500000.0
MASKED = -1e30
BF = jnp.bfloat16
F32 = jnp.float32


def rope_tables(positions):
    digit = 32
    frequency = ROPE_BASE ** (-(jnp.arange(HEAD // 2, dtype=F32) * (2.0 / HEAD)))
    frequency = jnp.concatenate([frequency, frequency])

    def looked_up(index, count, unit):
        angles = (jnp.arange(count) * unit).astype(F32)[:, None] * frequency[None, :]
        table = jnp.concatenate([jnp.cos(angles), jnp.sin(angles)], axis=1)
        chosen = (index[:, None] == jnp.arange(count)[None, :]).astype(F32)
        both = jnp.dot(chosen, table, precision=lax.Precision.HIGHEST)
        return both[:, :HEAD], both[:, HEAD:]

    high_cosine, high_sine = looked_up(
        positions // digit, -(-positions.shape[0] // digit), digit
    )
    low_cosine, low_sine = looked_up(positions % digit, digit, 1)
    signs = jnp.where(jnp.arange(HEAD) < HEAD // 2, -1.0, 1.0).astype(F32)[None, :]
    return (
        high_cosine * low_cosine - high_sine * low_sine,
        (high_sine * low_cosine + high_cosine * low_sine) * signs,
    )


def dot(a, b):
    return jnp.dot(a, b, preferred_element_type=F32)


def dot_nt(a, b):
    return lax.dot_general(a, b, (((1,), (1,)), ((), ())), preferred_element_type=F32)


def dot_tn(a, b):
    return lax.dot_general(a, b, (((0,), (0,)), ((), ())), preferred_element_type=F32)


class Ring:
    def __init__(self, name, size):
        self.name, self.size = name, size
        self.here = lax.axis_index(name)

    def fetch(self, values, step):
        if step % self.size == 0:
            return values
        pairs = [(i, (i - step) % self.size) for i in range(self.size)]
        return lax.ppermute(values, self.name, pairs)

    def send(self, values, pairs):
        return lax.ppermute(values, self.name, pairs)

    def give(self, values, step):
        return self.fetch(values, -step)

    def at(self, step):
        return lax.rem(self.here + (step % self.size), self.size)


def gather_col(col, values):
    if col.size != 4:
        return [col.fetch(values, k) for k in range(col.size)]
    two = col.send(values, [(0, 2), (1, 3), (2, 0), (3, 1)])
    below = col.send(values, [(0, 1), (1, 2), (2, 3)])
    above = col.send(values, [(1, 0), (2, 1), (3, 2)])
    relayed = col.send(two, [(2, 3), (1, 0)])
    return [
        values,
        jnp.where(col.here == 3, relayed, above),
        two,
        jnp.where(col.here == 0, relayed, below),
    ]


def reduce_col(col, blocks):
    low = [block.astype(BF) for block in blocks]
    result = blocks[0]
    if col.size != 4:
        for k in range(1, col.size):
            result = result + col.give(low[k], k).astype(F32)
        return result
    relayed = col.send(jnp.where(col.here == 3, low[1], low[3]), [(3, 2), (0, 1)])
    above = col.send(low[3], [(1, 0), (2, 1), (3, 2)])
    below = col.send(low[1], [(0, 1), (1, 2), (2, 3)])
    two = (blocks[2] + relayed.astype(F32)).astype(BF)
    two = col.send(two, [(0, 2), (1, 3), (2, 0), (3, 1)])
    return result + above.astype(F32) + below.astype(F32) + two.astype(F32)


def after(values, *earlier):
    return lax.optimization_barrier((values, earlier))[0]


def block_at(values, index, size, axis):
    return lax.dynamic_slice_in_dim(values, index * size, size, axis)


def assemble(ring, blocks, axis):
    size = blocks[0].shape[axis]
    shape = list(blocks[0].shape)
    shape[axis] = size * ring.size
    whole = jnp.zeros(shape, blocks[0].dtype)
    for step, block in enumerate(blocks):
        whole = lax.dynamic_update_slice_in_dim(whole, block, ring.at(step) * size, axis)
    return whole


def from_here(ring, values, size, axis):
    twice = jnp.concatenate([values, values], axis=axis)
    return lax.dynamic_slice_in_dim(twice, ring.here * size, size * ring.size, axis)


def to_order(ring, values, size, axis):
    twice = jnp.concatenate([values, values], axis=axis)
    start = lax.rem(ring.size - ring.here, ring.size) * size
    return lax.dynamic_slice_in_dim(twice, start, size * ring.size, axis)


def exchange(ring, block_for):
    return [ring.fetch(block_for(ring.at(-step)), step) for step in range(ring.size)]


def gather_tokens(row, col, values):
    return [
        jnp.concatenate([row.fetch(block, j) for j in range(row.size)], axis=0)
        for block in gather_col(col, values)
    ]


def sum_rows(row, partial):
    parts = jnp.split(partial, row.size, axis=0)
    total = parts[0]
    for j in range(1, row.size):
        total = total + row.give(parts[j].astype(BF), j).astype(F32)
    return total


def sum_tokens(row, col, partials):
    return reduce_col(col, [sum_rows(row, partial) for partial in partials])


def sum_all(row, col, values):
    size = values.shape[1] // row.size
    total = values
    for j in range(1, row.size):
        total = total + jnp.roll(row.fetch(values, j), j * size, axis=1)
    result = total
    for k in range(1, col.size):
        result = result + col.fetch(total, k)
    return result


def rms_scale(values):
    return lax.rsqrt(jnp.mean(values * values, axis=1, keepdims=True) + EPSILON)


def rms_back(grad_normed, branch, scales, gains):
    weighted = grad_normed * gains
    inner = jnp.mean(weighted * branch, axis=1, keepdims=True)
    grad_branch = scales * weighted - branch * (scales * scales * scales) * inner
    grad_gains = jnp.sum(grad_normed * branch * scales, axis=0)
    return grad_branch, grad_gains


def turn(values, cosine, sine):
    return values * cosine + pltpu.roll(values, values.shape[-1] // 2, 1) * sine


def kernel_dot(a, b, dims):
    return lax.dot_general(a, b, (dims, ((), ())), preferred_element_type=F32)


def block_scores(queries, keys, doc_rows, doc_cols, slot_rows, slot_cols):
    scores = kernel_dot(queries, keys, ((1,), (1,))) * (HEAD**-0.5)
    allowed = (doc_rows == doc_cols) & (slot_cols <= slot_rows)
    return jnp.where(allowed, scores, MASKED)


def forward_kernel(
    block_rows,
    query_ref,
    key_ref,
    value_ref,
    query_scale_ref,
    key_scale_ref,
    query_gain_ref,
    key_gain_ref,
    cosine_ref,
    sine_ref,
    doc_rows_ref,
    doc_cols_ref,
    slot_rows_ref,
    slot_cols_ref,
    query_rot_ref,
    key_rot_ref,
    value_low_ref,
    mixture_ref,
    log_ref,
):
    cosine, sine = cosine_ref[...], sine_ref[...]
    normed = query_ref[...] * query_scale_ref[...] * query_gain_ref[...]
    query_rot_ref[...] = turn(normed, cosine, sine).astype(BF)
    normed = key_ref[...] * key_scale_ref[...] * key_gain_ref[...]
    key_rot_ref[...] = turn(normed, cosine, sine).astype(BF)
    value_low_ref[...] = value_ref[...].astype(BF)
    keys, values = key_rot_ref[...], value_low_ref[...]
    for start in range(0, query_ref.shape[0], block_rows):
        rows = pl.ds(start, block_rows)
        scores = block_scores(
            query_rot_ref[rows, :],
            keys,
            doc_rows_ref[rows, :],
            doc_cols_ref[...],
            slot_rows_ref[rows, :],
            slot_cols_ref[...],
        )
        largest = jnp.max(scores, axis=1, keepdims=True)
        weights = jnp.exp(scores - largest)
        totals = jnp.sum(weights, axis=1, keepdims=True)
        chances = (weights * (1.0 / totals)).astype(BF)
        mixture_ref[rows, :] = kernel_dot(chances, values, ((1,), (0,))).astype(BF)
        log_ref[0, rows, :] = largest + jnp.log(totals)


def backward_kernel(
    block_rows,
    query_ref,
    key_ref,
    query_scale_ref,
    key_scale_ref,
    query_gain_ref,
    key_gain_ref,
    cosine_ref,
    sine_ref,
    doc_rows_ref,
    doc_cols_ref,
    slot_rows_ref,
    slot_cols_ref,
    query_rot_ref,
    key_rot_ref,
    value_low_ref,
    grad_ref,
    log_ref,
    query_weighted_ref,
    key_weighted_ref,
    grad_value_ref,
    query_inner_ref,
    key_inner_ref,
    query_gain_grad_ref,
    key_gain_grad_ref,
    key_total,
    value_total,
):
    cosine, sine = cosine_ref[...], sine_ref[...]
    keys, values = key_rot_ref[...], value_low_ref[...]
    factor = HEAD**-0.5
    for start in range(0, query_ref.shape[0], block_rows):
        rows = pl.ds(start, block_rows)
        queries, grads = query_rot_ref[rows, :], grad_ref[rows, :]
        scores = block_scores(
            queries,
            keys,
            doc_rows_ref[rows, :],
            doc_cols_ref[...],
            slot_rows_ref[rows, :],
            slot_cols_ref[...],
        )
        chances = jnp.exp(scores - log_ref[0, rows, :])
        value_part = kernel_dot(chances.astype(BF), grads, ((0,), (0,)))
        grad_chances = kernel_dot(grads, values, ((1,), (1,)))
        inner = jnp.sum(chances * grad_chances, axis=1, keepdims=True)
        grad_scores = (chances * (grad_chances - inner)).astype(BF)
        query_weighted_ref[rows, :] = kernel_dot(grad_scores, keys, ((1,), (0,))) * factor
        key_part = kernel_dot(grad_scores, queries, ((0,), (0,))) * factor
        if start == 0:
            value_total[...] = value_part
            key_total[...] = key_part
        else:
            value_total[...] += value_part
            key_total[...] += key_part
    grad_value_ref[...] = value_total[...].astype(BF)
    for grad, raw_ref, scale_ref, gain_ref, weighted_ref, inner_ref, gain_grad_ref in (
        (
            query_weighted_ref[...],
            query_ref,
            query_scale_ref,
            query_gain_ref,
            query_weighted_ref,
            query_inner_ref,
            query_gain_grad_ref,
        ),
        (
            key_total[...],
            key_ref,
            key_scale_ref,
            key_gain_ref,
            key_weighted_ref,
            key_inner_ref,
            key_gain_grad_ref,
        ),
    ):
        unturned = turn(grad, cosine, -sine)
        raw = raw_ref[...]
        gain_grad_ref[0] = jnp.sum(unturned * raw * scale_ref[...], axis=0, keepdims=True)
        weighted = unturned * gain_ref[...]
        weighted_ref[...] = weighted
        inner_ref[0] = jnp.sum(weighted * raw, axis=1, keepdims=True)


def head_specs(length, heads):
    return {
        "head": lambda first: pl.BlockSpec((length, HEAD), lambda h, first=first: (0, first + h)),
        "gain": pl.BlockSpec((1, HEAD), lambda h: (0, h)),
        "column": pl.BlockSpec((length, 1), lambda h: (0, 0)),
        "line": pl.BlockSpec((1, length), lambda h: (0, 0)),
        "table": pl.BlockSpec((length, HEAD), lambda h: (0, 0)),
        "head_column": pl.BlockSpec((1, length, 1), lambda h: (h, 0, 0)),
        "head_line": pl.BlockSpec((1, 1, HEAD), lambda h: (h, 0, 0)),
    }


def attend_forward(raw, query_scale, key_scale, gains, tables, marks):
    length = raw.shape[0]
    heads = raw.shape[1] // (3 * HEAD)
    spec = head_specs(length, heads)
    wide = jax.ShapeDtypeStruct((length, heads * HEAD), BF)
    return pl.pallas_call(
        functools.partial(forward_kernel, min(256, length)),
        grid=(heads,),
        in_specs=[spec["head"](0), spec["head"](heads), spec["head"](2 * heads)]
        + [spec["column"]] * 2
        + [spec["gain"]] * 2
        + [spec["table"]] * 2
        + [spec["column"], spec["line"], spec["column"], spec["line"]],
        out_specs=[spec["head"](0)] * 4 + [spec["head_column"]],
        out_shape=[wide] * 4 + [jax.ShapeDtypeStruct((heads, length, 1), F32)],
        compiler_params=pltpu.CompilerParams(vmem_limit_bytes=40 << 20),
        cost_estimate=pl.CostEstimate(
            flops=heads * 4 * length * length * HEAD,
            bytes_accessed=heads * length * HEAD * 20,
            transcendentals=heads * length * length,
        ),
        name="attend_forward",
    )(raw, raw, raw, query_scale, key_scale, *gains, *tables, *marks)


def attend_backward(raw, query_scale, key_scale, gains, tables, marks, saved, grad, logs):
    length = raw.shape[0]
    heads = raw.shape[1] // (3 * HEAD)
    spec = head_specs(length, heads)
    wide = jax.ShapeDtypeStruct((length, heads * HEAD), F32)
    low = jax.ShapeDtypeStruct((length, heads * HEAD), BF)
    tall = jax.ShapeDtypeStruct((heads, length, 1), F32)
    flat = jax.ShapeDtypeStruct((heads, 1, HEAD), F32)
    return pl.pallas_call(
        functools.partial(backward_kernel, min(256, length)),
        grid=(heads,),
        in_specs=[spec["head"](0), spec["head"](heads)]
        + [spec["column"]] * 2
        + [spec["gain"]] * 2
        + [spec["table"]] * 2
        + [spec["column"], spec["line"], spec["column"], spec["line"]]
        + [spec["head"](0)] * 4
        + [spec["head_column"]],
        out_specs=[spec["head"](0)] * 3 + [spec["head_column"]] * 2 + [spec["head_line"]] * 2,
        out_shape=[wide, wide, low, tall, tall, flat, flat],
        scratch_shapes=[pltpu.VMEM((length, HEAD), F32)] * 2,
        compiler_params=pltpu.CompilerParams(vmem_limit_bytes=40 << 20),
        cost_estimate=pl.CostEstimate(
            flops=heads * 10 * length * length * HEAD,
            bytes_accessed=heads * length * HEAD * 30,
            transcendentals=heads * length * length,
        ),
        name="attend_backward",
    )(raw, raw, query_scale, key_scale, *gains, *tables, *marks, *saved, grad, logs)


def device_program(sizes):
    n_dp, n_row, n_col = sizes["dp"], sizes["row"], sizes["col"]

    def per_device(
        layer_input,
        doc_ids,
        positions,
        w_query,
        w_key,
        w_value,
        w_out,
        w_gate,
        w_up,
        w_down,
        gain_query,
        gain_key,
        gain_attn,
        gain_ffn,
        grad_output,
    ):
        row, col = Ring("row", n_row), Ring("col", n_col)
        dp = lax.axis_index("dp")
        length = doc_ids.shape[0]
        row_tokens = layer_input.shape[0]
        own_tokens = row_tokens // n_col
        features = layer_input.shape[1]
        width = features * n_col
        head_cols = w_query.shape[1] // n_col
        hidden_cols = w_gate.shape[1] // n_col
        in_rows = features // n_dp
        out_rows = head_cols // n_dp
        down_rows = hidden_cols // n_dp

        def gather_dp(values):
            return lax.all_gather(values, "dp", axis=0, tiled=True)

        steps = [1 << bit for bit in range(n_dp.bit_length() - 1)]

        def partner(values, step):
            return lax.ppermute(values, "dp", [(i, i ^ step) for i in range(n_dp)])

        class GroupSum:
            def __init__(self, block_for):
                blocks = [block_for(dp ^ d) for d in range(n_dp)]
                half = blocks[0].shape[-1] // 2
                self.halves = [
                    (dict(enumerate(b[..., :half] for b in blocks)), list(steps)),
                    (dict(enumerate(b[..., half:] for b in blocks)), list(steps[::-1])),
                ]
                self.came = None
                self.send()

            def send(self):
                self.came = []
                for blocks, order in self.halves:
                    given = [blocks[d] for d in sorted(blocks) if d & order[0]]
                    self.came.append(partner(jnp.stack(given), order[0]))

            def land(self, chain, more=True):
                self.came, chain = lax.optimization_barrier((self.came, chain))
                for (blocks, order), came in zip(self.halves, self.came):
                    step = order.pop(0)
                    for place, d in enumerate([d for d in sorted(blocks) if d & step]):
                        kept = blocks[d ^ step].astype(F32) + came[place].astype(F32)
                        blocks[d ^ step] = kept.astype(BF)
                        del blocks[d]
                if self.halves[0][1]:
                    self.send()
                return chain

            def finish(self, chain):
                while self.halves[0][1]:
                    chain = self.land(chain)
                whole = jnp.concatenate([blocks[0] for blocks, _ in self.halves], axis=-1)
                return whole, chain

        def qkv_block(index):
            return jnp.concatenate(
                [
                    lax.dynamic_slice(
                        w, (dp * in_rows, index * head_cols), (in_rows, head_cols)
                    )
                    for w in (w_query, w_key, w_value)
                ],
                axis=1,
            )

        def gate_up_block(index):
            return jnp.concatenate(
                [
                    lax.dynamic_slice(
                        w, (dp * in_rows, index * hidden_cols), (in_rows, hidden_cols)
                    )
                    for w in (w_gate, w_up)
                ],
                axis=1,
            )

        def out_block(index):
            return lax.dynamic_slice_in_dim(
                w_out, index * head_cols + dp * out_rows, out_rows, 0
            )

        def down_block(index):
            return lax.dynamic_slice_in_dim(
                w_down, index * hidden_cols + dp * down_rows, down_rows, 0
            )

        qkv_parts = jnp.stack(exchange(col, qkv_block))
        w_qkv = gather_dp(qkv_parts[None])
        w_qkv = [w_qkv[:, k].reshape(features, 3 * head_cols) for k in range(n_col)]
        out_parts = assemble(col, exchange(col, out_block), 1)
        w_out_all = gather_dp(out_parts)

        turned_docs = from_here(row, doc_ids, row_tokens, 0)
        turned_positions = from_here(row, positions, row_tokens, 0)
        slots = lax.rem(jnp.arange(length) + row.here * row_tokens, length)
        tables = rope_tables(turned_positions)
        near, tables = lax.optimization_barrier((gather_col(col, layer_input), tables))
        input_rows = [
            jnp.concatenate([row.fetch(block, j) for j in range(n_row)], axis=0)
            for block in near
        ]
        own_input = jnp.concatenate(
            [block_at(block, col.here, own_tokens, 0) for block in near], axis=1
        )
        own_input = to_order(col, own_input, features, 1).astype(F32)

        w_down, grad_output = after((w_down, grad_output), near)
        down_parts = exchange(col, down_block)
        cotangent = exchange(
            col, lambda index: block_at(grad_output, index, own_tokens, 0)
        )

        raw = sum(dot(rows, w) for rows, w in zip(input_rows, w_qkv))
        query_raw = raw[:, :head_cols]
        key_raw = raw[:, head_cols : 2 * head_cols]
        squares = jnp.stack(
            [jnp.sum(query_raw * query_raw, axis=1), jnp.sum(key_raw * key_raw, axis=1)]
        )
        squares = sum_all(row, col, squares)
        gains = jnp.stack([gain_attn, gain_ffn])
        gains = assemble(col, [col.fetch(gains, k) for k in range(n_col)], 1)
        gain_attn_all, gain_ffn_all = gains[0:1], gains[1:2]

        squares, down_parts, cotangent = lax.optimization_barrier(
            (squares, down_parts, cotangent)
        )
        w_down_all = gather_dp(assemble(col, down_parts, 1))
        cotangent = assemble(col, cotangent, 1).astype(F32)
        w_gate, w_up = after((w_gate, w_up), down_parts)
        gate_up_parts = exchange(col, gate_up_block)

        scales = lax.rsqrt(squares / width + EPSILON)
        query_scale, key_scale = scales[0][:, None], scales[1][:, None]
        head_gains = (gain_query[None, :], gain_key[None, :])
        marks = (turned_docs[:, None], turned_docs[None, :], slots[:, None], slots[None, :])
        *saved, mixture, logs = attend_forward(
            raw, query_scale, key_scale, head_gains, tables, marks
        )
        mixture = from_here(
            col, mixture.reshape(n_row, row_tokens, head_cols), own_tokens, 1
        ).reshape(n_row, n_col, own_tokens, head_cols)
        mixture = [mixture[:, k].reshape(-1, head_cols) for k in range(n_col)]
        attended = [dot(block, w_out_all) for block in mixture]
        gate_up_parts, attended = lax.optimization_barrier((gate_up_parts, attended))
        gate_up_parts = assemble(col, [part[None] for part in gate_up_parts], 0)
        w_gate_up = gather_dp(gate_up_parts[None])
        w_gate_up = w_gate_up.transpose(1, 0, 2, 3).reshape(width, 2 * hidden_cols)
        attended = sum_tokens(row, col, attended)
        attn_scale = rms_scale(attended)
        hidden_state = own_input + attended * attn_scale * gain_attn_all

        state_rows = gather_tokens(row, col, hidden_state.astype(BF))
        kept, activated = [], []
        for block in state_rows:
            gate_up = dot(block, w_gate_up)
            gate_values, up_values = gate_up[:, :hidden_cols], gate_up[:, hidden_cols:]
            sigmoid_gate = jax.nn.sigmoid(gate_values)
            silu_gate = gate_values * sigmoid_gate
            kept.append((gate_values, up_values, sigmoid_gate, silu_gate))
            activated.append((silu_gate * up_values).astype(BF))
        lowered = sum_tokens(row, col, [dot(block, w_down_all) for block in activated])
        ffn_scale = rms_scale(lowered)
        own_output = (hidden_state + lowered * ffn_scale * gain_ffn_all).astype(BF)
        layer_output = assemble(
            col,
            exchange(col, lambda index: block_at(own_output, index, features, 1)),
            0,
        )

        grad_lowered, grad_gain_ffn = rms_back(cotangent, lowered, ffn_scale, gain_ffn_all)
        lowered_rows = gather_tokens(row, col, grad_lowered.astype(BF))
        grad_gate_up, state_part = [], []
        for block, (gate_values, up_values, sigmoid_gate, silu_gate) in zip(lowered_rows, kept):
            grad_activated = dot_nt(block, w_down_all)
            grad_gate = (
                grad_activated
                * up_values
                * (sigmoid_gate * (1.0 + gate_values * (1.0 - sigmoid_gate)))
            )
            grad_up = grad_activated * silu_gate
            grad_gate_up.append(
                jnp.concatenate([grad_gate.astype(BF), grad_up.astype(BF)], axis=1)
            )
            state_part.append(dot_nt(grad_gate_up[-1], w_gate_up))
        grad_w_down = dot_tn(jnp.concatenate(activated), jnp.concatenate(lowered_rows))
        grad_w_down = grad_w_down.astype(BF)
        down_sum = GroupSum(lambda index: block_at(grad_w_down, index, down_rows, 0))
        grad_w_gate_up = dot_tn(jnp.concatenate(state_rows), jnp.concatenate(grad_gate_up))
        grad_w_gate_up = grad_w_gate_up.astype(BF)
        gate_up_grads = grad_w_gate_up.reshape(n_col, n_dp, in_rows, 2 * hidden_cols)
        gate_up_sum = GroupSum(
            lambda index: lax.dynamic_index_in_dim(gate_up_grads, index, 1, False)
        )
        state_part = sum_tokens(row, col, state_part)
        state_part = down_sum.land(state_part)
        state_part = gate_up_sum.land(state_part)
        down_sum, state_part = down_sum.finish(state_part)
        grad_state = cotangent + state_part
        grad_attended, grad_gain_attn = rms_back(
            grad_state, attended, attn_scale, gain_attn_all
        )
        attended_rows = gather_tokens(row, col, grad_attended.astype(BF))
        gate_up_sum, attended_rows = gate_up_sum.finish(attended_rows)
        mixture, attended_rows = jnp.concatenate(mixture), jnp.concatenate(attended_rows)
        gate_up_sum = gate_up_sum.reshape(-1, 2 * hidden_cols)

        def give_back(parts_for):
            return gather_dp(
                assemble(col, [part[None] for part in exchange(col, parts_for)], 0)[None]
            )

        down_sum, gate_up_sum = after((down_sum, gate_up_sum), attended_rows)
        down_all = give_back(lambda index: block_at(down_sum, index, features, 1))
        gate_up_all = give_back(lambda index: block_at(gate_up_sum, index, in_rows, 0))
        grad_w_out = dot_tn(mixture, attended_rows).astype(BF)
        out_sum = GroupSum(lambda index: block_at(grad_w_out, index, out_rows, 0))
        grad_mixture = dot_nt(attended_rows, w_out_all).astype(BF)
        grad_mixture = grad_mixture.reshape(n_col, n_row, own_tokens, head_cols)
        grad_mixture = grad_mixture.swapaxes(0, 1).reshape(n_row, row_tokens, head_cols)
        grad_mixture = to_order(col, grad_mixture, own_tokens, 1).reshape(length, head_cols)
        (
            query_weighted,
            key_weighted,
            grad_value,
            query_inner,
            key_inner,
            grad_gain_query,
            grad_gain_key,
        ) = attend_backward(
            raw, query_scale, key_scale, head_gains, tables, marks, saved, grad_mixture, logs
        )
        inner = jnp.stack([jnp.sum(query_inner, axis=0)[:, 0], jnp.sum(key_inner, axis=0)[:, 0]])
        inner = sum_all(row, col, inner) / width
        grad_query = (
            query_scale * query_weighted
            - query_raw * (query_scale * query_scale * query_scale) * inner[0][:, None]
        )
        grad_key = (
            key_scale * key_weighted
            - key_raw * (key_scale * key_scale * key_scale) * inner[1][:, None]
        )
        grad_qkv = jnp.concatenate(
            [grad_query.astype(BF), grad_key.astype(BF), grad_value], axis=1
        )
        grad_w_qkv = jnp.stack([dot_tn(rows, grad_qkv).astype(BF) for rows in input_rows])
        qkv_grads = grad_w_qkv.reshape(n_col, n_dp, in_rows, 3 * head_cols)
        qkv_sum = GroupSum(lambda index: lax.dynamic_index_in_dim(qkv_grads, index, 1, False))
        ordered_qkv = after(grad_qkv, grad_w_qkv)
        out_sum, ordered_qkv = out_sum.finish(ordered_qkv)
        out_all = give_back(lambda index: block_at(out_sum, index, features, 1))
        input_part = [sum_rows(row, dot_nt(ordered_qkv, w)) for w in w_qkv]
        qkv_sum, input_part = qkv_sum.finish(input_part)
        qkv_back = [col.fetch(qkv_sum[-k % n_col], k)[None] for k in range(n_col)]
        qkv_back, input_part = lax.optimization_barrier((qkv_back, input_part))
        qkv_all = gather_dp(assemble(col, qkv_back, 0)[None])
        own_state = grad_state.astype(BF)
        grad_input = reduce_col(col, input_part) + assemble(
            col,
            exchange(col, lambda index: block_at(own_state, index, features, 1)),
            0,
        ).astype(F32)

        def columns_of(whole, start, size):
            return jnp.concatenate(
                [
                    whole[:, k, :, start : start + size].reshape(features, size)
                    for k in range(n_col)
                ],
                axis=1,
            ).astype(F32)

        grad_w_down = down_all.swapaxes(0, 1).reshape(w_down.shape).astype(F32)
        grad_w_gate = columns_of(gate_up_all, 0, hidden_cols)
        grad_w_up = columns_of(gate_up_all, hidden_cols, hidden_cols)
        grad_w_out = out_all.swapaxes(0, 1).reshape(w_out.shape).astype(F32)
        grad_w_query = columns_of(qkv_all, 0, head_cols)
        grad_w_key = columns_of(qkv_all, head_cols, head_cols)
        grad_w_value = columns_of(qkv_all, 2 * head_cols, head_cols)

        small = jnp.stack([grad_gain_attn, grad_gain_ffn])
        pieces = exchange(col, lambda index: block_at(small, index, features, 1))
        small = sum(pieces[1:], pieces[0])
        total_small = small
        for j in range(1, n_row):
            total_small = total_small + row.fetch(small, j)
        gain_sums = lax.psum(
            (total_small, jnp.stack([grad_gain_query.reshape(-1), grad_gain_key.reshape(-1)])), "dp"
        )
        return (
            layer_output,
            grad_input,
            grad_w_query,
            grad_w_key,
            grad_w_value,
            grad_w_out,
            grad_w_gate,
            grad_w_up,
            grad_w_down,
            gain_sums[1][0],
            gain_sums[1][1],
            gain_sums[0][0],
            gain_sums[0][1],
        )

    return per_device


def solution(mesh):
    in_specs = (
        P(("dp", "row"), "col"),
        P("dp"),
        P("dp"),
        P("col", "row"),
        P("col", "row"),
        P("col", "row"),
        P("row", "col"),
        P("col", "row"),
        P("col", "row"),
        P("row", "col"),
        P(("row", "col")),
        P(("row", "col")),
        P("col"),
        P("col"),
        P(("dp", "row"), "col"),
    )
    out_specs = (
        P(("dp", "row"), "col"),
        P(("dp", "row"), "col"),
        P("col", "row"),
        P("col", "row"),
        P("col", "row"),
        P("row", "col"),
        P("col", "row"),
        P("col", "row"),
        P("row", "col"),
        P(("row", "col")),
        P(("row", "col")),
        P("col"),
        P("col"),
    )
    return jax.shard_map(
        device_program(dict(mesh.shape)),
        mesh=mesh,
        in_specs=in_specs,
        out_specs=out_specs,
        check_vma=False,
    )
```

```python
import functools
import math

import jax
import jax.numpy as jnp
from jax import lax
from jax.experimental import pallas as pl
from jax.experimental.pallas import tpu as pltpu
from jax.sharding import PartitionSpec as P

HEAD = 128
EPSILON = 1e-06
ROPE_BASE = 500000.0
MASKED = -1e30
BF = jnp.bfloat16
F32 = jnp.float32


def rope_tables(positions):
    digit = 32
    frequency = ROPE_BASE ** (-(jnp.arange(HEAD // 2, dtype=F32) * (2.0 / HEAD)))
    frequency = jnp.concatenate([frequency, frequency])

    def looked_up(index, count, unit):
        angles = (jnp.arange(count) * unit).astype(F32)[:, None] * frequency[None, :]
        table = jnp.concatenate([jnp.cos(angles), jnp.sin(angles)], axis=1)
        chosen = (index[:, None] == jnp.arange(count)[None, :]).astype(F32)
        both = jnp.dot(chosen, table, precision=lax.Precision.HIGHEST)
        return both[:, :HEAD], both[:, HEAD:]

    high_cosine, high_sine = looked_up(
        positions // digit, -(-positions.shape[0] // digit), digit
    )
    low_cosine, low_sine = looked_up(positions % digit, digit, 1)
    signs = jnp.where(jnp.arange(HEAD) < HEAD // 2, -1.0, 1.0).astype(F32)[None, :]
    return (
        high_cosine * low_cosine - high_sine * low_sine,
        (high_sine * low_cosine + high_cosine * low_sine) * signs,
    )


def dot(a, b):
    return jnp.dot(a, b, preferred_element_type=F32)


def dot_nt(a, b):
    return lax.dot_general(a, b, (((1,), (1,)), ((), ())), preferred_element_type=F32)


def dot_tn(a, b):
    return lax.dot_general(a, b, (((0,), (0,)), ((), ())), preferred_element_type=F32)


class Ring:
    def __init__(self, name, size):
        self.name, self.size = name, size
        self.here = lax.axis_index(name)

    def fetch(self, values, step):
        if step % self.size == 0:
            return values
        pairs = [(i, (i - step) % self.size) for i in range(self.size)]
        return lax.ppermute(values, self.name, pairs)

    def send(self, values, pairs):
        return lax.ppermute(values, self.name, pairs)

    def give(self, values, step):
        return self.fetch(values, -step)

    def at(self, step):
        return lax.rem(self.here + (step % self.size), self.size)


def after(values, *earlier):
    return lax.optimization_barrier((values, earlier))[0]


def gather_steps(col, values, early=(), beside=()):
    two = col.send(values, [(0, 2), (1, 3), (2, 0), (3, 1)])
    below = col.send(values, [(0, 1), (1, 2), (2, 3)])
    above = col.send(values, [(1, 0), (2, 1), (3, 2)])
    two, early = lax.optimization_barrier((two, early))
    beside = beside(early) if callable(beside) else beside
    two, below, above, beside = lax.optimization_barrier((two, below, above, beside))
    relayed = col.send(two, [(2, 3), (1, 0)])
    return two, below, above, relayed, early, beside


def gather_col(col, values, early, beside):
    if col.size != 4:
        return [col.fetch(values, k) for k in range(col.size)], early, beside
    two, below, above, relayed, early, beside = gather_steps(col, values, early, beside)
    near = [
        values,
        jnp.where(col.here == 3, relayed, above),
        two,
        jnp.where(col.here == 0, relayed, below),
    ]
    return near, early, beside


def by_arrival(col, blocks):
    if col.size != 4:
        return blocks
    last = col.here == 3
    return [
        blocks[0],
        jnp.where(last, blocks[3], blocks[1]),
        blocks[2],
        jnp.where(last, blocks[1], blocks[3]),
    ]


def gather_near(col, values, early=(), beside=()):
    if col.size != 4:
        beside = beside(early) if callable(beside) else beside
        return [col.fetch(values, k) for k in range(col.size)], early, beside
    two, below, above, relayed, early, beside = gather_steps(col, values, early, beside)
    inside = (col.here == 1) | (col.here == 2)
    near = [
        values,
        jnp.where(col.here == 3, below, above),
        two,
        jnp.where(inside, below, relayed),
    ]
    return near, early, beside


def reduce_near(col, blocks, between=()):
    low = [block.astype(BF) for block in blocks]
    result = blocks[0]
    if col.size != 4:
        for k in range(1, col.size):
            result = result + col.give(low[k], k).astype(F32)
        return result, between
    relayed = col.send(low[3], [(3, 2), (0, 1)])
    below = col.send(low[1], [(0, 1), (1, 2), (2, 3)])
    above = col.send(
        jnp.where(col.here == 3, low[1], low[3]), [(1, 0), (2, 1), (3, 2)]
    )
    two = (blocks[2] + relayed.astype(F32)).astype(BF)
    two, between = lax.optimization_barrier((two, between))
    two = col.send(two, [(0, 2), (1, 3), (2, 0), (3, 1)])
    return result + above.astype(F32) + below.astype(F32) + two.astype(F32), between


def block_at(values, index, size, axis):
    return lax.dynamic_slice_in_dim(values, index * size, size, axis)


def assemble_kernel(here_ref, *refs):
    blocks, whole = refs[:-1], refs[-1]
    for step, block in enumerate(blocks):

        @pl.when(pl.program_id(0) == step)
        def _():
            whole[...] = block[...]


def assemble(ring, blocks, axis):
    shape = list(blocks[0].shape)
    size = len(blocks)
    zeros = (0,) * len(shape)

    def place(step, here):
        return zeros[:axis] + (lax.rem(here[0] + step, size),) + zeros[axis + 1 :]

    block_shape = tuple(shape)
    shape[axis] *= size
    return pl.pallas_call(
        assemble_kernel,
        grid_spec=pltpu.PrefetchScalarGridSpec(
            num_scalar_prefetch=1,
            grid=(size,),
            in_specs=[pl.BlockSpec(block_shape, lambda step, here: zeros)] * size,
            out_specs=pl.BlockSpec(block_shape, place),
        ),
        out_shape=jax.ShapeDtypeStruct(tuple(shape), blocks[0].dtype),
        compiler_params=pltpu.CompilerParams(vmem_limit_bytes=32 << 20),
        cost_estimate=pl.CostEstimate(
            flops=0,
            bytes_accessed=2 * math.prod(shape) * blocks[0].dtype.itemsize,
            transcendentals=0,
        ),
        name="assemble",
    )(ring.here.astype(jnp.int32)[None], *blocks)


def first_weights_kernel(sizes, places_ref, *refs):
    pieces, (in_ref, out_ref) = refs[:-2], refs[-2:]
    n_col, n_out, out_rows, wide = sizes
    features = out_ref.shape[1] // n_col
    narrow = features // n_out

    def store(piece, first):
        for k in range(piece.shape[0]):
            in_ref[first + k] = piece[k, :, :wide]
            start = lax.rem(places_ref[1] + first + k, n_col) * features
            for i in range(n_out):
                place = pl.multiple_of(start + i * narrow, narrow)
                out_ref[:, pl.ds(place, narrow)] = piece[
                    k, i * out_rows : (i + 1) * out_rows, wide:
                ]

    for d in range(3):

        @pl.when(pl.program_id(0) == d)
        def _():
            store(pieces[d], 0)

    @pl.when(pl.program_id(0) == 3)
    def _():
        store(pieces[3], 0)
        store(pieces[4], pieces[3].shape[0])


def first_weights(dp, here, pieces, wide, n_out):
    n_col, in_rows, columns = pieces[0].shape
    out_rows = in_rows // n_out
    features = n_out * (columns - wide)
    whole = [
        pl.BlockSpec(piece.shape, lambda step, places: (0, 0, 0)) for piece in pieces
    ]
    return pl.pallas_call(
        functools.partial(first_weights_kernel, (n_col, n_out, out_rows, wide)),
        grid_spec=pltpu.PrefetchScalarGridSpec(
            num_scalar_prefetch=1,
            grid=(4,),
            in_specs=whole,
            out_specs=[
                pl.BlockSpec(
                    (n_col, in_rows, wide), lambda step, places: (0, places[0] ^ step, 0)
                ),
                pl.BlockSpec(
                    (out_rows, n_col * features), lambda step, places: (places[0] ^ step, 0)
                ),
            ],
        ),
        out_shape=[
            jax.ShapeDtypeStruct((n_col, 4 * in_rows, wide), BF),
            jax.ShapeDtypeStruct((4 * out_rows, n_col * features), BF),
        ],
        compiler_params=pltpu.CompilerParams(vmem_limit_bytes=32 << 20),
        cost_estimate=pl.CostEstimate(
            flops=0, bytes_accessed=8 * n_col * in_rows * columns * 2, transcendentals=0
        ),
        name="first_weights",
    )(jnp.stack([dp, here]).astype(jnp.int32), *pieces)


def pair_gradients_kernel(all_ref, gate_ref, up_ref):
    gate_ref[...] = all_ref[0, 0, 0].astype(F32)
    up_ref[...] = all_ref[0, 0, 1].astype(F32)


def pair_gradients(gathered):
    n_dp, n_col, pair, rows, hidden = gathered.shape
    side = pl.BlockSpec((rows, hidden), lambda p, z: (p, z))
    return pl.pallas_call(
        pair_gradients_kernel,
        grid=(n_dp, n_col),
        in_specs=[pl.BlockSpec((1, 1, pair, rows, hidden), lambda p, z: (p, z, 0, 0, 0))],
        out_specs=[side, side],
        out_shape=[jax.ShapeDtypeStruct((n_dp * rows, n_col * hidden), F32)] * 2,
        compiler_params=pltpu.CompilerParams(vmem_limit_bytes=56 << 20),
        cost_estimate=pl.CostEstimate(
            flops=0, bytes_accessed=6 * math.prod(gathered.shape), transcendentals=0
        ),
        name="pair_gradients",
    )(gathered)


def last_gradients_kernel(n_out, places_ref, *refs):
    pieces, outs = refs[:-4], refs[-4:]
    n_col = pieces[0].shape[0]
    features = outs[3].shape[3]
    head_cols = outs[0].shape[1] // n_col
    narrow = features // n_out

    def store(piece, first):
        rows = piece.shape[1] // n_out
        for k in range(piece.shape[0]):
            source = lax.rem(places_ref[1] + first + k, n_col)
            place = pl.ds(pl.multiple_of(source * head_cols, head_cols), head_cols)
            for i in range(3):
                outs[i][:, place] = piece[k, :, i * head_cols : (i + 1) * head_cols].astype(F32)
            for i in range(n_out):
                outs[3][source, 0, :, i * narrow : (i + 1) * narrow] = piece[
                    k, i * rows : (i + 1) * rows, 3 * head_cols :
                ].astype(F32)

    for d in range(3):

        @pl.when(pl.program_id(0) == d)
        def _():
            store(pieces[d], 0)

    @pl.when(pl.program_id(0) == 3)
    def _():
        store(pieces[3], 0)
        store(pieces[4], pieces[3].shape[0])


def last_gradients(dp, here, pieces, head_cols, n_out):
    n_col, rows, columns = pieces[0].shape
    features = n_out * (columns - 3 * head_cols)
    side = pl.BlockSpec(
        (rows, n_col * head_cols), lambda step, places: (places[0] ^ step, 0)
    )
    side_shape = jax.ShapeDtypeStruct((4 * rows, n_col * head_cols), F32)
    *sides, out = pl.pallas_call(
        functools.partial(last_gradients_kernel, n_out),
        grid_spec=pltpu.PrefetchScalarGridSpec(
            num_scalar_prefetch=1,
            grid=(4,),
            in_specs=[
                pl.BlockSpec(piece.shape, lambda step, places: (0, 0, 0)) for piece in pieces
            ],
            out_specs=[side] * 3
            + [
                pl.BlockSpec(
                    (n_col, 1, rows // n_out, features),
                    lambda step, places: (0, places[0] ^ step, 0, 0),
                )
            ],
        ),
        out_shape=[side_shape] * 3
        + [jax.ShapeDtypeStruct((n_col, 4, rows // n_out, features), F32)],
        compiler_params=pltpu.CompilerParams(vmem_limit_bytes=56 << 20),
        cost_estimate=pl.CostEstimate(
            flops=0, bytes_accessed=24 * n_col * rows * columns, transcendentals=0
        ),
        name="last_gradients",
    )(jnp.stack([dp, here]).astype(jnp.int32), *pieces)
    return sides, out.reshape(-1, features)


def own_block_kernel(here_ref, *refs):
    blocks, whole = refs[:-1], refs[-1]
    for step, block in enumerate(blocks):

        @pl.when(pl.program_id(0) == step)
        def _():
            whole[...] = block[...]


def own_rows(ring, blocks):
    size = len(blocks)
    rows, columns = blocks[0].shape[0] // size, blocks[0].shape[1]
    return pl.pallas_call(
        own_block_kernel,
        grid_spec=pltpu.PrefetchScalarGridSpec(
            num_scalar_prefetch=1,
            grid=(size,),
            in_specs=[pl.BlockSpec((rows, columns), lambda step, here: (here[0], 0))] * size,
            out_specs=pl.BlockSpec(
                (rows, columns), lambda step, here: (0, lax.rem(here[0] + step, size))
            ),
        ),
        out_shape=jax.ShapeDtypeStruct((rows, columns * size), blocks[0].dtype),
        compiler_params=pltpu.CompilerParams(vmem_limit_bytes=32 << 20),
        name="own_rows",
    )(ring.here.astype(jnp.int32)[None], *blocks)


def from_here(ring, values, size, axis):
    twice = jnp.concatenate([values, values], axis=axis)
    return lax.dynamic_slice_in_dim(twice, ring.here * size, size * ring.size, axis)


def to_order(ring, values, size, axis):
    twice = jnp.concatenate([values, values], axis=axis)
    start = lax.rem(ring.size - ring.here, ring.size) * size
    return lax.dynamic_slice_in_dim(twice, start, size * ring.size, axis)


def exchange(ring, block_for):
    return [ring.fetch(block_for(ring.at(-step)), step) for step in range(ring.size)]


def gather_tokens(row, col, values, early=(), beside=()):
    near, early, beside = gather_near(col, values, early, beside)
    blocks = [
        jnp.concatenate([row.fetch(block, j) for j in range(row.size)], axis=0)
        for block in near
    ]
    return blocks, early, beside


def sum_rows(row, partial):
    size = partial.shape[0] // row.size
    total = partial[:size]
    for j in range(1, row.size):
        total = total + row.give(partial[j * size : (j + 1) * size].astype(BF), j).astype(F32)
    return total


def sum_all(row, col, values, block_for):
    length = values.shape[1]
    size = length // row.size
    total = values
    for j in range(1, row.size):
        total = total + jnp.roll(row.fetch(values, j), j * size, axis=1)
    came = [
        col.fetch(jnp.concatenate([total, block_for(col.at(-k))], axis=1), k)
        for k in range(col.size)
    ]
    result = came[0]
    for part in came[1:]:
        result = result + part
    return result[:, :length], [part[:, length:] for part in came]


def rms_scale(values):
    return lax.rsqrt(jnp.mean(values * values, axis=1, keepdims=True) + EPSILON)


def rms_back(grad_normed, branch, scales, gains):
    weighted = grad_normed * gains
    inner = jnp.mean(weighted * branch, axis=1, keepdims=True)
    grad_branch = scales * weighted - branch * (scales * scales * scales) * inner
    grad_gains = jnp.sum(grad_normed * branch * scales, axis=0)
    return grad_branch, grad_gains


def turn(values, cosine, sine):
    return values * cosine + pltpu.roll(values, values.shape[-1] // 2, 1) * sine


def kernel_dot(a, b, dims):
    return lax.dot_general(a, b, (dims, ((), ())), preferred_element_type=F32)


def softmax_parts(queries, keys, doc_rows, slot_rows, lines):
    scores = kernel_dot(queries, keys, ((1,), (1,))) * (HEAD**-0.5)
    allowed = (doc_rows == lines[2:3, :]) & (lines[3:4, :] <= slot_rows)
    scores = jnp.where(allowed, scores, MASKED)
    weights = jnp.exp(scores - jnp.max(scores, axis=1, keepdims=True))
    return weights * (1.0 / jnp.sum(weights, axis=1, keepdims=True))


def place_of(block, here, n_col):
    row, index = block // n_col, block % n_col
    step = lax.rem(index + n_col - here, n_col)
    if n_col == 4:
        step = jnp.where((here == 3) & (step % 2 == 1), 4 - step, step)
    return step, row


def forward_kernel(
    sizes,
    here_ref,
    query_ref,
    key_ref,
    value_ref,
    lines_ref,
    query_gain_ref,
    key_gain_ref,
    cosine_ref,
    sine_ref,
    query_rot_ref,
    key_rot_ref,
    value_low_ref,
    mixture_ref,
):
    n_row, n_col, small, large = sizes
    cosine, sine, lines = cosine_ref[...], sine_ref[...], lines_ref[...]
    columns = jnp.transpose(lines)
    normed = query_ref[...] * columns[:, 0:1] * query_gain_ref[...]
    query_rot_ref[...] = turn(normed, cosine, sine).astype(BF)
    normed = key_ref[...] * columns[:, 1:2] * key_gain_ref[...]
    key_rot_ref[...] = turn(normed, cosine, sine).astype(BF)
    value_low_ref[...] = value_ref[...].astype(BF)
    keys, values = key_rot_ref[...], value_low_ref[...]
    for start in range(0, query_ref.shape[0], large):
        rows = slice(start, start + large)
        chances = softmax_parts(
            query_rot_ref[rows, :], keys, columns[rows, 2:3], columns[rows, 3:4], lines
        )
        mixture = kernel_dot(chances.astype(BF), values, ((1,), (0,))).astype(BF)
        for inner in range(0, large, small):
            step, row = place_of((start + inner) // small, here_ref[0], n_col)
            place = pl.multiple_of((step * n_row + row) * small, small)
            mixture_ref[pl.ds(place, small), :] = mixture[inner : inner + small]


def backward_kernel(
    sizes,
    here_ref,
    query_ref,
    key_ref,
    lines_ref,
    query_gain_ref,
    key_gain_ref,
    cosine_ref,
    sine_ref,
    query_rot_ref,
    key_rot_ref,
    value_low_ref,
    grad_ref,
    query_weighted_ref,
    key_weighted_ref,
    grad_value_ref,
    inner_ref,
    query_gain_grad_ref,
    key_gain_grad_ref,
    key_total,
    value_total,
):
    n_row, n_col, small, large = sizes
    cosine, sine, lines = cosine_ref[...], sine_ref[...], lines_ref[...]
    columns = jnp.transpose(lines)
    keys, values = key_rot_ref[...], value_low_ref[...]
    factor = HEAD**-0.5
    for start in range(0, query_ref.shape[0], large):
        rows = slice(start, start + large)
        queries = query_rot_ref[rows, :]
        grads = []
        for inner in range(0, large, small):
            step, row = place_of((start + inner) // small, here_ref[0], n_col)
            place = pl.multiple_of((step * n_row + row) * small, small)
            grads.append(grad_ref[pl.ds(place, small), :])
        grads = jnp.concatenate(grads, axis=0)
        chances = softmax_parts(
            queries, keys, columns[rows, 2:3], columns[rows, 3:4], lines
        )
        value_part = kernel_dot(chances.astype(BF), grads, ((0,), (0,)))
        grad_chances = kernel_dot(grads, values, ((1,), (1,)))
        inner = jnp.sum(chances * grad_chances, axis=1, keepdims=True)
        grad_scores = (chances * (grad_chances - inner)).astype(BF)
        query_weighted_ref[rows, :] = kernel_dot(grad_scores, keys, ((1,), (0,))) * factor
        key_part = kernel_dot(grad_scores, queries, ((0,), (0,))) * factor
        if start == 0:
            value_total[...] = value_part
            key_total[...] = key_part
        else:
            value_total[...] += value_part
            key_total[...] += key_part
    grad_value_ref[...] = value_total[...].astype(BF)
    ones = jnp.ones((8, HEAD), F32)
    inners = []
    for grad, raw_ref, which, gain_ref, weighted_ref, gain_grad_ref in (
        (
            query_weighted_ref[...],
            query_ref,
            0,
            query_gain_ref,
            query_weighted_ref,
            query_gain_grad_ref,
        ),
        (
            key_total[...],
            key_ref,
            1,
            key_gain_ref,
            key_weighted_ref,
            key_gain_grad_ref,
        ),
    ):
        unturned = turn(grad, cosine, -sine)
        raw = raw_ref[...]
        gain_grad_ref[0] = jnp.sum(
            unturned * raw * columns[:, which : which + 1], axis=0, keepdims=True
        )
        weighted = unturned * gain_ref[...]
        weighted_ref[...] = weighted
        inners.append(
            lax.dot_general(
                ones,
                weighted * raw,
                (((1,), (1,)), ((), ())),
                precision=lax.Precision.HIGHEST,
                preferred_element_type=F32,
            )
        )
    which = lax.broadcasted_iota(jnp.int32, inner_ref.shape, 0)
    both = jnp.where(which == 0, inners[0], inners[1])

    @pl.when(pl.program_id(0) == 0)
    def _():
        inner_ref[...] = both

    @pl.when(pl.program_id(0) > 0)
    def _():
        inner_ref[...] += both


def head_specs(length):
    return {
        "head": lambda first: pl.BlockSpec(
            (length, HEAD), lambda h, here, first=first: (0, first + h)
        ),
        "gain": pl.BlockSpec((1, HEAD), lambda h, here: (0, h)),
        "lines": pl.BlockSpec((8, length), lambda h, here: (0, 0)),
        "table": pl.BlockSpec((length, HEAD), lambda h, here: (0, 0)),
        "head_line": pl.BlockSpec((1, 1, HEAD), lambda h, here: (h, 0, 0)),
    }


def attend_forward(row, col, raw, lines, gains, tables):
    length = raw.shape[0]
    heads = raw.shape[1] // (3 * HEAD)
    spec = head_specs(length)
    small = length // (row.size * col.size)
    wide = jax.ShapeDtypeStruct((length, heads * HEAD), BF)
    return pl.pallas_call(
        functools.partial(
            forward_kernel, (row.size, col.size, small, max(small, min(256, length)))
        ),
        grid_spec=pltpu.PrefetchScalarGridSpec(
            num_scalar_prefetch=1,
            grid=(heads,),
            in_specs=[spec["head"](0), spec["head"](heads), spec["head"](2 * heads)]
            + [spec["lines"]]
            + [spec["gain"]] * 2
            + [spec["table"]] * 2,
            out_specs=[spec["head"](0)] * 4,
        ),
        out_shape=[wide] * 4,
        compiler_params=pltpu.CompilerParams(vmem_limit_bytes=56 << 20),
        cost_estimate=pl.CostEstimate(
            flops=heads * 4 * length * length * HEAD,
            bytes_accessed=heads * length * HEAD * 20,
            transcendentals=heads * length * length,
        ),
        name="attend_forward",
    )(col.here.astype(jnp.int32)[None], raw, raw, raw, lines, *gains, *tables)


def attend_backward(row, col, raw, lines, gains, tables, saved, grad):
    length = raw.shape[0]
    heads = raw.shape[1] // (3 * HEAD)
    spec = head_specs(length)
    small = length // (row.size * col.size)
    wide = jax.ShapeDtypeStruct((length, heads * HEAD), F32)
    low = jax.ShapeDtypeStruct((length, heads * HEAD), BF)
    flat = jax.ShapeDtypeStruct((heads, 1, HEAD), F32)
    return pl.pallas_call(
        functools.partial(
            backward_kernel, (row.size, col.size, small, max(small, min(256, length)))
        ),
        grid_spec=pltpu.PrefetchScalarGridSpec(
            num_scalar_prefetch=1,
            grid=(heads,),
            in_specs=[spec["head"](0), spec["head"](heads), spec["lines"]]
            + [spec["gain"]] * 2
            + [spec["table"]] * 2
            + [spec["head"](0)] * 4,
            out_specs=[spec["head"](0)] * 3 + [spec["lines"]] + [spec["head_line"]] * 2,
            scratch_shapes=[pltpu.VMEM((length, HEAD), F32)] * 2,
        ),
        out_shape=[wide, wide, low, jax.ShapeDtypeStruct((8, length), F32), flat, flat],
        compiler_params=pltpu.CompilerParams(vmem_limit_bytes=56 << 20),
        cost_estimate=pl.CostEstimate(
            flops=heads * 10 * length * length * HEAD,
            bytes_accessed=heads * length * HEAD * 30,
            transcendentals=heads * length * length,
        ),
        name="attend_backward",
    )(col.here.astype(jnp.int32)[None], raw, raw, lines, *gains, *tables, *saved, grad)


def device_program(sizes):
    n_dp, n_row, n_col = sizes["dp"], sizes["row"], sizes["col"]

    def per_device(
        layer_input,
        doc_ids,
        positions,
        w_query,
        w_key,
        w_value,
        w_out,
        w_gate,
        w_up,
        w_down,
        gain_query,
        gain_key,
        gain_attn,
        gain_ffn,
        grad_output,
    ):
        row, col = Ring("row", n_row), Ring("col", n_col)
        dp = lax.axis_index("dp")
        length = doc_ids.shape[0]
        row_tokens = layer_input.shape[0]
        own_tokens = row_tokens // n_col
        features = layer_input.shape[1]
        width = features * n_col
        head_cols = w_query.shape[1] // n_col
        hidden_cols = w_gate.shape[1] // n_col
        in_rows = features // n_dp
        out_rows = head_cols // n_dp
        down_rows = hidden_cols // n_dp

        def gather_dp(values):
            return lax.all_gather(values, "dp", axis=0, tiled=True)

        steps = [1 << bit for bit in range(n_dp.bit_length() - 1)]

        def partner(values, step):
            return lax.ppermute(values, "dp", [(i, i ^ step) for i in range(n_dp)])

        class GroupSum:
            def __init__(self, block_for):
                blocks = [block_for(dp ^ d) for d in range(n_dp)]
                self.halves = [
                    (dict(enumerate(left for left, _ in blocks)), list(steps)),
                    (dict(enumerate(right for _, right in blocks)), list(steps[::-1])),
                ]
                self.came = None
                self.send()

            def send(self):
                self.came = []
                for blocks, order in self.halves:
                    given = [blocks[d] for d in sorted(blocks) if d & order[0]]
                    self.came.append(partner(jnp.stack(given), order[0]))

            def land(self, chain, more=True):
                self.came, chain = lax.optimization_barrier((self.came, chain))
                for (blocks, order), came in zip(self.halves, self.came):
                    step = order.pop(0)
                    for place, d in enumerate([d for d in sorted(blocks) if d & step]):
                        kept = blocks[d ^ step].astype(F32) + came[place].astype(F32)
                        blocks[d ^ step] = kept.astype(BF)
                        del blocks[d]
                if self.halves[0][1]:
                    self.send()
                return chain

            def finish(self, chain):
                while self.halves[0][1]:
                    chain = self.land(chain)
                return [blocks[0] for blocks, _ in self.halves], chain

        def gather_four(values, beside=()):
            half = values.shape[0] // 2
            one, two = partner(values, 1), partner(values, 2)
            (one, two), beside = lax.optimization_barrier(((one, two), beside))
            far = [partner(one[:half], 2), partner(two[half:], 1)]
            return [[values], [one], [two], far], beside

        def halves_of(values):
            half = values.shape[-1] // 2
            return values[..., :half], values[..., half:]

        def qkv_block(index):
            return jnp.concatenate(
                [
                    lax.dynamic_slice(
                        w, (dp * in_rows, index * head_cols), (in_rows, head_cols)
                    )
                    for w in (w_query, w_key, w_value)
                ],
                axis=1,
            )

        def gate_up_block(index):
            return jnp.stack(
                [
                    lax.dynamic_slice(
                        w, (dp * in_rows, index * hidden_cols), (in_rows, hidden_cols)
                    )
                    for w in (w_gate, w_up)
                ]
            )

        def out_block(index):
            return lax.dynamic_slice_in_dim(
                w_out, index * head_cols + dp * out_rows, out_rows, 0
            )

        def down_block(index):
            return lax.dynamic_slice_in_dim(
                w_down, index * hidden_cols + dp * down_rows, down_rows, 0
            )

        def first_block(index):
            out = out_block(index).reshape(out_rows, n_out, -1).swapaxes(0, 1)
            return jnp.concatenate([qkv_block(index), out.reshape(in_rows, -1)], axis=1)

        n_out = in_rows // out_rows
        first_parts = exchange(col, first_block)

        turned_docs = from_here(row, doc_ids, row_tokens, 0)
        turned_positions = from_here(row, positions, row_tokens, 0)
        slots = lax.rem(jnp.arange(length) + row.here * row_tokens, length)
        tables = rope_tables(turned_positions)
        if n_dp == 4:
            pieces, _ = gather_four(jnp.stack(first_parts))
            near, arrived, tables = gather_col(col, layer_input, pieces[1] + pieces[2], tables)
            pieces = pieces[0] + arrived + pieces[3]
            w_qkv, w_out_all = first_weights(dp, col.here, pieces, 3 * head_cols, n_out)
        else:
            near, _, tables = gather_col(col, layer_input, (), tables)
            first = gather_dp(jnp.stack(first_parts)[None])
            w_qkv = first[..., : 3 * head_cols].swapaxes(0, 1).reshape(n_col, features, -1)
            w_out_all = first[..., 3 * head_cols :].reshape(n_dp, n_col, n_out, out_rows, -1)
            w_out_all = w_out_all.transpose(0, 3, 1, 2, 4).reshape(head_cols, width)
            w_out_all = to_order(col, w_out_all, features, 1)
        w_qkv = [w_qkv[k] for k in range(n_col)]
        input_rows = [
            jnp.concatenate([row.fetch(block, j) for j in range(n_row)], axis=0)
            for block in near
        ]
        own_input = own_rows(col, near).astype(F32)

        w_down = after(w_down, near)
        down_parts = exchange(col, down_block)

        raw = sum(dot(rows, w) for rows, w in zip(input_rows, w_qkv))
        query_raw = raw[:, :head_cols]
        key_raw = raw[:, head_cols : 2 * head_cols]
        squares = jnp.stack(
            [jnp.sum(query_raw * query_raw, axis=1), jnp.sum(key_raw * key_raw, axis=1)]
        )
        gains = jnp.stack([gain_attn, gain_ffn])
        squares, gains = sum_all(row, col, squares, lambda index: gains)
        squares, w_out_all, down_parts = lax.optimization_barrier(
            (squares, w_out_all, down_parts)
        )
        w_down_all = gather_dp(assemble(col, down_parts, 1))
        gains = assemble(col, gains, 1)
        gain_attn_all, gain_ffn_all = gains[0:1], gains[1:2]
        w_gate, w_up = after((w_gate, w_up), down_parts)
        gate_up_parts = exchange(col, gate_up_block)

        scales = lax.rsqrt(squares / width + EPSILON)
        query_scale, key_scale = scales[0][:, None], scales[1][:, None]
        head_gains = (gain_query[None, :], gain_key[None, :])
        marks = jnp.stack([turned_docs, slots]).astype(F32)
        lines = jnp.concatenate([scales, marks, jnp.zeros((4, length), F32)], axis=0)
        *saved, mixture = attend_forward(row, col, raw, lines, head_gains, tables)
        gate_up_parts, mixture = lax.optimization_barrier((gate_up_parts, mixture))
        attended = []
        for k in range(n_col):
            total, *others = (
                dot(block_at(mixture, k * n_row + j, own_tokens, 0), w_out_all)
                for j in range(n_row)
            )
            for j, other in enumerate(others):
                total = total + row.give(other.astype(BF), j + 1).astype(F32)
            attended.append(total)
        gate_up_parts = assemble(
            col, [part[:, None] for part in after(gate_up_parts, w_down_all)], 1
        )
        gate_up_parts, attended = lax.optimization_barrier((gate_up_parts, attended))
        attended, _ = reduce_near(col, attended)
        w_gate_up = lax.all_gather(gate_up_parts[:, :, None], "dp", axis=2, tiled=True)
        w_gate_up = w_gate_up.reshape(2, width, hidden_cols)
        attn_scale = rms_scale(attended)
        hidden_state = own_input + attended * attn_scale * gain_attn_all

        state_rows, _, w_gate_up = gather_tokens(
            row, col, hidden_state.astype(BF), (), w_gate_up
        )
        w_gate, w_up = w_gate_up[0], w_gate_up[1]
        grad_output = after(grad_output, state_rows)
        cotangent = exchange(
            col, lambda index: block_at(grad_output, index, own_tokens, 0)
        )
        kept, activated = [], []
        for block in state_rows:
            pair = lax.optimization_barrier((dot(block, w_gate), dot(block, w_up)))
            gate_values, up_values = pair
            kept.append(pair)
            activated.append((gate_values * jax.nn.sigmoid(gate_values) * up_values).astype(BF))
        lowered = [sum_rows(row, dot(block, w_down_all)) for block in activated]
        lowered, cotangent = lax.optimization_barrier((lowered, cotangent))
        cotangent = assemble(col, cotangent, 1).astype(F32)
        lowered, _ = reduce_near(col, lowered)
        ffn_scale = rms_scale(lowered)
        own_output = (hidden_state + lowered * ffn_scale * gain_ffn_all).astype(BF)

        grad_lowered, grad_gain_ffn = rms_back(cotangent, lowered, ffn_scale, gain_ffn_all)
        lowered_rows, _, _ = gather_tokens(row, col, grad_lowered.astype(BF))
        gate_grads, up_grads, state_part = [], [], []
        for block, (gate_values, up_values) in zip(lowered_rows, kept):
            sigmoid_gate = jax.nn.sigmoid(gate_values)
            grad_activated = dot_nt(block, w_down_all)
            grad_gate = (
                grad_activated
                * up_values
                * (sigmoid_gate * (1.0 + gate_values * (1.0 - sigmoid_gate)))
            )
            grad_up = grad_activated * (gate_values * sigmoid_gate)
            pair = lax.optimization_barrier((grad_gate.astype(BF), grad_up.astype(BF)))
            gate_grads.append(pair[0])
            up_grads.append(pair[1])
            state_part.append(sum_rows(row, dot_nt(pair[0], w_gate) + dot_nt(pair[1], w_up)))
        wide = (
            jnp.concatenate(activated),
            jnp.concatenate(lowered_rows),
            jnp.concatenate(state_rows),
            jnp.concatenate(gate_grads),
            jnp.concatenate(up_grads),
        )
        activated, lowered_rows, state_rows, gate_grads, up_grads = after(wide, state_part)
        grad_w_down = dot_tn(activated, lowered_rows).astype(BF)
        down_sum = GroupSum(
            lambda index: halves_of(block_at(grad_w_down, index, down_rows, 0))
        )
        gate_up_grads = [
            dot_tn(after(state_rows, grad_w_down), grads)
            .astype(BF)
            .reshape(n_col, n_dp, in_rows, hidden_cols)
            for grads in (gate_grads, up_grads)
        ]
        state_part, gate_up_grads = reduce_near(col, state_part, gate_up_grads)
        gate_up_sum = GroupSum(
            lambda index: [
                lax.dynamic_index_in_dim(grads, index, 1, False) for grads in gate_up_grads
            ]
        )
        state_part = down_sum.land(state_part)
        grad_state = cotangent + state_part
        grad_attended, grad_gain_attn = rms_back(
            grad_state, attended, attn_scale, gain_attn_all
        )

        def second_step(came):
            gate_up_sum.came = came
            gate_up_sum.land(())
            return gate_up_sum.came, down_sum.came

        attended_rows, _, (gate_up_sum.came, down_sum.came) = gather_tokens(
            row, col, grad_attended.astype(BF), gate_up_sum.came, second_step
        )
        down_parts, _ = down_sum.finish(())
        down_parts = jnp.concatenate(down_parts, axis=1)
        down_parts = exchange(
            col, lambda index, whole=down_parts: block_at(whole, index, features, 1)
        )
        gate_up_sum, _ = gate_up_sum.finish(())

        grad_mixture = [dot_nt(block, w_out_all).astype(BF) for block in attended_rows]
        attended_rows = jnp.concatenate(attended_rows)
        grad_mixture = jnp.concatenate(grad_mixture)
        (
            query_weighted,
            key_weighted,
            grad_value,
            inner,
            grad_gain_query,
            grad_gain_key,
        ) = attend_backward(row, col, raw, lines, head_gains, tables, saved, grad_mixture)
        down_parts, inner = lax.optimization_barrier((down_parts, inner))
        down_back = assemble(col, [part[None] for part in down_parts], 0)
        down_all = gather_dp(down_back[None])
        small = jnp.stack([grad_gain_attn, grad_gain_ffn])
        inner, small = sum_all(row, col, inner[:2], lambda index: block_at(small, index, features, 1))
        inner = inner / width
        gate_up_whole = after(jnp.stack(gate_up_sum), inner)
        gate_up_parts = exchange(
            col, lambda index: lax.dynamic_index_in_dim(gate_up_whole, index, 1, False)
        )
        small = sum(small[1:], small[0])
        head_gain_grads = [grad_gain_query.reshape(-1), grad_gain_key.reshape(-1)]
        small = sum((row.fetch(small, j) for j in range(1, n_row)), small)
        small = jnp.concatenate([small, jnp.stack(head_gain_grads)], axis=1)
        for step in steps:
            small = small + partner(small, step)
        grad_query = (
            query_scale * query_weighted
            - query_raw * (query_scale * query_scale * query_scale) * inner[0][:, None]
        )
        grad_key = (
            key_scale * key_weighted
            - key_raw * (key_scale * key_scale * key_scale) * inner[1][:, None]
        )
        grad_qkv = jnp.concatenate(
            [grad_query.astype(BF), grad_key.astype(BF), grad_value], axis=1
        )
        grad_w_qkv = jnp.stack([dot_tn(rows, grad_qkv).astype(BF) for rows in input_rows])
        qkv_grads = grad_w_qkv.reshape(n_col, n_dp, in_rows, 3 * head_cols)
        out_grads = dot_tn(mixture, after(attended_rows, inner)).astype(BF)
        out_grads = out_grads.reshape(n_dp, out_rows, n_col, n_out, -1)
        out_grads = out_grads.transpose(2, 0, 3, 1, 4).reshape(n_col, n_dp, in_rows, -1)
        out_grads = from_here(col, out_grads, 1, 0)

        def last_block(index):
            return halves_of(
                jnp.concatenate(
                    [
                        lax.dynamic_index_in_dim(grads, index, 1, False)
                        for grads in (qkv_grads, out_grads)
                    ],
                    axis=-1,
                )
            )

        qkv_grads, out_grads, small, gate_up_parts, grad_qkv = lax.optimization_barrier(
            (qkv_grads, out_grads, small, gate_up_parts, grad_qkv)
        )
        last_sum = GroupSum(last_block)
        gate_up_back = assemble(
            col, [part[None] for part in after(gate_up_parts, down_back)], 0
        )
        gate_up_all = gather_dp(gate_up_back[None])
        input_part = [sum_rows(row, dot_nt(grad_qkv, w)) for w in w_qkv]
        gate_up_back, input_part = lax.optimization_barrier((gate_up_back, input_part))
        grad_input, last_sum.came = reduce_near(
            col, by_arrival(col, input_part), last_sum.came
        )
        last_sum, _ = last_sum.finish(())
        last_sum = jnp.concatenate(last_sum, axis=-1)
        last_parts = [col.fetch(last_sum[-k % n_col], k) for k in range(n_col)]
        grad_w_down = down_all.swapaxes(0, 1).reshape(w_down.shape).astype(F32)
        last_parts, grad_w_down, grad_input = lax.optimization_barrier(
            (last_parts, grad_w_down, grad_input)
        )
        own_output, grad_state = after((own_output, grad_state), last_parts)
        own_state = grad_state.astype(BF)
        output_parts = exchange(col, lambda index: block_at(own_output, index, features, 1))
        state_parts = exchange(col, lambda index: block_at(own_state, index, features, 1))
        grad_w_wide = (
            *pair_gradients(gate_up_all),
            grad_w_down,
        )
        if n_dp == 4:
            pieces, (output_parts, state_parts) = gather_four(
                jnp.stack(last_parts), (output_parts, state_parts)
            )
            pieces, grad_w_wide = lax.optimization_barrier((pieces, grad_w_wide))
            (grad_w_query, grad_w_key, grad_w_value), grad_w_out = last_gradients(
                dp, col.here, sum(pieces, []), head_cols, n_out
            )
        else:
            last_parts = assemble(col, [part[None] for part in last_parts], 0)
            last_all = gather_dp(after(last_parts, gate_up_all)[None])

            def columns_of(whole):
                return jnp.concatenate(
                    [whole[:, k].reshape(features, -1) for k in range(n_col)], axis=1
                ).astype(F32)

            grad_w_query, grad_w_key, grad_w_value = (
                columns_of(last_all[..., i * head_cols : (i + 1) * head_cols])
                for i in range(3)
            )
            out_all = last_all[..., 3 * head_cols :].reshape(
                n_dp, n_col, n_out, out_rows, -1
            )
            grad_w_out = out_all.transpose(1, 0, 3, 2, 4).reshape(w_out.shape).astype(F32)
        grad_w_gate, grad_w_up, grad_w_down = grad_w_wide
        layer_output = assemble(col, output_parts, 0)
        grad_input = grad_input + assemble(col, state_parts, 0).astype(F32)
        return (
            layer_output,
            grad_input,
            grad_w_query,
            grad_w_key,
            grad_w_value,
            grad_w_out,
            grad_w_gate,
            grad_w_up,
            grad_w_down,
            small[0, features:],
            small[1, features:],
            small[0, :features],
            small[1, :features],
        )

    return per_device


def solution(mesh):
    in_specs = (
        P(("dp", "row"), "col"),
        P("dp"),
        P("dp"),
        P("col", "row"),
        P("col", "row"),
        P("col", "row"),
        P("row", "col"),
        P("col", "row"),
        P("col", "row"),
        P("row", "col"),
        P(("row", "col")),
        P(("row", "col")),
        P("col"),
        P("col"),
        P(("dp", "row"), "col"),
    )
    out_specs = (
        P(("dp", "row"), "col"),
        P(("dp", "row"), "col"),
        P("col", "row"),
        P("col", "row"),
        P("col", "row"),
        P("row", "col"),
        P("col", "row"),
        P("col", "row"),
        P("row", "col"),
        P(("row", "col")),
        P(("row", "col")),
        P("col"),
        P("col"),
    )
    return jax.shard_map(
        device_program(dict(mesh.shape)),
        mesh=mesh,
        in_specs=in_specs,
        out_specs=out_specs,
        check_vma=False,
    )
```

```python
import functools
import math

import jax
import jax.numpy as jnp
from jax import lax
from jax.experimental import pallas as pl
from jax.experimental.pallas import tpu as pltpu
from jax.sharding import PartitionSpec as P

HEAD = 128
EPSILON = 1e-06
ROPE_BASE = 500000.0
MASKED = -1e30
BF = jnp.bfloat16
F32 = jnp.float32


def rope_tables(positions):
    digit = 32
    frequency = ROPE_BASE ** (-(jnp.arange(HEAD // 2, dtype=F32) * (2.0 / HEAD)))
    frequency = jnp.concatenate([frequency, frequency])

    def looked_up(index, count, unit):
        angles = (jnp.arange(count) * unit).astype(F32)[:, None] * frequency[None, :]
        table = jnp.concatenate([jnp.cos(angles), jnp.sin(angles)], axis=1)
        chosen = (index[:, None] == jnp.arange(count)[None, :]).astype(F32)
        both = jnp.dot(chosen, table, precision=lax.Precision.HIGHEST)
        return both[:, :HEAD], both[:, HEAD:]

    high_cosine, high_sine = looked_up(
        positions // digit, -(-positions.shape[0] // digit), digit
    )
    low_cosine, low_sine = looked_up(positions % digit, digit, 1)
    signs = jnp.where(jnp.arange(HEAD) < HEAD // 2, -1.0, 1.0).astype(F32)[None, :]
    return (
        high_cosine * low_cosine - high_sine * low_sine,
        (high_sine * low_cosine + high_cosine * low_sine) * signs,
    )


def dot(a, b):
    return jnp.dot(a, b, preferred_element_type=F32)


def dot_nt(a, b):
    return lax.dot_general(a, b, (((1,), (1,)), ((), ())), preferred_element_type=F32)


def dot_tn(a, b):
    return lax.dot_general(a, b, (((0,), (0,)), ((), ())), preferred_element_type=F32)


class Ring:
    def __init__(self, name, size):
        self.name, self.size = name, size
        self.here = lax.axis_index(name)

    def fetch(self, values, step):
        if step % self.size == 0:
            return values
        pairs = [(i, (i - step) % self.size) for i in range(self.size)]
        return lax.ppermute(values, self.name, pairs)

    def send(self, values, pairs):
        return lax.ppermute(values, self.name, pairs)

    def give(self, values, step):
        return self.fetch(values, -step)

    def at(self, step):
        return lax.rem(self.here + (step % self.size), self.size)


def after(values, *earlier):
    return lax.optimization_barrier((values, earlier))[0]


def gather_steps(col, values, early=(), beside=()):
    two = col.send(values, [(0, 2), (1, 3), (2, 0), (3, 1)])
    below = col.send(values, [(0, 1), (1, 2), (2, 3)])
    above = col.send(values, [(1, 0), (2, 1), (3, 2)])
    two, early = lax.optimization_barrier((two, early))
    beside = beside(early) if callable(beside) else beside
    two, below, above, beside = lax.optimization_barrier((two, below, above, beside))
    relayed = col.send(two, [(2, 3), (1, 0)])
    return two, below, above, relayed, early, beside


def gather_col(col, values, early, beside):
    if col.size != 4:
        return [col.fetch(values, k) for k in range(col.size)], early, beside
    two, below, above, relayed, early, beside = gather_steps(col, values, early, beside)
    near = [
        values,
        jnp.where(col.here == 3, relayed, above),
        two,
        jnp.where(col.here == 0, relayed, below),
    ]
    return near, early, beside


def by_arrival(col, blocks):
    if col.size != 4:
        return blocks
    last = col.here == 3
    return [
        blocks[0],
        jnp.where(last, blocks[3], blocks[1]),
        blocks[2],
        jnp.where(last, blocks[1], blocks[3]),
    ]


def gather_near(col, values, early=(), beside=()):
    if col.size != 4:
        beside = beside(early) if callable(beside) else beside
        return [col.fetch(values, k) for k in range(col.size)], early, beside
    two, below, above, relayed, early, beside = gather_steps(col, values, early, beside)
    inside = (col.here == 1) | (col.here == 2)
    near = [
        values,
        jnp.where(col.here == 3, below, above),
        two,
        jnp.where(inside, below, relayed),
    ]
    return near, early, beside


def reduce_near(col, blocks, between=(), beside=()):
    low = [block.astype(BF) for block in blocks]
    result = blocks[0]
    if col.size != 4:
        for k in range(1, col.size):
            result = result + col.give(low[k], k).astype(F32)
        return result, between, beside
    relayed = col.send(low[3], [(3, 2), (0, 1)])
    below = col.send(low[1], [(0, 1), (1, 2), (2, 3)])
    above = col.send(
        jnp.where(col.here == 3, low[1], low[3]), [(1, 0), (2, 1), (3, 2)]
    )
    two = (blocks[2] + relayed.astype(F32)).astype(BF)
    two, between = lax.optimization_barrier((two, between))
    two = col.send(two, [(0, 2), (1, 3), (2, 0), (3, 1)])
    above, below, beside = lax.optimization_barrier((above, below, beside))
    result = result + above.astype(F32) + below.astype(F32) + two.astype(F32)
    return result, between, beside


def block_at(values, index, size, axis):
    return lax.dynamic_slice_in_dim(values, index * size, size, axis)


def assemble_kernel(here_ref, *refs):
    blocks, whole = refs[:-1], refs[-1]
    for step, block in enumerate(blocks):

        @pl.when(pl.program_id(0) == step)
        def _():
            whole[...] = block[...]


def assemble(ring, blocks, axis):
    shape = list(blocks[0].shape)
    size = len(blocks)
    zeros = (0,) * len(shape)

    def place(step, here):
        return zeros[:axis] + (lax.rem(here[0] + step, size),) + zeros[axis + 1 :]

    block_shape = tuple(shape)
    shape[axis] *= size
    return pl.pallas_call(
        assemble_kernel,
        grid_spec=pltpu.PrefetchScalarGridSpec(
            num_scalar_prefetch=1,
            grid=(size,),
            in_specs=[pl.BlockSpec(block_shape, lambda step, here: zeros)] * size,
            out_specs=pl.BlockSpec(block_shape, place),
        ),
        out_shape=jax.ShapeDtypeStruct(tuple(shape), blocks[0].dtype),
        compiler_params=pltpu.CompilerParams(vmem_limit_bytes=32 << 20),
        cost_estimate=pl.CostEstimate(
            flops=0,
            bytes_accessed=2 * math.prod(shape) * blocks[0].dtype.itemsize,
            transcendentals=0,
        ),
        name="assemble",
    )(ring.here.astype(jnp.int32)[None], *blocks)


def first_weights_kernel(sizes, places_ref, *refs):
    pieces, (in_ref, out_ref) = refs[:-2], refs[-2:]
    n_col, n_out, out_rows, wide = sizes
    features = out_ref.shape[1] // n_col
    narrow = features // n_out

    def store(piece, first):
        for k in range(piece.shape[0]):
            in_ref[first + k] = piece[k, :, :wide]
            start = lax.rem(places_ref[1] + first + k, n_col) * features
            for i in range(n_out):
                place = pl.multiple_of(start + i * narrow, narrow)
                out_ref[:, pl.ds(place, narrow)] = piece[
                    k, i * out_rows : (i + 1) * out_rows, wide:
                ]

    for d in range(3):

        @pl.when(pl.program_id(0) == d)
        def _():
            store(pieces[d], 0)

    @pl.when(pl.program_id(0) == 3)
    def _():
        store(pieces[3], 0)
        store(pieces[4], pieces[3].shape[0])


def first_weights(dp, here, pieces, wide, n_out):
    n_col, in_rows, columns = pieces[0].shape
    out_rows = in_rows // n_out
    features = n_out * (columns - wide)
    whole = [
        pl.BlockSpec(piece.shape, lambda step, places: (0, 0, 0)) for piece in pieces
    ]
    return pl.pallas_call(
        functools.partial(first_weights_kernel, (n_col, n_out, out_rows, wide)),
        grid_spec=pltpu.PrefetchScalarGridSpec(
            num_scalar_prefetch=1,
            grid=(4,),
            in_specs=whole,
            out_specs=[
                pl.BlockSpec(
                    (n_col, in_rows, wide), lambda step, places: (0, places[0] ^ step, 0)
                ),
                pl.BlockSpec(
                    (out_rows, n_col * features), lambda step, places: (places[0] ^ step, 0)
                ),
            ],
        ),
        out_shape=[
            jax.ShapeDtypeStruct((n_col, 4 * in_rows, wide), BF),
            jax.ShapeDtypeStruct((4 * out_rows, n_col * features), BF),
        ],
        compiler_params=pltpu.CompilerParams(vmem_limit_bytes=32 << 20),
        cost_estimate=pl.CostEstimate(
            flops=0, bytes_accessed=8 * n_col * in_rows * columns * 2, transcendentals=0
        ),
        name="first_weights",
    )(jnp.stack([dp, here]).astype(jnp.int32), *pieces)


def pair_gradients_kernel(all_ref, gate_ref, up_ref):
    hidden = all_ref.shape[4]
    for k in range(all_ref.shape[1]):
        place = slice(k * hidden, (k + 1) * hidden)
        gate_ref[:, place] = all_ref[0, k, 0].astype(F32)
        up_ref[:, place] = all_ref[0, k, 1].astype(F32)


def pair_gradients(gathered):
    n_dp, n_col, pair, rows, hidden = gathered.shape
    cut = 2 if rows % 32 == 0 else 1
    side = pl.BlockSpec((rows // cut, n_col * hidden), lambda p, i: (p * cut + i, 0))
    return pl.pallas_call(
        pair_gradients_kernel,
        grid=(n_dp, cut),
        in_specs=[
            pl.BlockSpec((1, n_col, pair, rows // cut, hidden), lambda p, i: (p, 0, 0, i, 0))
        ],
        out_specs=[side, side],
        out_shape=[jax.ShapeDtypeStruct((n_dp * rows, n_col * hidden), F32)] * 2,
        compiler_params=pltpu.CompilerParams(vmem_limit_bytes=56 << 20),
        cost_estimate=pl.CostEstimate(
            flops=0, bytes_accessed=6 * math.prod(gathered.shape), transcendentals=0
        ),
        name="pair_gradients",
    )(gathered)


def down_gradients_kernel(all_ref, down_ref):
    down_ref[...] = all_ref[...].astype(F32)


def down_gradients(gathered):
    n_dp, n_col, rows, features = gathered.shape
    block = (1, 1, rows, features)
    whole = pl.pallas_call(
        down_gradients_kernel,
        grid=(n_dp, n_col),
        in_specs=[pl.BlockSpec(block, lambda p, z: (p, z, 0, 0))],
        out_specs=pl.BlockSpec(block, lambda p, z: (z, p, 0, 0)),
        out_shape=jax.ShapeDtypeStruct((n_col, n_dp, rows, features), F32),
        compiler_params=pltpu.CompilerParams(vmem_limit_bytes=56 << 20),
        cost_estimate=pl.CostEstimate(
            flops=0, bytes_accessed=6 * math.prod(gathered.shape), transcendentals=0
        ),
        name="down_gradients",
    )(gathered)
    return whole.reshape(-1, features)


def last_gradients_kernel(n_out, places_ref, *refs):
    pieces, outs = refs[:-4], refs[-4:]
    n_col = pieces[0].shape[0]
    features = outs[3].shape[3]
    head_cols = outs[0].shape[1] // n_col
    narrow = features // n_out

    def store(piece, first):
        rows = piece.shape[1] // n_out
        for k in range(piece.shape[0]):
            source = lax.rem(places_ref[1] + first + k, n_col)
            place = pl.ds(pl.multiple_of(source * head_cols, head_cols), head_cols)
            for i in range(3):
                outs[i][:, place] = piece[k, :, i * head_cols : (i + 1) * head_cols].astype(F32)
            for i in range(n_out):
                outs[3][source, 0, :, i * narrow : (i + 1) * narrow] = piece[
                    k, i * rows : (i + 1) * rows, 3 * head_cols :
                ].astype(F32)

    for d in range(3):

        @pl.when(pl.program_id(0) == d)
        def _():
            store(pieces[d], 0)

    @pl.when(pl.program_id(0) == 3)
    def _():
        store(pieces[3], 0)
        store(pieces[4], pieces[3].shape[0])


def last_gradients(dp, here, pieces, head_cols, n_out):
    n_col, rows, columns = pieces[0].shape
    features = n_out * (columns - 3 * head_cols)
    side = pl.BlockSpec(
        (rows, n_col * head_cols), lambda step, places: (places[0] ^ step, 0)
    )
    side_shape = jax.ShapeDtypeStruct((4 * rows, n_col * head_cols), F32)
    *sides, out = pl.pallas_call(
        functools.partial(last_gradients_kernel, n_out),
        grid_spec=pltpu.PrefetchScalarGridSpec(
            num_scalar_prefetch=1,
            grid=(4,),
            in_specs=[
                pl.BlockSpec(piece.shape, lambda step, places: (0, 0, 0)) for piece in pieces
            ],
            out_specs=[side] * 3
            + [
                pl.BlockSpec(
                    (n_col, 1, rows // n_out, features),
                    lambda step, places: (0, places[0] ^ step, 0, 0),
                )
            ],
        ),
        out_shape=[side_shape] * 3
        + [jax.ShapeDtypeStruct((n_col, 4, rows // n_out, features), F32)],
        compiler_params=pltpu.CompilerParams(vmem_limit_bytes=56 << 20),
        cost_estimate=pl.CostEstimate(
            flops=0, bytes_accessed=24 * n_col * rows * columns, transcendentals=0
        ),
        name="last_gradients",
    )(jnp.stack([dp, here]).astype(jnp.int32), *pieces)
    return sides, out.reshape(-1, features)


def own_block_kernel(here_ref, *refs):
    blocks, whole = refs[:-1], refs[-1]
    for step, block in enumerate(blocks):

        @pl.when(pl.program_id(0) == step)
        def _():
            whole[...] = block[...]


def own_rows(ring, blocks):
    size = len(blocks)
    rows, columns = blocks[0].shape[0] // size, blocks[0].shape[1]
    return pl.pallas_call(
        own_block_kernel,
        grid_spec=pltpu.PrefetchScalarGridSpec(
            num_scalar_prefetch=1,
            grid=(size,),
            in_specs=[pl.BlockSpec((rows, columns), lambda step, here: (here[0], 0))] * size,
            out_specs=pl.BlockSpec(
                (rows, columns), lambda step, here: (0, lax.rem(here[0] + step, size))
            ),
        ),
        out_shape=jax.ShapeDtypeStruct((rows, columns * size), blocks[0].dtype),
        compiler_params=pltpu.CompilerParams(vmem_limit_bytes=32 << 20),
        name="own_rows",
    )(ring.here.astype(jnp.int32)[None], *blocks)


def from_here(ring, values, size, axis):
    twice = jnp.concatenate([values, values], axis=axis)
    return lax.dynamic_slice_in_dim(twice, ring.here * size, size * ring.size, axis)


def to_order(ring, values, size, axis):
    twice = jnp.concatenate([values, values], axis=axis)
    start = lax.rem(ring.size - ring.here, ring.size) * size
    return lax.dynamic_slice_in_dim(twice, start, size * ring.size, axis)


def exchange(ring, block_for):
    return [ring.fetch(block_for(ring.at(-step)), step) for step in range(ring.size)]


def gather_tokens(row, col, values, early=(), beside=()):
    near, early, beside = gather_near(col, values, early, beside)
    blocks = [
        jnp.concatenate([row.fetch(block, j) for j in range(row.size)], axis=0)
        for block in near
    ]
    return blocks, early, beside


def sum_rows(row, partial):
    size = partial.shape[0] // row.size
    total = partial[:size]
    for j in range(1, row.size):
        total = total + row.give(partial[j * size : (j + 1) * size].astype(BF), j).astype(F32)
    return total


def sum_all(row, col, values, block_for):
    length = values.shape[1]
    size = length // row.size
    total = values
    for j in range(1, row.size):
        total = total + jnp.roll(row.fetch(values, j), j * size, axis=1)
    came = [
        col.fetch(jnp.concatenate([total, block_for(col.at(-k))], axis=1), k)
        for k in range(col.size)
    ]
    result = came[0]
    for part in came[1:]:
        result = result + part
    return result[:, :length], [part[:, length:] for part in came]


def rms_scale(values):
    return lax.rsqrt(jnp.mean(values * values, axis=1, keepdims=True) + EPSILON)


def rms_back(grad_normed, branch, scales, gains):
    weighted = grad_normed * gains
    inner = jnp.mean(weighted * branch, axis=1, keepdims=True)
    grad_branch = scales * weighted - branch * (scales * scales * scales) * inner
    grad_gains = jnp.sum(grad_normed * branch * scales, axis=0)
    return grad_branch, grad_gains


def turn(values, cosine, sine):
    return values * cosine + pltpu.roll(values, values.shape[-1] // 2, 1) * sine


def kernel_dot(a, b, dims):
    return lax.dot_general(a, b, (dims, ((), ())), preferred_element_type=F32)


def softmax_parts(queries, keys, doc_rows, slot_rows, lines):
    scores = kernel_dot(queries, keys, ((1,), (1,))) * (HEAD**-0.5)
    allowed = (doc_rows == lines[2:3, :]) & (lines[3:4, :] <= slot_rows)
    scores = jnp.where(allowed, scores, MASKED)
    weights = jnp.exp(scores - jnp.max(scores, axis=1, keepdims=True))
    return weights * (1.0 / jnp.sum(weights, axis=1, keepdims=True))


def place_of(block, here, n_col):
    row, index = block // n_col, block % n_col
    step = lax.rem(index + n_col - here, n_col)
    if n_col == 4:
        step = jnp.where((here == 3) & (step % 2 == 1), 4 - step, step)
    return step, row


def forward_kernel(
    sizes,
    here_ref,
    query_ref,
    key_ref,
    value_ref,
    lines_ref,
    query_gain_ref,
    key_gain_ref,
    cosine_ref,
    sine_ref,
    query_rot_ref,
    key_rot_ref,
    value_low_ref,
    mixture_ref,
):
    n_row, n_col, small, large = sizes
    cosine, sine, lines = cosine_ref[...], sine_ref[...], lines_ref[...]
    columns = jnp.transpose(lines)
    normed = query_ref[...] * columns[:, 0:1] * query_gain_ref[...]
    query_rot_ref[...] = turn(normed, cosine, sine).astype(BF)
    normed = key_ref[...] * columns[:, 1:2] * key_gain_ref[...]
    key_rot_ref[...] = turn(normed, cosine, sine).astype(BF)
    value_low_ref[...] = value_ref[...].astype(BF)
    keys, values = key_rot_ref[...], value_low_ref[...]
    for start in range(0, query_ref.shape[0], large):
        rows = slice(start, start + large)
        chances = softmax_parts(
            query_rot_ref[rows, :], keys, columns[rows, 2:3], columns[rows, 3:4], lines
        )
        mixture = kernel_dot(chances.astype(BF), values, ((1,), (0,))).astype(BF)
        for inner in range(0, large, small):
            step, row = place_of((start + inner) // small, here_ref[0], n_col)
            place = pl.multiple_of((step * n_row + row) * small, small)
            mixture_ref[pl.ds(place, small), :] = mixture[inner : inner + small]


def backward_kernel(
    sizes,
    here_ref,
    query_ref,
    key_ref,
    lines_ref,
    query_gain_ref,
    key_gain_ref,
    cosine_ref,
    sine_ref,
    query_rot_ref,
    key_rot_ref,
    value_low_ref,
    grad_ref,
    query_weighted_ref,
    key_weighted_ref,
    grad_value_ref,
    inner_ref,
    query_gain_grad_ref,
    key_gain_grad_ref,
    key_total,
    value_total,
):
    n_row, n_col, small, large = sizes
    cosine, sine, lines = cosine_ref[...], sine_ref[...], lines_ref[...]
    columns = jnp.transpose(lines)
    keys, values = key_rot_ref[...], value_low_ref[...]
    factor = HEAD**-0.5
    for start in range(0, query_ref.shape[0], large):
        rows = slice(start, start + large)
        queries = query_rot_ref[rows, :]
        grads = []
        for inner in range(0, large, small):
            step, row = place_of((start + inner) // small, here_ref[0], n_col)
            place = pl.multiple_of((step * n_row + row) * small, small)
            grads.append(grad_ref[pl.ds(place, small), :])
        grads = jnp.concatenate(grads, axis=0)
        chances = softmax_parts(
            queries, keys, columns[rows, 2:3], columns[rows, 3:4], lines
        )
        value_part = kernel_dot(chances.astype(BF), grads, ((0,), (0,)))
        grad_chances = kernel_dot(grads, values, ((1,), (1,)))
        inner = jnp.sum(chances * grad_chances, axis=1, keepdims=True)
        grad_scores = (chances * (grad_chances - inner)).astype(BF)
        query_weighted_ref[rows, :] = kernel_dot(grad_scores, keys, ((1,), (0,))) * factor
        key_part = kernel_dot(grad_scores, queries, ((0,), (0,))) * factor
        if start == 0:
            value_total[...] = value_part
            key_total[...] = key_part
        else:
            value_total[...] += value_part
            key_total[...] += key_part
    grad_value_ref[...] = value_total[...].astype(BF)
    ones = jnp.ones((8, HEAD), F32)
    inners = []
    for grad, raw_ref, which, gain_ref, weighted_ref, gain_grad_ref in (
        (
            query_weighted_ref[...],
            query_ref,
            0,
            query_gain_ref,
            query_weighted_ref,
            query_gain_grad_ref,
        ),
        (
            key_total[...],
            key_ref,
            1,
            key_gain_ref,
            key_weighted_ref,
            key_gain_grad_ref,
        ),
    ):
        unturned = turn(grad, cosine, -sine)
        raw = raw_ref[...]
        gain_grad_ref[0] = jnp.sum(
            unturned * raw * columns[:, which : which + 1], axis=0, keepdims=True
        )
        weighted = unturned * gain_ref[...]
        weighted_ref[...] = weighted
        inners.append(
            lax.dot_general(
                ones,
                weighted * raw,
                (((1,), (1,)), ((), ())),
                precision=lax.Precision.HIGHEST,
                preferred_element_type=F32,
            )
        )
    which = lax.broadcasted_iota(jnp.int32, inner_ref.shape, 0)
    both = jnp.where(which == 0, inners[0], inners[1])

    @pl.when(pl.program_id(0) == 0)
    def _():
        inner_ref[...] = both

    @pl.when(pl.program_id(0) > 0)
    def _():
        inner_ref[...] += both


def head_specs(length):
    return {
        "head": lambda first: pl.BlockSpec(
            (length, HEAD), lambda h, here, first=first: (0, first + h)
        ),
        "gain": pl.BlockSpec((1, HEAD), lambda h, here: (0, h)),
        "lines": pl.BlockSpec((8, length), lambda h, here: (0, 0)),
        "table": pl.BlockSpec((length, HEAD), lambda h, here: (0, 0)),
        "head_line": pl.BlockSpec((1, 1, HEAD), lambda h, here: (h, 0, 0)),
    }


def attend_forward(row, col, raw, lines, gains, tables):
    length = raw.shape[0]
    heads = raw.shape[1] // (3 * HEAD)
    spec = head_specs(length)
    small = length // (row.size * col.size)
    wide = jax.ShapeDtypeStruct((length, heads * HEAD), BF)
    return pl.pallas_call(
        functools.partial(
            forward_kernel, (row.size, col.size, small, max(small, min(256, length)))
        ),
        grid_spec=pltpu.PrefetchScalarGridSpec(
            num_scalar_prefetch=1,
            grid=(heads,),
            in_specs=[spec["head"](0), spec["head"](heads), spec["head"](2 * heads)]
            + [spec["lines"]]
            + [spec["gain"]] * 2
            + [spec["table"]] * 2,
            out_specs=[spec["head"](0)] * 4,
        ),
        out_shape=[wide] * 4,
        compiler_params=pltpu.CompilerParams(vmem_limit_bytes=56 << 20),
        cost_estimate=pl.CostEstimate(
            flops=heads * 4 * length * length * HEAD,
            bytes_accessed=heads * length * HEAD * 20,
            transcendentals=heads * length * length,
        ),
        name="attend_forward",
    )(col.here.astype(jnp.int32)[None], raw, raw, raw, lines, *gains, *tables)


def attend_backward(row, col, raw, lines, gains, tables, saved, grad):
    length = raw.shape[0]
    heads = raw.shape[1] // (3 * HEAD)
    spec = head_specs(length)
    small = length // (row.size * col.size)
    wide = jax.ShapeDtypeStruct((length, heads * HEAD), F32)
    low = jax.ShapeDtypeStruct((length, heads * HEAD), BF)
    flat = jax.ShapeDtypeStruct((heads, 1, HEAD), F32)
    return pl.pallas_call(
        functools.partial(
            backward_kernel, (row.size, col.size, small, max(small, min(256, length)))
        ),
        grid_spec=pltpu.PrefetchScalarGridSpec(
            num_scalar_prefetch=1,
            grid=(heads,),
            in_specs=[spec["head"](0), spec["head"](heads), spec["lines"]]
            + [spec["gain"]] * 2
            + [spec["table"]] * 2
            + [spec["head"](0)] * 4,
            out_specs=[spec["head"](0)] * 3 + [spec["lines"]] + [spec["head_line"]] * 2,
            scratch_shapes=[pltpu.VMEM((length, HEAD), F32)] * 2,
        ),
        out_shape=[wide, wide, low, jax.ShapeDtypeStruct((8, length), F32), flat, flat],
        compiler_params=pltpu.CompilerParams(vmem_limit_bytes=56 << 20),
        cost_estimate=pl.CostEstimate(
            flops=heads * 10 * length * length * HEAD,
            bytes_accessed=heads * length * HEAD * 30,
            transcendentals=heads * length * length,
        ),
        name="attend_backward",
    )(col.here.astype(jnp.int32)[None], raw, raw, lines, *gains, *tables, *saved, grad)


def device_program(sizes):
    n_dp, n_row, n_col = sizes["dp"], sizes["row"], sizes["col"]

    def per_device(
        layer_input,
        doc_ids,
        positions,
        w_query,
        w_key,
        w_value,
        w_out,
        w_gate,
        w_up,
        w_down,
        gain_query,
        gain_key,
        gain_attn,
        gain_ffn,
        grad_output,
    ):
        row, col = Ring("row", n_row), Ring("col", n_col)
        dp = lax.axis_index("dp")
        length = doc_ids.shape[0]
        row_tokens = layer_input.shape[0]
        own_tokens = row_tokens // n_col
        features = layer_input.shape[1]
        width = features * n_col
        head_cols = w_query.shape[1] // n_col
        hidden_cols = w_gate.shape[1] // n_col
        in_rows = features // n_dp
        out_rows = head_cols // n_dp
        down_rows = hidden_cols // n_dp

        def gather_dp(values):
            return lax.all_gather(values, "dp", axis=0, tiled=True)

        steps = [1 << bit for bit in range(n_dp.bit_length() - 1)]

        def partner(values, step):
            return lax.ppermute(values, "dp", [(i, i ^ step) for i in range(n_dp)])

        class GroupSum:
            def __init__(self, block_for):
                blocks = [block_for(dp ^ d) for d in range(n_dp)]
                self.halves = [
                    (dict(enumerate(left for left, _ in blocks)), list(steps)),
                    (dict(enumerate(right for _, right in blocks)), list(steps[::-1])),
                ]
                self.came = None
                self.send()

            def send(self):
                self.came = []
                for blocks, order in self.halves:
                    given = [blocks[d] for d in sorted(blocks) if d & order[0]]
                    self.came.append(partner(jnp.stack(given), order[0]))

            def land(self, chain, more=True):
                self.came, chain = lax.optimization_barrier((self.came, chain))
                for (blocks, order), came in zip(self.halves, self.came):
                    step = order.pop(0)
                    for place, d in enumerate([d for d in sorted(blocks) if d & step]):
                        kept = blocks[d ^ step].astype(F32) + came[place].astype(F32)
                        blocks[d ^ step] = kept.astype(BF)
                        del blocks[d]
                if self.halves[0][1]:
                    self.send()
                return chain

            def finish(self, chain):
                while self.halves[0][1]:
                    chain = self.land(chain)
                return [blocks[0] for blocks, _ in self.halves], chain

        def gather_four(values, beside=()):
            half = values.shape[0] // 2
            one, two = partner(values, 1), partner(values, 2)
            (one, two), beside = lax.optimization_barrier(((one, two), beside))
            far = [partner(one[:half], 2), partner(two[half:], 1)]
            return [[values], [one], [two], far], beside

        def halves_of(values):
            half = values.shape[-1] // 2
            return values[..., :half], values[..., half:]

        def qkv_block(index):
            return jnp.concatenate(
                [
                    lax.dynamic_slice(
                        w, (dp * in_rows, index * head_cols), (in_rows, head_cols)
                    )
                    for w in (w_query, w_key, w_value)
                ],
                axis=1,
            )

        def gate_up_block(index):
            return jnp.stack(
                [
                    lax.dynamic_slice(
                        w, (dp * in_rows, index * hidden_cols), (in_rows, hidden_cols)
                    )
                    for w in (w_gate, w_up)
                ]
            )

        def out_block(index):
            return lax.dynamic_slice_in_dim(
                w_out, index * head_cols + dp * out_rows, out_rows, 0
            )

        def down_block(index):
            return lax.dynamic_slice_in_dim(
                w_down, index * hidden_cols + dp * down_rows, down_rows, 0
            )

        def first_block(index):
            out = out_block(index).reshape(out_rows, n_out, -1).swapaxes(0, 1)
            return jnp.concatenate([qkv_block(index), out.reshape(in_rows, -1)], axis=1)

        n_out = in_rows // out_rows
        first_parts = exchange(col, first_block)

        turned_docs = from_here(row, doc_ids, row_tokens, 0)
        turned_positions = from_here(row, positions, row_tokens, 0)
        slots = lax.rem(jnp.arange(length) + row.here * row_tokens, length)
        tables = rope_tables(turned_positions)
        first_parts, layer_input = lax.optimization_barrier((first_parts, layer_input))
        near, _, tables = gather_col(col, layer_input, (), tables)
        if n_dp == 4:
            pieces, _ = gather_four(jnp.stack(first_parts))
            pieces = sum(pieces, [])
            w_qkv, w_out_all = first_weights(dp, col.here, pieces, 3 * head_cols, n_out)
        else:
            first = gather_dp(jnp.stack(first_parts)[None])
            w_qkv = first[..., : 3 * head_cols].swapaxes(0, 1).reshape(n_col, features, -1)
            w_out_all = first[..., 3 * head_cols :].reshape(n_dp, n_col, n_out, out_rows, -1)
            w_out_all = w_out_all.transpose(0, 3, 1, 2, 4).reshape(head_cols, width)
            w_out_all = to_order(col, w_out_all, features, 1)
        w_down = after(w_down, near)
        down_parts = exchange(col, down_block)
        w_qkv = [w_qkv[k] for k in range(n_col)]
        input_rows = [
            jnp.concatenate([row.fetch(block, j) for j in range(n_row)], axis=0)
            for block in near
        ]
        own_input = own_rows(col, near).astype(F32)

        raw = sum(dot(rows, w) for rows, w in zip(input_rows, w_qkv))
        query_raw = raw[:, :head_cols]
        key_raw = raw[:, head_cols : 2 * head_cols]
        squares = jnp.stack(
            [jnp.sum(query_raw * query_raw, axis=1), jnp.sum(key_raw * key_raw, axis=1)]
        )
        squares, down_parts = lax.optimization_barrier((squares, down_parts))
        down_parts = assemble(col, down_parts, 1)
        gains = jnp.stack([gain_attn, gain_ffn])
        squares, gains = sum_all(row, col, squares, lambda index: gains)
        squares, w_out_all, down_parts = lax.optimization_barrier(
            (squares, w_out_all, down_parts)
        )
        w_down_all = gather_dp(down_parts)
        gains = assemble(col, gains, 1)
        gain_attn_all, gain_ffn_all = gains[0:1], gains[1:2]
        w_gate, w_up = after((w_gate, w_up), squares)
        gate_up_parts = exchange(col, gate_up_block)

        scales = lax.rsqrt(squares / width + EPSILON)
        query_scale, key_scale = scales[0][:, None], scales[1][:, None]
        head_gains = (gain_query[None, :], gain_key[None, :])
        marks = jnp.stack([turned_docs, slots]).astype(F32)
        lines = jnp.concatenate([scales, marks, jnp.zeros((4, length), F32)], axis=0)
        *saved, mixture = attend_forward(row, col, raw, lines, head_gains, tables)
        gate_up_parts[1::2], mixture = lax.optimization_barrier((gate_up_parts[1::2], mixture))
        attended = []
        for k in range(n_col):
            total, *others = (
                dot(block_at(mixture, k * n_row + j, own_tokens, 0), w_out_all)
                for j in range(n_row)
            )
            for j, other in enumerate(others):
                total = total + row.give(other.astype(BF), j + 1).astype(F32)
            attended.append(total)
        gate_up_parts, attended = lax.optimization_barrier((gate_up_parts, attended))
        gate_up_parts = assemble(
            col, [part[:, None] for part in after(gate_up_parts, w_down_all)], 1
        )
        gate_up_parts, attended = lax.optimization_barrier((gate_up_parts, attended))
        attended, _, _ = reduce_near(col, attended)
        w_gate_up = lax.all_gather(gate_up_parts[:, :, None], "dp", axis=2, tiled=True)
        w_gate_up = w_gate_up.reshape(2, width, hidden_cols)
        attn_scale = rms_scale(attended)
        hidden_state = own_input + attended * attn_scale * gain_attn_all

        state_rows, _, w_gate_up = gather_tokens(
            row, col, hidden_state.astype(BF), (), w_gate_up
        )
        w_gate, w_up = w_gate_up[0], w_gate_up[1]
        grad_output = after(grad_output, state_rows)
        cotangent = exchange(
            col, lambda index: block_at(grad_output, index, own_tokens, 0)
        )
        kept, activated = [], []
        for block in state_rows:
            pair = lax.optimization_barrier((dot(block, w_gate), dot(block, w_up)))
            gate_values, up_values = pair
            kept.append(pair)
            activated.append((gate_values * jax.nn.sigmoid(gate_values) * up_values).astype(BF))
        lowered = [sum_rows(row, dot(block, w_down_all)) for block in activated]
        lowered, cotangent = lax.optimization_barrier((lowered, cotangent))
        cotangent = assemble(col, cotangent, 1).astype(F32)
        lowered, _, _ = reduce_near(col, lowered)
        ffn_scale = rms_scale(lowered)
        own_output = (hidden_state + lowered * ffn_scale * gain_ffn_all).astype(BF)

        grad_lowered, grad_gain_ffn = rms_back(cotangent, lowered, ffn_scale, gain_ffn_all)
        lowered_rows, _, _ = gather_tokens(row, col, grad_lowered.astype(BF))
        gate_grads, up_grads, state_part = [], [], []
        for block, (gate_values, up_values) in zip(lowered_rows, kept):
            sigmoid_gate = jax.nn.sigmoid(gate_values)
            grad_activated = dot_nt(block, w_down_all)
            grad_gate = (
                grad_activated
                * up_values
                * (sigmoid_gate * (1.0 + gate_values * (1.0 - sigmoid_gate)))
            )
            grad_up = grad_activated * (gate_values * sigmoid_gate)
            pair = lax.optimization_barrier((grad_gate.astype(BF), grad_up.astype(BF)))
            gate_grads.append(pair[0])
            up_grads.append(pair[1])
            state_part.append(sum_rows(row, dot_nt(pair[0], w_gate) + dot_nt(pair[1], w_up)))
        wide = (
            jnp.concatenate(activated),
            jnp.concatenate(lowered_rows),
            jnp.concatenate(state_rows),
            jnp.concatenate(gate_grads),
            jnp.concatenate(up_grads),
        )
        activated, lowered_rows, state_rows, gate_grads, up_grads = after(wide, state_part)
        grad_w_down = dot_tn(activated, lowered_rows).astype(BF)
        down_sum = GroupSum(
            lambda index: halves_of(block_at(grad_w_down, index, down_rows, 0))
        )
        gate_up_grads = [
            dot_tn(after(state_rows, grad_w_down), grads)
            .astype(BF)
            .reshape(n_col, n_dp, in_rows, hidden_cols)
            for grads in (gate_grads, up_grads)
        ]
        state_part, _, gate_up_grads = reduce_near(
            col, state_part, grad_w_down, gate_up_grads
        )
        gate_up_sum = GroupSum(
            lambda index: [
                lax.dynamic_index_in_dim(grads, index, 1, False) for grads in gate_up_grads
            ]
        )
        state_part = down_sum.land(state_part)
        grad_state = cotangent + state_part
        grad_attended, grad_gain_attn = rms_back(
            grad_state, attended, attn_scale, gain_attn_all
        )
        attended_rows, (gate_up_sum.came, down_sum.came), _ = gather_tokens(
            row, col, grad_attended.astype(BF), (gate_up_sum.came, down_sum.came)
        )
        gate_up_sum.land(())
        gate_up_sum.came, attended_rows = lax.optimization_barrier(
            (gate_up_sum.came, attended_rows)
        )
        down_parts, _ = down_sum.finish(())
        down_parts = jnp.concatenate(down_parts, axis=1)
        down_parts = exchange(
            col, lambda index, whole=down_parts: block_at(whole, index, features, 1)
        )
        gate_up_sum, _ = gate_up_sum.finish(())

        grad_mixture = [dot_nt(block, w_out_all).astype(BF) for block in attended_rows]
        attended_rows = jnp.concatenate(attended_rows)
        grad_mixture = jnp.concatenate(grad_mixture)
        (
            query_weighted,
            key_weighted,
            grad_value,
            inner,
            grad_gain_query,
            grad_gain_key,
        ) = attend_backward(row, col, raw, lines, head_gains, tables, saved, grad_mixture)
        down_parts, inner = lax.optimization_barrier((down_parts, inner))
        down_back = assemble(col, [part[None] for part in down_parts], 0)
        down_all = gather_dp(down_back[None])
        small = jnp.stack([grad_gain_attn, grad_gain_ffn])
        inner, small = sum_all(row, col, inner[:2], lambda index: block_at(small, index, features, 1))
        inner = inner / width
        gate_up_whole = after(jnp.stack(gate_up_sum), inner)
        gate_up_parts = exchange(
            col, lambda index: lax.dynamic_index_in_dim(gate_up_whole, index, 1, False)
        )
        small = sum(small[1:], small[0])
        head_gain_grads = [grad_gain_query.reshape(-1), grad_gain_key.reshape(-1)]
        small = sum((row.fetch(small, j) for j in range(1, n_row)), small)
        small = jnp.concatenate([small, jnp.stack(head_gain_grads)], axis=1)
        for step in steps:
            small = small + partner(small, step)
        grad_query = (
            query_scale * query_weighted
            - query_raw * (query_scale * query_scale * query_scale) * inner[0][:, None]
        )
        grad_key = (
            key_scale * key_weighted
            - key_raw * (key_scale * key_scale * key_scale) * inner[1][:, None]
        )
        grad_qkv = jnp.concatenate(
            [grad_query.astype(BF), grad_key.astype(BF), grad_value], axis=1
        )
        grad_w_qkv = jnp.stack([dot_tn(rows, grad_qkv).astype(BF) for rows in input_rows])
        qkv_grads = grad_w_qkv.reshape(n_col, n_dp, in_rows, 3 * head_cols)
        out_grads = dot_tn(mixture, after(attended_rows, inner)).astype(BF)
        out_grads = out_grads.reshape(n_dp, out_rows, n_col, n_out, -1)
        out_grads = out_grads.transpose(2, 0, 3, 1, 4).reshape(n_col, n_dp, in_rows, -1)
        out_grads = from_here(col, out_grads, 1, 0)

        def last_block(index):
            return halves_of(
                jnp.concatenate(
                    [
                        lax.dynamic_index_in_dim(grads, index, 1, False)
                        for grads in (qkv_grads, out_grads)
                    ],
                    axis=-1,
                )
            )

        qkv_grads, out_grads, small, grad_qkv = lax.optimization_barrier(
            (qkv_grads, out_grads, small, grad_qkv)
        )
        last_sum = GroupSum(last_block)
        input_part = [dot_nt(grad_qkv, w) for w in w_qkv]
        gate_up_parts, last_sum.came, input_part = lax.optimization_barrier(
            (gate_up_parts, last_sum.came, input_part)
        )
        last_sum.land(())
        gate_up_back = assemble(
            col, [part[None] for part in after(gate_up_parts, down_back)], 0
        )
        gate_up_all = gather_dp(gate_up_back[None])
        input_part = [sum_rows(row, partial) for partial in input_part]
        gate_up_back, input_part = lax.optimization_barrier((gate_up_back, input_part))
        last_sum, _ = last_sum.finish(())
        last_sum = jnp.concatenate(last_sum, axis=-1)
        last_parts = [col.fetch(last_sum[-k % n_col], k) for k in range(n_col)]
        grad_w_down = down_gradients(down_all)
        grad_input, (last_parts, grad_w_down), _ = reduce_near(
            col, by_arrival(col, input_part), (last_parts, grad_w_down)
        )
        own_output, grad_state = after((own_output, grad_state), last_parts)
        own_state = grad_state.astype(BF)
        output_parts = exchange(col, lambda index: block_at(own_output, index, features, 1))
        state_parts = exchange(col, lambda index: block_at(own_state, index, features, 1))
        grad_w_wide = (
            *pair_gradients(gate_up_all),
            grad_w_down,
        )
        if n_dp == 4:
            pieces, (output_parts, state_parts) = gather_four(
                jnp.stack(last_parts), (output_parts, state_parts)
            )
            pieces, grad_w_wide = lax.optimization_barrier((pieces, grad_w_wide))
            (grad_w_query, grad_w_key, grad_w_value), grad_w_out = last_gradients(
                dp, col.here, sum(pieces, []), head_cols, n_out
            )
        else:
            last_parts = assemble(col, [part[None] for part in last_parts], 0)
            last_all = gather_dp(after(last_parts, gate_up_all)[None])

            def columns_of(whole):
                return jnp.concatenate(
                    [whole[:, k].reshape(features, -1) for k in range(n_col)], axis=1
                ).astype(F32)

            grad_w_query, grad_w_key, grad_w_value = (
                columns_of(last_all[..., i * head_cols : (i + 1) * head_cols])
                for i in range(3)
            )
            out_all = last_all[..., 3 * head_cols :].reshape(
                n_dp, n_col, n_out, out_rows, -1
            )
            grad_w_out = out_all.transpose(1, 0, 3, 2, 4).reshape(w_out.shape).astype(F32)
        grad_w_gate, grad_w_up, grad_w_down = grad_w_wide
        layer_output = assemble(col, output_parts, 0)
        grad_input = grad_input + assemble(col, state_parts, 0).astype(F32)
        return (
            layer_output,
            grad_input,
            grad_w_query,
            grad_w_key,
            grad_w_value,
            grad_w_out,
            grad_w_gate,
            grad_w_up,
            grad_w_down,
            small[0, features:],
            small[1, features:],
            small[0, :features],
            small[1, :features],
        )

    return per_device


def solution(mesh):
    in_specs = (
        P(("dp", "row"), "col"),
        P("dp"),
        P("dp"),
        P("col", "row"),
        P("col", "row"),
        P("col", "row"),
        P("row", "col"),
        P("col", "row"),
        P("col", "row"),
        P("row", "col"),
        P(("row", "col")),
        P(("row", "col")),
        P("col"),
        P("col"),
        P(("dp", "row"), "col"),
    )
    out_specs = (
        P(("dp", "row"), "col"),
        P(("dp", "row"), "col"),
        P("col", "row"),
        P("col", "row"),
        P("col", "row"),
        P("row", "col"),
        P("col", "row"),
        P("col", "row"),
        P("row", "col"),
        P(("row", "col")),
        P(("row", "col")),
        P("col"),
        P("col"),
    )
    return jax.shard_map(
        device_program(dict(mesh.shape)),
        mesh=mesh,
        in_specs=in_specs,
        out_specs=out_specs,
        check_vma=False,
    )
```

```python
import functools
import math

import jax
import jax.numpy as jnp
from jax import lax
from jax.experimental import pallas as pl
from jax.experimental.pallas import tpu as pltpu
from jax.sharding import PartitionSpec as P

HEAD = 128
EPSILON = 1e-06
ROPE_BASE = 500000.0
MASKED = -1e30
BF = jnp.bfloat16
F32 = jnp.float32


def rope_tables(positions):
    digit = 32
    frequency = ROPE_BASE ** (-(jnp.arange(HEAD // 2, dtype=F32) * (2.0 / HEAD)))
    frequency = jnp.concatenate([frequency, frequency])

    def looked_up(index, count, unit):
        angles = (jnp.arange(count) * unit).astype(F32)[:, None] * frequency[None, :]
        table = jnp.concatenate([jnp.cos(angles), jnp.sin(angles)], axis=1)
        chosen = (index[:, None] == jnp.arange(count)[None, :]).astype(F32)
        both = jnp.dot(chosen, table, precision=lax.Precision.HIGHEST)
        return both[:, :HEAD], both[:, HEAD:]

    high_cosine, high_sine = looked_up(
        positions // digit, -(-positions.shape[0] // digit), digit
    )
    low_cosine, low_sine = looked_up(positions % digit, digit, 1)
    signs = jnp.where(jnp.arange(HEAD) < HEAD // 2, -1.0, 1.0).astype(F32)[None, :]
    return (
        high_cosine * low_cosine - high_sine * low_sine,
        (high_sine * low_cosine + high_cosine * low_sine) * signs,
    )


def dot(a, b):
    return jnp.dot(a, b, preferred_element_type=F32)


def dot_nt(a, b):
    return lax.dot_general(a, b, (((1,), (1,)), ((), ())), preferred_element_type=F32)


def dot_tn(a, b):
    return lax.dot_general(a, b, (((0,), (0,)), ((), ())), preferred_element_type=F32)


class Ring:
    def __init__(self, name, size):
        self.name, self.size = name, size
        self.here = lax.axis_index(name)

    def fetch(self, values, step):
        if step % self.size == 0:
            return values
        pairs = [(i, (i - step) % self.size) for i in range(self.size)]
        return lax.ppermute(values, self.name, pairs)

    def send(self, values, pairs):
        return lax.ppermute(values, self.name, pairs)

    def give(self, values, step):
        return self.fetch(values, -step)

    def at(self, step):
        return lax.rem(self.here + (step % self.size), self.size)


def after(values, *earlier):
    return lax.optimization_barrier((values, earlier))[0]


def gather_steps(col, values, early=(), beside=(), late=()):
    two = col.send(values, [(0, 2), (1, 3), (2, 0), (3, 1)])
    below = col.send(values, [(0, 1), (1, 2), (2, 3)])
    above = col.send(values, [(1, 0), (2, 1), (3, 2)])
    two, early = lax.optimization_barrier((two, early))
    two, below, above, beside = lax.optimization_barrier((two, below, above, beside))
    relayed = col.send(two, [(2, 3), (1, 0)])
    relayed, late = lax.optimization_barrier((relayed, late))
    return two, below, above, relayed, early, beside, late


def gather_col(col, values, early, beside):
    if col.size != 4:
        return [col.fetch(values, k) for k in range(col.size)], early, beside
    two, below, above, relayed, early, beside, _ = gather_steps(col, values, early, beside)
    near = [
        values,
        jnp.where(col.here == 3, relayed, above),
        two,
        jnp.where(col.here == 0, relayed, below),
    ]
    return near, early, beside


def by_arrival(col, blocks):
    if col.size != 4:
        return blocks
    last = col.here == 3
    return [
        blocks[0],
        jnp.where(last, blocks[3], blocks[1]),
        blocks[2],
        jnp.where(last, blocks[1], blocks[3]),
    ]


def gather_near(col, values, early=(), late=()):
    if col.size != 4:
        return [col.fetch(values, k) for k in range(col.size)], early, late
    two, below, above, relayed, early, _, late = gather_steps(col, values, early, (), late)
    inside = (col.here == 1) | (col.here == 2)
    near = [
        values,
        jnp.where(col.here == 3, below, above),
        two,
        jnp.where(inside, below, relayed),
    ]
    return near, early, late


def reduce_near(col, blocks, between=(), beside=()):
    low = [block.astype(BF) for block in blocks]
    result = blocks[0]
    if col.size != 4:
        for k in range(1, col.size):
            result = result + col.give(low[k], k).astype(F32)
        return result, between, beside
    relayed = col.send(low[3], [(3, 2), (0, 1)])
    below = col.send(low[1], [(0, 1), (1, 2), (2, 3)])
    above = col.send(
        jnp.where(col.here == 3, low[1], low[3]), [(1, 0), (2, 1), (3, 2)]
    )
    two = (blocks[2] + relayed.astype(F32)).astype(BF)
    two, between = lax.optimization_barrier((two, between))
    two = col.send(two, [(0, 2), (1, 3), (2, 0), (3, 1)])
    above, below, beside = lax.optimization_barrier((above, below, beside))
    result = result + above.astype(F32) + below.astype(F32) + two.astype(F32)
    return result, between, beside


def block_at(values, index, size, axis):
    return lax.dynamic_slice_in_dim(values, index * size, size, axis)


def assemble_kernel(here_ref, *refs):
    blocks, whole = refs[:-1], refs[-1]
    for step, block in enumerate(blocks):

        @pl.when(pl.program_id(0) == step)
        def _():
            whole[...] = block[...]


def assemble(ring, blocks, axis):
    shape = list(blocks[0].shape)
    size = len(blocks)
    zeros = (0,) * len(shape)

    def place(step, here):
        return zeros[:axis] + (lax.rem(here[0] + step, size),) + zeros[axis + 1 :]

    block_shape = tuple(shape)
    shape[axis] *= size
    return pl.pallas_call(
        assemble_kernel,
        grid_spec=pltpu.PrefetchScalarGridSpec(
            num_scalar_prefetch=1,
            grid=(size,),
            in_specs=[pl.BlockSpec(block_shape, lambda step, here: zeros)] * size,
            out_specs=pl.BlockSpec(block_shape, place),
        ),
        out_shape=jax.ShapeDtypeStruct(tuple(shape), blocks[0].dtype),
        compiler_params=pltpu.CompilerParams(vmem_limit_bytes=32 << 20),
        cost_estimate=pl.CostEstimate(
            flops=0,
            bytes_accessed=2 * math.prod(shape) * blocks[0].dtype.itemsize,
            transcendentals=0,
        ),
        name="assemble",
    )(ring.here.astype(jnp.int32)[None], *blocks)


def first_weights_kernel(sizes, places_ref, *refs):
    pieces, (in_ref, out_ref) = refs[:-2], refs[-2:]
    n_col, n_out, out_rows, wide = sizes
    features = out_ref.shape[1] // n_col
    narrow = features // n_out

    def store(piece, first):
        for k in range(piece.shape[0]):
            in_ref[first + k] = piece[k, :, :wide]
            start = lax.rem(places_ref[1] + first + k, n_col) * features
            for i in range(n_out):
                place = pl.multiple_of(start + i * narrow, narrow)
                out_ref[:, pl.ds(place, narrow)] = piece[
                    k, i * out_rows : (i + 1) * out_rows, wide:
                ]

    for d in range(3):

        @pl.when(pl.program_id(0) == d)
        def _():
            store(pieces[d], 0)

    @pl.when(pl.program_id(0) == 3)
    def _():
        store(pieces[3], 0)
        store(pieces[4], pieces[3].shape[0])


def first_weights(dp, here, pieces, wide, n_out):
    n_col, in_rows, columns = pieces[0].shape
    out_rows = in_rows // n_out
    features = n_out * (columns - wide)
    whole = [
        pl.BlockSpec(piece.shape, lambda step, places: (0, 0, 0)) for piece in pieces
    ]
    return pl.pallas_call(
        functools.partial(first_weights_kernel, (n_col, n_out, out_rows, wide)),
        grid_spec=pltpu.PrefetchScalarGridSpec(
            num_scalar_prefetch=1,
            grid=(4,),
            in_specs=whole,
            out_specs=[
                pl.BlockSpec(
                    (n_col, in_rows, wide), lambda step, places: (0, places[0] ^ step, 0)
                ),
                pl.BlockSpec(
                    (out_rows, n_col * features), lambda step, places: (places[0] ^ step, 0)
                ),
            ],
        ),
        out_shape=[
            jax.ShapeDtypeStruct((n_col, 4 * in_rows, wide), BF),
            jax.ShapeDtypeStruct((4 * out_rows, n_col * features), BF),
        ],
        compiler_params=pltpu.CompilerParams(vmem_limit_bytes=32 << 20),
        cost_estimate=pl.CostEstimate(
            flops=0, bytes_accessed=8 * n_col * in_rows * columns * 2, transcendentals=0
        ),
        name="first_weights",
    )(jnp.stack([dp, here]).astype(jnp.int32), *pieces)


def pair_gradients_kernel(all_ref, gate_ref, up_ref):
    hidden = all_ref.shape[4]
    for k in range(all_ref.shape[1]):
        place = slice(k * hidden, (k + 1) * hidden)
        gate_ref[:, place] = all_ref[0, k, 0].astype(F32)
        up_ref[:, place] = all_ref[0, k, 1].astype(F32)


def pair_gradients(gathered):
    n_dp, n_col, pair, rows, hidden = gathered.shape
    cut = 2 if rows % 32 == 0 else 1
    side = pl.BlockSpec((rows // cut, n_col * hidden), lambda p, i: (p * cut + i, 0))
    return pl.pallas_call(
        pair_gradients_kernel,
        grid=(n_dp, cut),
        in_specs=[
            pl.BlockSpec((1, n_col, pair, rows // cut, hidden), lambda p, i: (p, 0, 0, i, 0))
        ],
        out_specs=[side, side],
        out_shape=[jax.ShapeDtypeStruct((n_dp * rows, n_col * hidden), F32)] * 2,
        compiler_params=pltpu.CompilerParams(vmem_limit_bytes=56 << 20),
        cost_estimate=pl.CostEstimate(
            flops=0, bytes_accessed=6 * math.prod(gathered.shape), transcendentals=0
        ),
        name="pair_gradients",
    )(gathered)


def down_gradients_kernel(all_ref, down_ref):
    down_ref[...] = all_ref[...].astype(F32)


def down_gradients(gathered):
    n_dp, n_col, rows, features = gathered.shape
    block = (1, 1, rows, features)
    whole = pl.pallas_call(
        down_gradients_kernel,
        grid=(n_dp, n_col),
        in_specs=[pl.BlockSpec(block, lambda p, z: (p, z, 0, 0))],
        out_specs=pl.BlockSpec(block, lambda p, z: (z, p, 0, 0)),
        out_shape=jax.ShapeDtypeStruct((n_col, n_dp, rows, features), F32),
        compiler_params=pltpu.CompilerParams(vmem_limit_bytes=56 << 20),
        cost_estimate=pl.CostEstimate(
            flops=0, bytes_accessed=6 * math.prod(gathered.shape), transcendentals=0
        ),
        name="down_gradients",
    )(gathered)
    return whole.reshape(-1, features)


def last_gradients_kernel(n_out, places_ref, *refs):
    pieces, outs = refs[:-4], refs[-4:]
    n_col = pieces[0].shape[0]
    features = outs[3].shape[3]
    head_cols = outs[0].shape[1] // n_col
    narrow = features // n_out

    def store(piece, first):
        rows = piece.shape[1] // n_out
        for k in range(piece.shape[0]):
            source = lax.rem(places_ref[1] + first + k, n_col)
            place = pl.ds(pl.multiple_of(source * head_cols, head_cols), head_cols)
            for i in range(3):
                outs[i][:, place] = piece[k, :, i * head_cols : (i + 1) * head_cols].astype(F32)
            for i in range(n_out):
                outs[3][source, 0, :, i * narrow : (i + 1) * narrow] = piece[
                    k, i * rows : (i + 1) * rows, 3 * head_cols :
                ].astype(F32)

    for d in range(3):

        @pl.when(pl.program_id(0) == d)
        def _():
            store(pieces[d], 0)

    @pl.when(pl.program_id(0) == 3)
    def _():
        store(pieces[3], 0)
        store(pieces[4], pieces[3].shape[0])


def last_gradients(dp, here, pieces, head_cols, n_out):
    n_col, rows, columns = pieces[0].shape
    features = n_out * (columns - 3 * head_cols)
    side = pl.BlockSpec(
        (rows, n_col * head_cols), lambda step, places: (places[0] ^ step, 0)
    )
    side_shape = jax.ShapeDtypeStruct((4 * rows, n_col * head_cols), F32)
    *sides, out = pl.pallas_call(
        functools.partial(last_gradients_kernel, n_out),
        grid_spec=pltpu.PrefetchScalarGridSpec(
            num_scalar_prefetch=1,
            grid=(4,),
            in_specs=[
                pl.BlockSpec(piece.shape, lambda step, places: (0, 0, 0)) for piece in pieces
            ],
            out_specs=[side] * 3
            + [
                pl.BlockSpec(
                    (n_col, 1, rows // n_out, features),
                    lambda step, places: (0, places[0] ^ step, 0, 0),
                )
            ],
        ),
        out_shape=[side_shape] * 3
        + [jax.ShapeDtypeStruct((n_col, 4, rows // n_out, features), F32)],
        compiler_params=pltpu.CompilerParams(vmem_limit_bytes=56 << 20),
        cost_estimate=pl.CostEstimate(
            flops=0, bytes_accessed=24 * n_col * rows * columns, transcendentals=0
        ),
        name="last_gradients",
    )(jnp.stack([dp, here]).astype(jnp.int32), *pieces)
    return sides, out.reshape(-1, features)


def own_block_kernel(here_ref, *refs):
    blocks, whole = refs[:-1], refs[-1]
    for step, block in enumerate(blocks):

        @pl.when(pl.program_id(0) == step)
        def _():
            whole[...] = block[...]


def own_rows(ring, blocks):
    size = len(blocks)
    rows, columns = blocks[0].shape[0] // size, blocks[0].shape[1]
    return pl.pallas_call(
        own_block_kernel,
        grid_spec=pltpu.PrefetchScalarGridSpec(
            num_scalar_prefetch=1,
            grid=(size,),
            in_specs=[pl.BlockSpec((rows, columns), lambda step, here: (here[0], 0))] * size,
            out_specs=pl.BlockSpec(
                (rows, columns), lambda step, here: (0, lax.rem(here[0] + step, size))
            ),
        ),
        out_shape=jax.ShapeDtypeStruct((rows, columns * size), blocks[0].dtype),
        compiler_params=pltpu.CompilerParams(vmem_limit_bytes=32 << 20),
        name="own_rows",
    )(ring.here.astype(jnp.int32)[None], *blocks)


def from_here(ring, values, size, axis):
    twice = jnp.concatenate([values, values], axis=axis)
    return lax.dynamic_slice_in_dim(twice, ring.here * size, size * ring.size, axis)


def to_order(ring, values, size, axis):
    twice = jnp.concatenate([values, values], axis=axis)
    start = lax.rem(ring.size - ring.here, ring.size) * size
    return lax.dynamic_slice_in_dim(twice, start, size * ring.size, axis)


def exchange(ring, block_for):
    return [ring.fetch(block_for(ring.at(-step)), step) for step in range(ring.size)]


def gather_tokens(row, col, values, early=(), late=()):
    near, early, late = gather_near(col, values, early, late)
    blocks = [
        jnp.concatenate([row.fetch(block, j) for j in range(row.size)], axis=0)
        for block in near
    ]
    return blocks, early, late


def sum_rows(row, partial):
    size = partial.shape[0] // row.size
    total = partial[:size]
    for j in range(1, row.size):
        total = total + row.give(partial[j * size : (j + 1) * size].astype(BF), j).astype(F32)
    return total


def sum_all(row, col, values, block_for):
    length = values.shape[1]
    size = length // row.size
    total = values
    for j in range(1, row.size):
        total = total + jnp.roll(row.fetch(values, j), j * size, axis=1)
    came = [
        col.fetch(jnp.concatenate([total, block_for(col.at(-k))], axis=1), k)
        for k in range(col.size)
    ]
    result = came[0]
    for part in came[1:]:
        result = result + part
    return result[:, :length], [part[:, length:] for part in came]


def rms_scale(values):
    return lax.rsqrt(jnp.mean(values * values, axis=1, keepdims=True) + EPSILON)


def rms_back(grad_normed, branch, scales, gains):
    weighted = grad_normed * gains
    inner = jnp.mean(weighted * branch, axis=1, keepdims=True)
    grad_branch = scales * weighted - branch * (scales * scales * scales) * inner
    grad_gains = jnp.sum(grad_normed * branch * scales, axis=0)
    return grad_branch, grad_gains


def turn(values, cosine, sine):
    return values * cosine + pltpu.roll(values, values.shape[-1] // 2, 1) * sine


def kernel_dot(a, b, dims):
    return lax.dot_general(a, b, (dims, ((), ())), preferred_element_type=F32)


def softmax_parts(queries, keys, doc_rows, slot_rows, lines):
    scores = kernel_dot(queries, keys, ((1,), (1,))) * (HEAD**-0.5)
    allowed = (doc_rows == lines[2:3, :]) & (lines[3:4, :] <= slot_rows)
    scores = jnp.where(allowed, scores, MASKED)
    weights = jnp.exp(scores - jnp.max(scores, axis=1, keepdims=True))
    return weights * (1.0 / jnp.sum(weights, axis=1, keepdims=True))


def place_of(block, here, n_col):
    row, index = block // n_col, block % n_col
    step = lax.rem(index + n_col - here, n_col)
    if n_col == 4:
        step = jnp.where((here == 3) & (step % 2 == 1), 4 - step, step)
    return step, row


def forward_kernel(
    sizes,
    here_ref,
    query_ref,
    key_ref,
    value_ref,
    lines_ref,
    query_gain_ref,
    key_gain_ref,
    cosine_ref,
    sine_ref,
    query_rot_ref,
    key_rot_ref,
    value_low_ref,
    mixture_ref,
):
    n_row, n_col, small, large = sizes
    cosine, sine, lines = cosine_ref[...], sine_ref[...], lines_ref[...]
    columns = jnp.transpose(lines)
    normed = query_ref[...] * columns[:, 0:1] * query_gain_ref[...]
    query_rot_ref[...] = turn(normed, cosine, sine).astype(BF)
    normed = key_ref[...] * columns[:, 1:2] * key_gain_ref[...]
    key_rot_ref[...] = turn(normed, cosine, sine).astype(BF)
    value_low_ref[...] = value_ref[...].astype(BF)
    keys, values = key_rot_ref[...], value_low_ref[...]
    for start in range(0, query_ref.shape[0], large):
        rows = slice(start, start + large)
        chances = softmax_parts(
            query_rot_ref[rows, :], keys, columns[rows, 2:3], columns[rows, 3:4], lines
        )
        mixture = kernel_dot(chances.astype(BF), values, ((1,), (0,))).astype(BF)
        for inner in range(0, large, small):
            step, row = place_of((start + inner) // small, here_ref[0], n_col)
            place = pl.multiple_of((step * n_row + row) * small, small)
            mixture_ref[pl.ds(place, small), :] = mixture[inner : inner + small]


def backward_kernel(
    sizes,
    here_ref,
    query_ref,
    key_ref,
    lines_ref,
    query_gain_ref,
    key_gain_ref,
    cosine_ref,
    sine_ref,
    query_rot_ref,
    key_rot_ref,
    value_low_ref,
    grad_ref,
    query_weighted_ref,
    key_weighted_ref,
    grad_value_ref,
    inner_ref,
    query_gain_grad_ref,
    key_gain_grad_ref,
    key_total,
    value_total,
):
    n_row, n_col, small, large = sizes
    cosine, sine, lines = cosine_ref[...], sine_ref[...], lines_ref[...]
    columns = jnp.transpose(lines)
    keys, values = key_rot_ref[...], value_low_ref[...]
    factor = HEAD**-0.5
    for start in range(0, query_ref.shape[0], large):
        rows = slice(start, start + large)
        queries = query_rot_ref[rows, :]
        grads = []
        for inner in range(0, large, small):
            step, row = place_of((start + inner) // small, here_ref[0], n_col)
            place = pl.multiple_of((step * n_row + row) * small, small)
            grads.append(grad_ref[pl.ds(place, small), :])
        grads = jnp.concatenate(grads, axis=0)
        chances = softmax_parts(
            queries, keys, columns[rows, 2:3], columns[rows, 3:4], lines
        )
        value_part = kernel_dot(chances.astype(BF), grads, ((0,), (0,)))
        grad_chances = kernel_dot(grads, values, ((1,), (1,)))
        inner = jnp.sum(chances * grad_chances, axis=1, keepdims=True)
        grad_scores = (chances * (grad_chances - inner)).astype(BF)
        query_weighted_ref[rows, :] = kernel_dot(grad_scores, keys, ((1,), (0,))) * factor
        key_part = kernel_dot(grad_scores, queries, ((0,), (0,))) * factor
        if start == 0:
            value_total[...] = value_part
            key_total[...] = key_part
        else:
            value_total[...] += value_part
            key_total[...] += key_part
    grad_value_ref[...] = value_total[...].astype(BF)
    ones = jnp.ones((8, HEAD), F32)
    inners = []
    for grad, raw_ref, which, gain_ref, weighted_ref, gain_grad_ref in (
        (
            query_weighted_ref[...],
            query_ref,
            0,
            query_gain_ref,
            query_weighted_ref,
            query_gain_grad_ref,
        ),
        (
            key_total[...],
            key_ref,
            1,
            key_gain_ref,
            key_weighted_ref,
            key_gain_grad_ref,
        ),
    ):
        unturned = turn(grad, cosine, -sine)
        raw = raw_ref[...]
        gain_grad_ref[0] = jnp.sum(
            unturned * raw * columns[:, which : which + 1], axis=0, keepdims=True
        )
        weighted = unturned * gain_ref[...]
        weighted_ref[...] = weighted
        inners.append(
            lax.dot_general(
                ones,
                weighted * raw,
                (((1,), (1,)), ((), ())),
                precision=lax.Precision.HIGHEST,
                preferred_element_type=F32,
            )
        )
    which = lax.broadcasted_iota(jnp.int32, inner_ref.shape, 0)
    both = jnp.where(which == 0, inners[0], inners[1])

    @pl.when(pl.program_id(0) == 0)
    def _():
        inner_ref[...] = both

    @pl.when(pl.program_id(0) > 0)
    def _():
        inner_ref[...] += both


def head_specs(length):
    return {
        "head": lambda first: pl.BlockSpec(
            (length, HEAD), lambda h, here, first=first: (0, first + h)
        ),
        "gain": pl.BlockSpec((1, HEAD), lambda h, here: (0, h)),
        "lines": pl.BlockSpec((8, length), lambda h, here: (0, 0)),
        "table": pl.BlockSpec((length, HEAD), lambda h, here: (0, 0)),
        "head_line": pl.BlockSpec((1, 1, HEAD), lambda h, here: (h, 0, 0)),
    }


def attend_forward(row, col, raw, lines, gains, tables):
    length = raw.shape[0]
    heads = raw.shape[1] // (3 * HEAD)
    spec = head_specs(length)
    small = length // (row.size * col.size)
    wide = jax.ShapeDtypeStruct((length, heads * HEAD), BF)
    return pl.pallas_call(
        functools.partial(
            forward_kernel, (row.size, col.size, small, max(small, min(256, length)))
        ),
        grid_spec=pltpu.PrefetchScalarGridSpec(
            num_scalar_prefetch=1,
            grid=(heads,),
            in_specs=[spec["head"](0), spec["head"](heads), spec["head"](2 * heads)]
            + [spec["lines"]]
            + [spec["gain"]] * 2
            + [spec["table"]] * 2,
            out_specs=[spec["head"](0)] * 4,
        ),
        out_shape=[wide] * 4,
        compiler_params=pltpu.CompilerParams(vmem_limit_bytes=56 << 20),
        cost_estimate=pl.CostEstimate(
            flops=heads * 4 * length * length * HEAD,
            bytes_accessed=heads * length * HEAD * 20,
            transcendentals=heads * length * length,
        ),
        name="attend_forward",
    )(col.here.astype(jnp.int32)[None], raw, raw, raw, lines, *gains, *tables)


def attend_backward(row, col, raw, lines, gains, tables, saved, grad):
    length = raw.shape[0]
    heads = raw.shape[1] // (3 * HEAD)
    spec = head_specs(length)
    small = length // (row.size * col.size)
    wide = jax.ShapeDtypeStruct((length, heads * HEAD), F32)
    low = jax.ShapeDtypeStruct((length, heads * HEAD), BF)
    flat = jax.ShapeDtypeStruct((heads, 1, HEAD), F32)
    return pl.pallas_call(
        functools.partial(
            backward_kernel, (row.size, col.size, small, max(small, min(256, length)))
        ),
        grid_spec=pltpu.PrefetchScalarGridSpec(
            num_scalar_prefetch=1,
            grid=(heads,),
            in_specs=[spec["head"](0), spec["head"](heads), spec["lines"]]
            + [spec["gain"]] * 2
            + [spec["table"]] * 2
            + [spec["head"](0)] * 4,
            out_specs=[spec["head"](0)] * 3 + [spec["lines"]] + [spec["head_line"]] * 2,
            scratch_shapes=[pltpu.VMEM((length, HEAD), F32)] * 2,
        ),
        out_shape=[wide, wide, low, jax.ShapeDtypeStruct((8, length), F32), flat, flat],
        compiler_params=pltpu.CompilerParams(vmem_limit_bytes=56 << 20),
        cost_estimate=pl.CostEstimate(
            flops=heads * 10 * length * length * HEAD,
            bytes_accessed=heads * length * HEAD * 30,
            transcendentals=heads * length * length,
        ),
        name="attend_backward",
    )(col.here.astype(jnp.int32)[None], raw, raw, lines, *gains, *tables, *saved, grad)


def device_program(sizes):
    n_dp, n_row, n_col = sizes["dp"], sizes["row"], sizes["col"]

    def per_device(
        layer_input,
        doc_ids,
        positions,
        w_query,
        w_key,
        w_value,
        w_out,
        w_gate,
        w_up,
        w_down,
        gain_query,
        gain_key,
        gain_attn,
        gain_ffn,
        grad_output,
    ):
        row, col = Ring("row", n_row), Ring("col", n_col)
        dp = lax.axis_index("dp")
        length = doc_ids.shape[0]
        row_tokens = layer_input.shape[0]
        own_tokens = row_tokens // n_col
        features = layer_input.shape[1]
        width = features * n_col
        head_cols = w_query.shape[1] // n_col
        hidden_cols = w_gate.shape[1] // n_col
        in_rows = features // n_dp
        out_rows = head_cols // n_dp
        down_rows = hidden_cols // n_dp

        def gather_dp(values):
            return lax.all_gather(values, "dp", axis=0, tiled=True)

        steps = [1 << bit for bit in range(n_dp.bit_length() - 1)]

        def partner(values, step):
            return lax.ppermute(values, "dp", [(i, i ^ step) for i in range(n_dp)])

        class GroupSum:
            def __init__(self, block_for):
                blocks = [block_for(dp ^ d) for d in range(n_dp)]
                self.halves = [
                    (dict(enumerate(left for left, _ in blocks)), list(steps)),
                    (dict(enumerate(right for _, right in blocks)), list(steps[::-1])),
                ]
                self.came = None
                self.send()

            def send(self):
                self.came = []
                for blocks, order in self.halves:
                    given = [blocks[d] for d in sorted(blocks) if d & order[0]]
                    self.came.append(partner(jnp.stack(given), order[0]))

            def land(self, chain, more=True):
                self.came, chain = lax.optimization_barrier((self.came, chain))
                for (blocks, order), came in zip(self.halves, self.came):
                    step = order.pop(0)
                    for place, d in enumerate([d for d in sorted(blocks) if d & step]):
                        kept = blocks[d ^ step].astype(F32) + came[place].astype(F32)
                        blocks[d ^ step] = kept.astype(BF)
                        del blocks[d]
                if self.halves[0][1]:
                    self.send()
                return chain

            def finish(self, chain):
                while self.halves[0][1]:
                    chain = self.land(chain)
                return [blocks[0] for blocks, _ in self.halves], chain

        def gather_four(values, beside=()):
            half = values.shape[0] // 2
            one, two = partner(values, 1), partner(values, 2)
            (one, two), beside = lax.optimization_barrier(((one, two), beside))
            far = [partner(one[:half], 2), partner(two[half:], 1)]
            return [[values], [one], [two], far], beside

        def halves_of(values):
            half = values.shape[-1] // 2
            return values[..., :half], values[..., half:]

        def qkv_block(index):
            return jnp.concatenate(
                [
                    lax.dynamic_slice(
                        w, (dp * in_rows, index * head_cols), (in_rows, head_cols)
                    )
                    for w in (w_query, w_key, w_value)
                ],
                axis=1,
            )

        def gate_up_block(index):
            return jnp.stack(
                [
                    lax.dynamic_slice(
                        w, (dp * in_rows, index * hidden_cols), (in_rows, hidden_cols)
                    )
                    for w in (w_gate, w_up)
                ]
            )

        def out_block(index):
            return lax.dynamic_slice_in_dim(
                w_out, index * head_cols + dp * out_rows, out_rows, 0
            )

        def down_block(index):
            return lax.dynamic_slice_in_dim(
                w_down, index * hidden_cols + dp * down_rows, down_rows, 0
            )

        def first_block(index):
            out = out_block(index).reshape(out_rows, n_out, -1).swapaxes(0, 1)
            return jnp.concatenate([qkv_block(index), out.reshape(in_rows, -1)], axis=1)

        n_out = in_rows // out_rows
        first_parts = exchange(col, first_block)

        turned_docs = from_here(row, doc_ids, row_tokens, 0)
        turned_positions = from_here(row, positions, row_tokens, 0)
        slots = lax.rem(jnp.arange(length) + row.here * row_tokens, length)
        tables = rope_tables(turned_positions)
        first_parts, layer_input = lax.optimization_barrier((first_parts, layer_input))
        near, _, tables = gather_col(col, layer_input, (), tables)
        if n_dp == 4:
            pieces, _ = gather_four(jnp.stack(first_parts))
            pieces = sum(pieces, [])
            w_qkv, w_out_all = first_weights(dp, col.here, pieces, 3 * head_cols, n_out)
        else:
            first = gather_dp(jnp.stack(first_parts)[None])
            w_qkv = first[..., : 3 * head_cols].swapaxes(0, 1).reshape(n_col, features, -1)
            w_out_all = first[..., 3 * head_cols :].reshape(n_dp, n_col, n_out, out_rows, -1)
            w_out_all = w_out_all.transpose(0, 3, 1, 2, 4).reshape(head_cols, width)
            w_out_all = to_order(col, w_out_all, features, 1)
        w_down = after(w_down, near)
        down_parts = exchange(col, down_block)
        w_qkv = [w_qkv[k] for k in range(n_col)]
        input_rows = [
            jnp.concatenate([row.fetch(block, j) for j in range(n_row)], axis=0)
            for block in near
        ]
        own_input = own_rows(col, near).astype(F32)

        raw = sum(dot(rows, w) for rows, w in zip(input_rows, w_qkv))
        query_raw = raw[:, :head_cols]
        key_raw = raw[:, head_cols : 2 * head_cols]
        squares = jnp.stack(
            [jnp.sum(query_raw * query_raw, axis=1), jnp.sum(key_raw * key_raw, axis=1)]
        )
        squares, down_parts = lax.optimization_barrier((squares, down_parts))
        down_parts = assemble(col, down_parts, 1)
        w_gate, w_up = after((w_gate, w_up), down_parts)
        gate_up_parts = exchange(col, gate_up_block)
        gains = jnp.stack([gain_attn, gain_ffn])
        squares, gains = sum_all(row, col, squares, lambda index: gains)
        squares, w_out_all, gate_up_parts[1::2] = lax.optimization_barrier(
            (squares, w_out_all, gate_up_parts[1::2])
        )
        w_down_all = gather_dp(down_parts)
        gains = assemble(col, gains, 1)
        gain_attn_all, gain_ffn_all = gains[0:1], gains[1:2]

        scales = lax.rsqrt(squares / width + EPSILON)
        query_scale, key_scale = scales[0][:, None], scales[1][:, None]
        head_gains = (gain_query[None, :], gain_key[None, :])
        marks = jnp.stack([turned_docs, slots]).astype(F32)
        lines = jnp.concatenate([scales, marks, jnp.zeros((4, length), F32)], axis=0)
        *saved, mixture = attend_forward(row, col, raw, lines, head_gains, tables)
        attended = []
        for k in range(n_col):
            total, *others = (
                dot(block_at(mixture, k * n_row + j, own_tokens, 0), w_out_all)
                for j in range(n_row)
            )
            for j, other in enumerate(others):
                total = total + row.give(other.astype(BF), j + 1).astype(F32)
            attended.append(total)
        gate_up_parts, attended = lax.optimization_barrier((gate_up_parts, attended))
        gate_up_parts = assemble(
            col, [part[:, None] for part in after(gate_up_parts, w_down_all)], 1
        )
        gate_up_parts, attended = lax.optimization_barrier((gate_up_parts, attended))
        attended, _, _ = reduce_near(col, attended)
        w_gate_up = lax.all_gather(gate_up_parts[:, :, None], "dp", axis=2, tiled=True)
        w_gate_up = w_gate_up.reshape(2, width, hidden_cols)
        attn_scale = rms_scale(attended)
        hidden_state = own_input + attended * attn_scale * gain_attn_all

        state_rows, _, w_gate_up = gather_tokens(
            row, col, hidden_state.astype(BF), (), w_gate_up
        )
        w_gate, w_up = w_gate_up[0], w_gate_up[1]
        grad_output = after(grad_output, state_rows)
        cotangent = exchange(
            col, lambda index: block_at(grad_output, index, own_tokens, 0)
        )
        kept, activated = [], []
        for block in state_rows:
            pair = lax.optimization_barrier((dot(block, w_gate), dot(block, w_up)))
            gate_values, up_values = pair
            kept.append(pair)
            activated.append((gate_values * jax.nn.sigmoid(gate_values) * up_values).astype(BF))
        lowered = [sum_rows(row, dot(block, w_down_all)) for block in activated]
        lowered, cotangent = lax.optimization_barrier((lowered, cotangent))
        cotangent = assemble(col, cotangent, 1).astype(F32)
        lowered, _, _ = reduce_near(col, lowered)
        ffn_scale = rms_scale(lowered)
        own_output = (hidden_state + lowered * ffn_scale * gain_ffn_all).astype(BF)

        grad_lowered, grad_gain_ffn = rms_back(cotangent, lowered, ffn_scale, gain_ffn_all)
        lowered_rows, _, _ = gather_tokens(row, col, grad_lowered.astype(BF))
        gate_grads, up_grads, state_part = [], [], []
        for block, (gate_values, up_values) in zip(lowered_rows, kept):
            sigmoid_gate = jax.nn.sigmoid(gate_values)
            grad_activated = dot_nt(block, w_down_all)
            grad_gate = (
                grad_activated
                * up_values
                * (sigmoid_gate * (1.0 + gate_values * (1.0 - sigmoid_gate)))
            )
            grad_up = grad_activated * (gate_values * sigmoid_gate)
            pair = lax.optimization_barrier((grad_gate.astype(BF), grad_up.astype(BF)))
            gate_grads.append(pair[0])
            up_grads.append(pair[1])
            state_part.append(sum_rows(row, dot_nt(pair[0], w_gate) + dot_nt(pair[1], w_up)))
        wide = (
            jnp.concatenate(activated),
            jnp.concatenate(lowered_rows),
            jnp.concatenate(state_rows),
            jnp.concatenate(gate_grads),
            jnp.concatenate(up_grads),
        )
        activated, lowered_rows, state_rows, gate_grads, up_grads = after(wide, state_part)
        grad_w_down = dot_tn(activated, lowered_rows).astype(BF)
        down_sum = GroupSum(
            lambda index: halves_of(block_at(grad_w_down, index, down_rows, 0))
        )
        gate_up_grads = [
            dot_tn(after(state_rows, grad_w_down), grads)
            .astype(BF)
            .reshape(n_col, n_dp, in_rows, hidden_cols)
            for grads in (gate_grads, up_grads)
        ]
        state_part, _, gate_up_grads = reduce_near(
            col, state_part, grad_w_down, gate_up_grads
        )
        gate_up_sum = GroupSum(
            lambda index: [
                lax.dynamic_index_in_dim(grads, index, 1, False) for grads in gate_up_grads
            ]
        )
        state_part = down_sum.land(state_part)
        grad_state = cotangent + state_part
        grad_attended, grad_gain_attn = rms_back(
            grad_state, attended, attn_scale, gain_attn_all
        )
        attended_rows, gate_up_sum.came, _ = gather_tokens(
            row, col, grad_attended.astype(BF), gate_up_sum.came
        )
        gate_up_sum.land(())
        down_parts, attended_rows = down_sum.finish(attended_rows)
        down_parts = jnp.concatenate(down_parts, axis=1)
        down_parts = exchange(
            col, lambda index, whole=down_parts: block_at(whole, index, features, 1)
        )

        grad_mixture = [dot_nt(block, w_out_all).astype(BF) for block in attended_rows]
        attended_rows = jnp.concatenate(attended_rows)
        grad_mixture = jnp.concatenate(grad_mixture)
        (
            query_weighted,
            key_weighted,
            grad_value,
            inner,
            grad_gain_query,
            grad_gain_key,
        ) = attend_backward(row, col, raw, lines, head_gains, tables, saved, grad_mixture)
        gate_up_sum.came, down_parts, inner = lax.optimization_barrier(
            (gate_up_sum.came, down_parts, inner)
        )
        gate_up_sum, _ = gate_up_sum.finish(())
        down_back = assemble(col, [part[None] for part in down_parts], 0)
        down_all = gather_dp(down_back[None])
        small = jnp.stack([grad_gain_attn, grad_gain_ffn])
        inner, small = sum_all(row, col, inner[:2], lambda index: block_at(small, index, features, 1))
        inner = inner / width
        gate_up_whole = after(jnp.stack(gate_up_sum), inner)
        gate_up_parts = exchange(
            col, lambda index: lax.dynamic_index_in_dim(gate_up_whole, index, 1, False)
        )
        small = sum(small[1:], small[0])
        head_gain_grads = [grad_gain_query.reshape(-1), grad_gain_key.reshape(-1)]
        small = sum((row.fetch(small, j) for j in range(1, n_row)), small)
        small = jnp.concatenate([small, jnp.stack(head_gain_grads)], axis=1)
        for step in steps:
            small = small + partner(small, step)
        grad_query = (
            query_scale * query_weighted
            - query_raw * (query_scale * query_scale * query_scale) * inner[0][:, None]
        )
        grad_key = (
            key_scale * key_weighted
            - key_raw * (key_scale * key_scale * key_scale) * inner[1][:, None]
        )
        grad_qkv = jnp.concatenate(
            [grad_query.astype(BF), grad_key.astype(BF), grad_value], axis=1
        )
        grad_w_qkv = jnp.stack([dot_tn(rows, grad_qkv).astype(BF) for rows in input_rows])
        qkv_grads = grad_w_qkv.reshape(n_col, n_dp, in_rows, 3 * head_cols)
        out_grads = dot_tn(mixture, after(attended_rows, inner)).astype(BF)
        out_grads = out_grads.reshape(n_dp, out_rows, n_col, n_out, -1)
        out_grads = out_grads.transpose(2, 0, 3, 1, 4).reshape(n_col, n_dp, in_rows, -1)
        out_grads = from_here(col, out_grads, 1, 0)

        def last_block(index):
            return halves_of(
                jnp.concatenate(
                    [
                        lax.dynamic_index_in_dim(grads, index, 1, False)
                        for grads in (qkv_grads, out_grads)
                    ],
                    axis=-1,
                )
            )

        qkv_grads, out_grads, small, grad_qkv = lax.optimization_barrier(
            (qkv_grads, out_grads, small, grad_qkv)
        )
        last_sum = GroupSum(last_block)
        input_part = [dot_nt(grad_qkv, w) for w in w_qkv]
        gate_up_parts, last_sum.came, input_part = lax.optimization_barrier(
            (gate_up_parts, last_sum.came, input_part)
        )
        last_sum.land(())
        gate_up_back = assemble(
            col, [part[None] for part in after(gate_up_parts, down_back)], 0
        )
        gate_up_all = gather_dp(gate_up_back[None])
        input_part = [sum_rows(row, partial) for partial in input_part]
        gate_up_back, input_part = lax.optimization_barrier((gate_up_back, input_part))
        last_sum, _ = last_sum.finish(())
        last_sum = jnp.concatenate(last_sum, axis=-1)
        last_parts = [col.fetch(last_sum[-k % n_col], k) for k in range(n_col)]
        grad_w_down = down_gradients(down_all)
        grad_input, (last_parts, grad_w_down), _ = reduce_near(
            col, by_arrival(col, input_part), (last_parts, grad_w_down)
        )
        own_output, grad_state = after((own_output, grad_state), last_parts)
        own_state = grad_state.astype(BF)
        output_parts = exchange(col, lambda index: block_at(own_output, index, features, 1))
        state_parts = exchange(col, lambda index: block_at(own_state, index, features, 1))
        grad_w_wide = (
            *pair_gradients(gate_up_all),
            grad_w_down,
        )
        if n_dp == 4:
            pieces, (output_parts, state_parts) = gather_four(
                jnp.stack(last_parts), (output_parts, state_parts)
            )
            pieces, grad_w_wide = lax.optimization_barrier((pieces, grad_w_wide))
            (grad_w_query, grad_w_key, grad_w_value), grad_w_out = last_gradients(
                dp, col.here, sum(pieces, []), head_cols, n_out
            )
        else:
            last_parts = assemble(col, [part[None] for part in last_parts], 0)
            last_all = gather_dp(after(last_parts, gate_up_all)[None])

            def columns_of(whole):
                return jnp.concatenate(
                    [whole[:, k].reshape(features, -1) for k in range(n_col)], axis=1
                ).astype(F32)

            grad_w_query, grad_w_key, grad_w_value = (
                columns_of(last_all[..., i * head_cols : (i + 1) * head_cols])
                for i in range(3)
            )
            out_all = last_all[..., 3 * head_cols :].reshape(
                n_dp, n_col, n_out, out_rows, -1
            )
            grad_w_out = out_all.transpose(1, 0, 3, 2, 4).reshape(w_out.shape).astype(F32)
        grad_w_gate, grad_w_up, grad_w_down = grad_w_wide
        layer_output = assemble(col, output_parts, 0)
        grad_input = grad_input + assemble(col, state_parts, 0).astype(F32)
        return (
            layer_output,
            grad_input,
            grad_w_query,
            grad_w_key,
            grad_w_value,
            grad_w_out,
            grad_w_gate,
            grad_w_up,
            grad_w_down,
            small[0, features:],
            small[1, features:],
            small[0, :features],
            small[1, :features],
        )

    return per_device


def solution(mesh):
    in_specs = (
        P(("dp", "row"), "col"),
        P("dp"),
        P("dp"),
        P("col", "row"),
        P("col", "row"),
        P("col", "row"),
        P("row", "col"),
        P("col", "row"),
        P("col", "row"),
        P("row", "col"),
        P(("row", "col")),
        P(("row", "col")),
        P("col"),
        P("col"),
        P(("dp", "row"), "col"),
    )
    out_specs = (
        P(("dp", "row"), "col"),
        P(("dp", "row"), "col"),
        P("col", "row"),
        P("col", "row"),
        P("col", "row"),
        P("row", "col"),
        P("col", "row"),
        P("col", "row"),
        P("row", "col"),
        P(("row", "col")),
        P(("row", "col")),
        P("col"),
        P("col"),
    )
    return jax.shard_map(
        device_program(dict(mesh.shape)),
        mesh=mesh,
        in_specs=in_specs,
        out_specs=out_specs,
        check_vma=False,
    )
```

```python
import functools
import math

import jax
import jax.numpy as jnp
from jax import lax
from jax.experimental import pallas as pl
from jax.experimental.pallas import tpu as pltpu
from jax.sharding import PartitionSpec as P

HEAD = 128
EPSILON = 1e-06
ROPE_BASE = 500000.0
MASKED = -1e30
BF = jnp.bfloat16
F32 = jnp.float32


def rope_tables(positions):
    digit = 32
    frequency = ROPE_BASE ** (-(jnp.arange(HEAD // 2, dtype=F32) * (2.0 / HEAD)))
    frequency = jnp.concatenate([frequency, frequency])

    def looked_up(index, count, unit):
        angles = (jnp.arange(count) * unit).astype(F32)[:, None] * frequency[None, :]
        table = jnp.concatenate([jnp.cos(angles), jnp.sin(angles)], axis=1)
        chosen = (index[:, None] == jnp.arange(count)[None, :]).astype(F32)
        both = jnp.dot(chosen, table, precision=lax.Precision.HIGHEST)
        return both[:, :HEAD], both[:, HEAD:]

    high_cosine, high_sine = looked_up(
        positions // digit, -(-positions.shape[0] // digit), digit
    )
    low_cosine, low_sine = looked_up(positions % digit, digit, 1)
    signs = jnp.where(jnp.arange(HEAD) < HEAD // 2, -1.0, 1.0).astype(F32)[None, :]
    return (
        high_cosine * low_cosine - high_sine * low_sine,
        (high_sine * low_cosine + high_cosine * low_sine) * signs,
    )


def dot(a, b):
    return jnp.dot(a, b, preferred_element_type=F32)


def dot_nt(a, b):
    return lax.dot_general(a, b, (((1,), (1,)), ((), ())), preferred_element_type=F32)


def dot_tn(a, b):
    return lax.dot_general(a, b, (((0,), (0,)), ((), ())), preferred_element_type=F32)


class Ring:
    def __init__(self, name, size):
        self.name, self.size = name, size
        self.here = lax.axis_index(name)

    def fetch(self, values, step):
        if step % self.size == 0:
            return values
        pairs = [(i, (i - step) % self.size) for i in range(self.size)]
        return lax.ppermute(values, self.name, pairs)

    def send(self, values, pairs):
        return lax.ppermute(values, self.name, pairs)

    def give(self, values, step):
        return self.fetch(values, -step)

    def at(self, step):
        return lax.rem(self.here + (step % self.size), self.size)


def after(values, *earlier):
    return lax.optimization_barrier((values, earlier))[0]


def gather_steps(col, values, early=(), beside=()):
    two = col.send(values, [(0, 2), (1, 3), (2, 0), (3, 1)])
    below = col.send(values, [(0, 1), (1, 2), (2, 3)])
    above = col.send(values, [(1, 0), (2, 1), (3, 2)])
    two, early = lax.optimization_barrier((two, early))
    two, below, above, beside = lax.optimization_barrier((two, below, above, beside))
    relayed = col.send(two, [(2, 3), (1, 0)])
    return two, below, above, relayed, early, beside


def gather_col(col, values, early, beside):
    if col.size != 4:
        return [col.fetch(values, k) for k in range(col.size)], early, beside
    two, below, above, relayed, early, beside = gather_steps(col, values, early, beside)
    near = [
        values,
        jnp.where(col.here == 3, relayed, above),
        two,
        jnp.where(col.here == 0, relayed, below),
    ]
    return near, early, beside


def by_arrival(col, blocks):
    if col.size != 4:
        return blocks
    last = col.here == 3
    return [
        blocks[0],
        jnp.where(last, blocks[3], blocks[1]),
        blocks[2],
        jnp.where(last, blocks[1], blocks[3]),
    ]


def gather_near(col, values, early=(), late=()):
    if col.size != 4:
        return [col.fetch(values, k) for k in range(col.size)], early, late
    two, below, above, relayed, early, late = gather_steps(col, values, early, late)
    inside = (col.here == 1) | (col.here == 2)
    near = [
        values,
        jnp.where(col.here == 3, below, above),
        two,
        jnp.where(inside, below, relayed),
    ]
    return near, early, late


def reduce_near(col, blocks, between=(), beside=()):
    low = [block.astype(BF) for block in blocks]
    result = blocks[0]
    if col.size != 4:
        for k in range(1, col.size):
            result = result + col.give(low[k], k).astype(F32)
        return result, between, beside
    relayed = col.send(low[3], [(3, 2), (0, 1)])
    below = col.send(low[1], [(0, 1), (1, 2), (2, 3)])
    above = col.send(
        jnp.where(col.here == 3, low[1], low[3]), [(1, 0), (2, 1), (3, 2)]
    )
    two = (blocks[2] + relayed.astype(F32)).astype(BF)
    two, between = lax.optimization_barrier((two, between))
    two = col.send(two, [(0, 2), (1, 3), (2, 0), (3, 1)])
    above, below, beside = lax.optimization_barrier((above, below, beside))
    result = result + above.astype(F32) + below.astype(F32) + two.astype(F32)
    return result, between, beside


def block_at(values, index, size, axis):
    return lax.dynamic_slice_in_dim(values, index * size, size, axis)


def assemble_kernel(here_ref, *refs):
    blocks, whole = refs[:-1], refs[-1]
    for step, block in enumerate(blocks):

        @pl.when(pl.program_id(0) == step)
        def _():
            whole[...] = block[...]


def assemble(ring, blocks, axis):
    shape = list(blocks[0].shape)
    size = len(blocks)
    zeros = (0,) * len(shape)

    def place(step, here):
        return zeros[:axis] + (lax.rem(here[0] + step, size),) + zeros[axis + 1 :]

    block_shape = tuple(shape)
    shape[axis] *= size
    return pl.pallas_call(
        assemble_kernel,
        grid_spec=pltpu.PrefetchScalarGridSpec(
            num_scalar_prefetch=1,
            grid=(size,),
            in_specs=[pl.BlockSpec(block_shape, lambda step, here: zeros)] * size,
            out_specs=pl.BlockSpec(block_shape, place),
        ),
        out_shape=jax.ShapeDtypeStruct(tuple(shape), blocks[0].dtype),
        compiler_params=pltpu.CompilerParams(vmem_limit_bytes=32 << 20),
        cost_estimate=pl.CostEstimate(
            flops=0,
            bytes_accessed=2 * math.prod(shape) * blocks[0].dtype.itemsize,
            transcendentals=0,
        ),
        name="assemble",
    )(ring.here.astype(jnp.int32)[None], *blocks)


def first_weights_kernel(sizes, places_ref, *refs):
    pieces, (in_ref, out_ref) = refs[:-2], refs[-2:]
    n_col, n_out, out_rows, wide = sizes
    features = out_ref.shape[1] // n_col
    narrow = features // n_out

    def store(piece, first):
        for k in range(piece.shape[0]):
            in_ref[first + k] = piece[k, :, :wide]
            start = lax.rem(places_ref[1] + first + k, n_col) * features
            for i in range(n_out):
                place = pl.multiple_of(start + i * narrow, narrow)
                out_ref[:, pl.ds(place, narrow)] = piece[
                    k, i * out_rows : (i + 1) * out_rows, wide:
                ]

    for d in range(3):

        @pl.when(pl.program_id(0) == d)
        def _():
            store(pieces[d], 0)

    @pl.when(pl.program_id(0) == 3)
    def _():
        store(pieces[3], 0)
        store(pieces[4], pieces[3].shape[0])


def first_weights(dp, here, pieces, wide, n_out):
    n_col, in_rows, columns = pieces[0].shape
    out_rows = in_rows // n_out
    features = n_out * (columns - wide)
    whole = [
        pl.BlockSpec(piece.shape, lambda step, places: (0, 0, 0)) for piece in pieces
    ]
    return pl.pallas_call(
        functools.partial(first_weights_kernel, (n_col, n_out, out_rows, wide)),
        grid_spec=pltpu.PrefetchScalarGridSpec(
            num_scalar_prefetch=1,
            grid=(4,),
            in_specs=whole,
            out_specs=[
                pl.BlockSpec(
                    (n_col, in_rows, wide), lambda step, places: (0, places[0] ^ step, 0)
                ),
                pl.BlockSpec(
                    (out_rows, n_col * features), lambda step, places: (places[0] ^ step, 0)
                ),
            ],
        ),
        out_shape=[
            jax.ShapeDtypeStruct((n_col, 4 * in_rows, wide), BF),
            jax.ShapeDtypeStruct((4 * out_rows, n_col * features), BF),
        ],
        compiler_params=pltpu.CompilerParams(vmem_limit_bytes=32 << 20),
        cost_estimate=pl.CostEstimate(
            flops=0, bytes_accessed=8 * n_col * in_rows * columns * 2, transcendentals=0
        ),
        name="first_weights",
    )(jnp.stack([dp, here]).astype(jnp.int32), *pieces)


def pair_gradients_kernel(all_ref, gate_ref, up_ref):
    hidden = all_ref.shape[4]
    for k in range(all_ref.shape[1]):
        place = slice(k * hidden, (k + 1) * hidden)
        gate_ref[:, place] = all_ref[0, k, 0].astype(F32)
        up_ref[:, place] = all_ref[0, k, 1].astype(F32)


def pair_gradients(gathered):
    n_dp, n_col, pair, rows, hidden = gathered.shape
    cut = 2 if rows % 32 == 0 else 1
    side = pl.BlockSpec((rows // cut, n_col * hidden), lambda p, i: (p * cut + i, 0))
    return pl.pallas_call(
        pair_gradients_kernel,
        grid=(n_dp, cut),
        in_specs=[
            pl.BlockSpec((1, n_col, pair, rows // cut, hidden), lambda p, i: (p, 0, 0, i, 0))
        ],
        out_specs=[side, side],
        out_shape=[jax.ShapeDtypeStruct((n_dp * rows, n_col * hidden), F32)] * 2,
        compiler_params=pltpu.CompilerParams(vmem_limit_bytes=56 << 20),
        cost_estimate=pl.CostEstimate(
            flops=0, bytes_accessed=6 * math.prod(gathered.shape), transcendentals=0
        ),
        name="pair_gradients",
    )(gathered)


def down_gradients_kernel(all_ref, down_ref):
    down_ref[...] = all_ref[...].astype(F32)


def down_gradients(gathered):
    n_dp, n_col, rows, features = gathered.shape
    block = (1, 1, rows, features)
    whole = pl.pallas_call(
        down_gradients_kernel,
        grid=(n_dp, n_col),
        in_specs=[pl.BlockSpec(block, lambda p, z: (p, z, 0, 0))],
        out_specs=pl.BlockSpec(block, lambda p, z: (z, p, 0, 0)),
        out_shape=jax.ShapeDtypeStruct((n_col, n_dp, rows, features), F32),
        compiler_params=pltpu.CompilerParams(vmem_limit_bytes=56 << 20),
        cost_estimate=pl.CostEstimate(
            flops=0, bytes_accessed=6 * math.prod(gathered.shape), transcendentals=0
        ),
        name="down_gradients",
    )(gathered)
    return whole.reshape(-1, features)


def last_gradients_kernel(n_out, places_ref, *refs):
    pieces, outs = refs[:-4], refs[-4:]
    n_col = pieces[0].shape[0]
    features = outs[3].shape[3]
    head_cols = outs[0].shape[1] // n_col
    narrow = features // n_out

    def store(piece, first):
        rows = piece.shape[1] // n_out
        for k in range(piece.shape[0]):
            source = lax.rem(places_ref[1] + first + k, n_col)
            place = pl.ds(pl.multiple_of(source * head_cols, head_cols), head_cols)
            for i in range(3):
                outs[i][:, place] = piece[k, :, i * head_cols : (i + 1) * head_cols].astype(F32)
            for i in range(n_out):
                outs[3][source, 0, :, i * narrow : (i + 1) * narrow] = piece[
                    k, i * rows : (i + 1) * rows, 3 * head_cols :
                ].astype(F32)

    for d in range(3):

        @pl.when(pl.program_id(0) == d)
        def _():
            store(pieces[d], 0)

    @pl.when(pl.program_id(0) == 3)
    def _():
        store(pieces[3], 0)
        store(pieces[4], pieces[3].shape[0])


def last_gradients(dp, here, pieces, head_cols, n_out):
    n_col, rows, columns = pieces[0].shape
    features = n_out * (columns - 3 * head_cols)
    side = pl.BlockSpec(
        (rows, n_col * head_cols), lambda step, places: (places[0] ^ step, 0)
    )
    side_shape = jax.ShapeDtypeStruct((4 * rows, n_col * head_cols), F32)
    *sides, out = pl.pallas_call(
        functools.partial(last_gradients_kernel, n_out),
        grid_spec=pltpu.PrefetchScalarGridSpec(
            num_scalar_prefetch=1,
            grid=(4,),
            in_specs=[
                pl.BlockSpec(piece.shape, lambda step, places: (0, 0, 0)) for piece in pieces
            ],
            out_specs=[side] * 3
            + [
                pl.BlockSpec(
                    (n_col, 1, rows // n_out, features),
                    lambda step, places: (0, places[0] ^ step, 0, 0),
                )
            ],
        ),
        out_shape=[side_shape] * 3
        + [jax.ShapeDtypeStruct((n_col, 4, rows // n_out, features), F32)],
        compiler_params=pltpu.CompilerParams(vmem_limit_bytes=56 << 20),
        cost_estimate=pl.CostEstimate(
            flops=0, bytes_accessed=24 * n_col * rows * columns, transcendentals=0
        ),
        name="last_gradients",
    )(jnp.stack([dp, here]).astype(jnp.int32), *pieces)
    return sides, out.reshape(-1, features)


def own_block_kernel(here_ref, *refs):
    blocks, whole = refs[:-1], refs[-1]
    for step, block in enumerate(blocks):

        @pl.when(pl.program_id(0) == step)
        def _():
            whole[...] = block[...]


def own_rows(ring, blocks):
    size = len(blocks)
    rows, columns = blocks[0].shape[0] // size, blocks[0].shape[1]
    return pl.pallas_call(
        own_block_kernel,
        grid_spec=pltpu.PrefetchScalarGridSpec(
            num_scalar_prefetch=1,
            grid=(size,),
            in_specs=[pl.BlockSpec((rows, columns), lambda step, here: (here[0], 0))] * size,
            out_specs=pl.BlockSpec(
                (rows, columns), lambda step, here: (0, lax.rem(here[0] + step, size))
            ),
        ),
        out_shape=jax.ShapeDtypeStruct((rows, columns * size), blocks[0].dtype),
        compiler_params=pltpu.CompilerParams(vmem_limit_bytes=32 << 20),
        name="own_rows",
    )(ring.here.astype(jnp.int32)[None], *blocks)


def from_here(ring, values, size, axis):
    twice = jnp.concatenate([values, values], axis=axis)
    return lax.dynamic_slice_in_dim(twice, ring.here * size, size * ring.size, axis)


def to_order(ring, values, size, axis):
    twice = jnp.concatenate([values, values], axis=axis)
    start = lax.rem(ring.size - ring.here, ring.size) * size
    return lax.dynamic_slice_in_dim(twice, start, size * ring.size, axis)


def exchange(ring, block_for):
    return [ring.fetch(block_for(ring.at(-step)), step) for step in range(ring.size)]


def gather_tokens(row, col, values, early=(), late=()):
    near, early, late = gather_near(col, values, early, late)
    blocks = [
        jnp.concatenate([row.fetch(block, j) for j in range(row.size)], axis=0)
        for block in near
    ]
    return blocks, early, late


def sum_rows(row, partial):
    size = partial.shape[0] // row.size
    total = partial[:size]
    for j in range(1, row.size):
        total = total + row.give(partial[j * size : (j + 1) * size].astype(BF), j).astype(F32)
    return total


def sum_all(row, col, values, block_for):
    length = values.shape[1]
    size = length // row.size
    total = values
    for j in range(1, row.size):
        total = total + jnp.roll(row.fetch(values, j), j * size, axis=1)
    came = [
        col.fetch(jnp.concatenate([total, block_for(col.at(-k))], axis=1), k)
        for k in range(col.size)
    ]
    result = came[0]
    for part in came[1:]:
        result = result + part
    return result[:, :length], [part[:, length:] for part in came]


def rms_scale(values):
    return lax.rsqrt(jnp.mean(values * values, axis=1, keepdims=True) + EPSILON)


def rms_back(grad_normed, branch, scales, gains):
    weighted = grad_normed * gains
    inner = jnp.mean(weighted * branch, axis=1, keepdims=True)
    grad_branch = scales * weighted - branch * (scales * scales * scales) * inner
    grad_gains = jnp.sum(grad_normed * branch * scales, axis=0)
    return grad_branch, grad_gains


def turn(values, cosine, sine):
    return values * cosine + pltpu.roll(values, values.shape[-1] // 2, 1) * sine


def kernel_dot(a, b, dims):
    return lax.dot_general(a, b, (dims, ((), ())), preferred_element_type=F32)


def softmax_parts(queries, keys, doc_rows, slot_rows, lines):
    scores = kernel_dot(queries, keys, ((1,), (1,))) * (HEAD**-0.5)
    allowed = (doc_rows == lines[2:3, :]) & (lines[3:4, :] <= slot_rows)
    scores = jnp.where(allowed, scores, MASKED)
    weights = jnp.exp(scores - jnp.max(scores, axis=1, keepdims=True))
    return weights * (1.0 / jnp.sum(weights, axis=1, keepdims=True))


def place_of(block, here, n_col):
    row, index = block // n_col, block % n_col
    step = lax.rem(index + n_col - here, n_col)
    if n_col == 4:
        step = jnp.where((here == 3) & (step % 2 == 1), 4 - step, step)
    return step, row


def forward_kernel(
    sizes,
    here_ref,
    query_ref,
    key_ref,
    value_ref,
    lines_ref,
    query_gain_ref,
    key_gain_ref,
    cosine_ref,
    sine_ref,
    query_rot_ref,
    key_rot_ref,
    value_low_ref,
    mixture_ref,
):
    n_row, n_col, small, large = sizes
    cosine, sine, lines = cosine_ref[...], sine_ref[...], lines_ref[...]
    columns = jnp.transpose(lines)
    normed = query_ref[...] * columns[:, 0:1] * query_gain_ref[...]
    query_rot_ref[...] = turn(normed, cosine, sine).astype(BF)
    normed = key_ref[...] * columns[:, 1:2] * key_gain_ref[...]
    key_rot_ref[...] = turn(normed, cosine, sine).astype(BF)
    value_low_ref[...] = value_ref[...].astype(BF)
    keys, values = key_rot_ref[...], value_low_ref[...]
    for start in range(0, query_ref.shape[0], large):
        rows = slice(start, start + large)
        chances = softmax_parts(
            query_rot_ref[rows, :], keys, columns[rows, 2:3], columns[rows, 3:4], lines
        )
        mixture = kernel_dot(chances.astype(BF), values, ((1,), (0,))).astype(BF)
        for inner in range(0, large, small):
            step, row = place_of((start + inner) // small, here_ref[0], n_col)
            place = pl.multiple_of((step * n_row + row) * small, small)
            mixture_ref[pl.ds(place, small), :] = mixture[inner : inner + small]


def backward_kernel(
    sizes,
    here_ref,
    query_ref,
    key_ref,
    lines_ref,
    query_gain_ref,
    key_gain_ref,
    cosine_ref,
    sine_ref,
    query_rot_ref,
    key_rot_ref,
    value_low_ref,
    grad_ref,
    query_weighted_ref,
    key_weighted_ref,
    grad_value_ref,
    inner_ref,
    query_gain_grad_ref,
    key_gain_grad_ref,
    key_total,
    value_total,
):
    n_row, n_col, small, large = sizes
    cosine, sine, lines = cosine_ref[...], sine_ref[...], lines_ref[...]
    columns = jnp.transpose(lines)
    keys, values = key_rot_ref[...], value_low_ref[...]
    factor = HEAD**-0.5
    for start in range(0, query_ref.shape[0], large):
        rows = slice(start, start + large)
        queries = query_rot_ref[rows, :]
        grads = []
        for inner in range(0, large, small):
            step, row = place_of((start + inner) // small, here_ref[0], n_col)
            place = pl.multiple_of((step * n_row + row) * small, small)
            grads.append(grad_ref[pl.ds(place, small), :])
        grads = jnp.concatenate(grads, axis=0)
        chances = softmax_parts(
            queries, keys, columns[rows, 2:3], columns[rows, 3:4], lines
        )
        value_part = kernel_dot(chances.astype(BF), grads, ((0,), (0,)))
        grad_chances = kernel_dot(grads, values, ((1,), (1,)))
        inner = jnp.sum(chances * grad_chances, axis=1, keepdims=True)
        grad_scores = (chances * (grad_chances - inner)).astype(BF)
        query_weighted_ref[rows, :] = kernel_dot(grad_scores, keys, ((1,), (0,))) * factor
        key_part = kernel_dot(grad_scores, queries, ((0,), (0,))) * factor
        if start == 0:
            value_total[...] = value_part
            key_total[...] = key_part
        else:
            value_total[...] += value_part
            key_total[...] += key_part
    grad_value_ref[...] = value_total[...].astype(BF)
    ones = jnp.ones((8, HEAD), F32)
    inners = []
    for grad, raw_ref, which, gain_ref, weighted_ref, gain_grad_ref in (
        (
            query_weighted_ref[...],
            query_ref,
            0,
            query_gain_ref,
            query_weighted_ref,
            query_gain_grad_ref,
        ),
        (
            key_total[...],
            key_ref,
            1,
            key_gain_ref,
            key_weighted_ref,
            key_gain_grad_ref,
        ),
    ):
        unturned = turn(grad, cosine, -sine)
        raw = raw_ref[...]
        gain_grad_ref[0] = jnp.sum(
            unturned * raw * columns[:, which : which + 1], axis=0, keepdims=True
        )
        weighted = unturned * gain_ref[...]
        weighted_ref[...] = weighted
        inners.append(
            lax.dot_general(
                ones,
                weighted * raw,
                (((1,), (1,)), ((), ())),
                precision=lax.Precision.HIGHEST,
                preferred_element_type=F32,
            )
        )
    which = lax.broadcasted_iota(jnp.int32, inner_ref.shape, 0)
    both = jnp.where(which == 0, inners[0], inners[1])

    @pl.when(pl.program_id(0) == 0)
    def _():
        inner_ref[...] = both

    @pl.when(pl.program_id(0) > 0)
    def _():
        inner_ref[...] += both


def head_specs(length):
    return {
        "head": lambda first: pl.BlockSpec(
            (length, HEAD), lambda h, here, first=first: (0, first + h)
        ),
        "gain": pl.BlockSpec((1, HEAD), lambda h, here: (0, h)),
        "lines": pl.BlockSpec((8, length), lambda h, here: (0, 0)),
        "table": pl.BlockSpec((length, HEAD), lambda h, here: (0, 0)),
        "head_line": pl.BlockSpec((1, 1, HEAD), lambda h, here: (h, 0, 0)),
    }


def attend_forward(row, col, raw, lines, gains, tables):
    length = raw.shape[0]
    heads = raw.shape[1] // (3 * HEAD)
    spec = head_specs(length)
    small = length // (row.size * col.size)
    wide = jax.ShapeDtypeStruct((length, heads * HEAD), BF)
    return pl.pallas_call(
        functools.partial(
            forward_kernel, (row.size, col.size, small, max(small, min(256, length)))
        ),
        grid_spec=pltpu.PrefetchScalarGridSpec(
            num_scalar_prefetch=1,
            grid=(heads,),
            in_specs=[spec["head"](0), spec["head"](heads), spec["head"](2 * heads)]
            + [spec["lines"]]
            + [spec["gain"]] * 2
            + [spec["table"]] * 2,
            out_specs=[spec["head"](0)] * 4,
        ),
        out_shape=[wide] * 4,
        compiler_params=pltpu.CompilerParams(vmem_limit_bytes=56 << 20),
        cost_estimate=pl.CostEstimate(
            flops=heads * 4 * length * length * HEAD,
            bytes_accessed=heads * length * HEAD * 20,
            transcendentals=heads * length * length,
        ),
        name="attend_forward",
    )(col.here.astype(jnp.int32)[None], raw, raw, raw, lines, *gains, *tables)


def attend_backward(row, col, raw, lines, gains, tables, saved, grad):
    length = raw.shape[0]
    heads = raw.shape[1] // (3 * HEAD)
    spec = head_specs(length)
    small = length // (row.size * col.size)
    wide = jax.ShapeDtypeStruct((length, heads * HEAD), F32)
    low = jax.ShapeDtypeStruct((length, heads * HEAD), BF)
    flat = jax.ShapeDtypeStruct((heads, 1, HEAD), F32)
    return pl.pallas_call(
        functools.partial(
            backward_kernel, (row.size, col.size, small, max(small, min(256, length)))
        ),
        grid_spec=pltpu.PrefetchScalarGridSpec(
            num_scalar_prefetch=1,
            grid=(heads,),
            in_specs=[spec["head"](0), spec["head"](heads), spec["lines"]]
            + [spec["gain"]] * 2
            + [spec["table"]] * 2
            + [spec["head"](0)] * 4,
            out_specs=[spec["head"](0)] * 3 + [spec["lines"]] + [spec["head_line"]] * 2,
            scratch_shapes=[pltpu.VMEM((length, HEAD), F32)] * 2,
        ),
        out_shape=[wide, wide, low, jax.ShapeDtypeStruct((8, length), F32), flat, flat],
        compiler_params=pltpu.CompilerParams(vmem_limit_bytes=56 << 20),
        cost_estimate=pl.CostEstimate(
            flops=heads * 10 * length * length * HEAD,
            bytes_accessed=heads * length * HEAD * 30,
            transcendentals=heads * length * length,
        ),
        name="attend_backward",
    )(col.here.astype(jnp.int32)[None], raw, raw, lines, *gains, *tables, *saved, grad)


def device_program(sizes):
    n_dp, n_row, n_col = sizes["dp"], sizes["row"], sizes["col"]

    def per_device(
        layer_input,
        doc_ids,
        positions,
        w_query,
        w_key,
        w_value,
        w_out,
        w_gate,
        w_up,
        w_down,
        gain_query,
        gain_key,
        gain_attn,
        gain_ffn,
        grad_output,
    ):
        row, col = Ring("row", n_row), Ring("col", n_col)
        dp = lax.axis_index("dp")
        length = doc_ids.shape[0]
        row_tokens = layer_input.shape[0]
        own_tokens = row_tokens // n_col
        features = layer_input.shape[1]
        width = features * n_col
        head_cols = w_query.shape[1] // n_col
        hidden_cols = w_gate.shape[1] // n_col
        in_rows = features // n_dp
        out_rows = head_cols // n_dp
        down_rows = hidden_cols // n_dp

        def gather_dp(values):
            return lax.all_gather(values, "dp", axis=0, tiled=True)

        steps = [1 << bit for bit in range(n_dp.bit_length() - 1)]

        def partner(values, step):
            return lax.ppermute(values, "dp", [(i, i ^ step) for i in range(n_dp)])

        class GroupSum:
            def __init__(self, block_for):
                blocks = [block_for(dp ^ d) for d in range(n_dp)]
                self.halves = [
                    (dict(enumerate(left for left, _ in blocks)), list(steps)),
                    (dict(enumerate(right for _, right in blocks)), list(steps[::-1])),
                ]
                self.came = None
                self.send()

            def send(self):
                self.came = []
                for blocks, order in self.halves:
                    given = [blocks[d] for d in sorted(blocks) if d & order[0]]
                    self.came.append(partner(jnp.stack(given), order[0]))

            def land(self, chain, more=True):
                self.came, chain = lax.optimization_barrier((self.came, chain))
                for (blocks, order), came in zip(self.halves, self.came):
                    step = order.pop(0)
                    for place, d in enumerate([d for d in sorted(blocks) if d & step]):
                        kept = blocks[d ^ step].astype(F32) + came[place].astype(F32)
                        blocks[d ^ step] = kept.astype(BF)
                        del blocks[d]
                if self.halves[0][1]:
                    self.send()
                return chain

            def finish(self, chain):
                while self.halves[0][1]:
                    chain = self.land(chain)
                return [blocks[0] for blocks, _ in self.halves], chain

        def gather_four(values, beside=()):
            half = values.shape[0] // 2
            one, two = partner(values, 1), partner(values, 2)
            (one, two), beside = lax.optimization_barrier(((one, two), beside))
            far = [partner(one[:half], 2), partner(two[half:], 1)]
            return [[values], [one], [two], far], beside

        def halves_of(values):
            half = values.shape[-1] // 2
            return values[..., :half], values[..., half:]

        def qkv_block(index):
            return jnp.concatenate(
                [
                    lax.dynamic_slice(
                        w, (dp * in_rows, index * head_cols), (in_rows, head_cols)
                    )
                    for w in (w_query, w_key, w_value)
                ],
                axis=1,
            )

        def gate_up_block(index):
            return jnp.stack(
                [
                    lax.dynamic_slice(
                        w, (dp * in_rows, index * hidden_cols), (in_rows, hidden_cols)
                    )
                    for w in (w_gate, w_up)
                ]
            )

        def out_block(index):
            return lax.dynamic_slice_in_dim(
                w_out, index * head_cols + dp * out_rows, out_rows, 0
            )

        def down_block(index):
            return lax.dynamic_slice_in_dim(
                w_down, index * hidden_cols + dp * down_rows, down_rows, 0
            )

        def first_block(index):
            out = out_block(index).reshape(out_rows, n_out, -1).swapaxes(0, 1)
            return jnp.concatenate([qkv_block(index), out.reshape(in_rows, -1)], axis=1)

        n_out = in_rows // out_rows
        first_parts = exchange(col, first_block)

        turned_docs = from_here(row, doc_ids, row_tokens, 0)
        turned_positions = from_here(row, positions, row_tokens, 0)
        slots = lax.rem(jnp.arange(length) + row.here * row_tokens, length)
        tables = rope_tables(turned_positions)
        first_parts, layer_input = lax.optimization_barrier((first_parts, layer_input))
        near, _, tables = gather_col(col, layer_input, (), tables)
        if n_dp == 4:
            pieces, _ = gather_four(jnp.stack(first_parts))
            pieces = sum(pieces, [])
            w_qkv, w_out_all = first_weights(dp, col.here, pieces, 3 * head_cols, n_out)
        else:
            first = gather_dp(jnp.stack(first_parts)[None])
            w_qkv = first[..., : 3 * head_cols].swapaxes(0, 1).reshape(n_col, features, -1)
            w_out_all = first[..., 3 * head_cols :].reshape(n_dp, n_col, n_out, out_rows, -1)
            w_out_all = w_out_all.transpose(0, 3, 1, 2, 4).reshape(head_cols, width)
            w_out_all = to_order(col, w_out_all, features, 1)
        w_down = after(w_down, near)
        down_parts = exchange(col, down_block)
        w_qkv = [w_qkv[k] for k in range(n_col)]
        input_rows = [
            jnp.concatenate([row.fetch(block, j) for j in range(n_row)], axis=0)
            for block in near
        ]
        own_input = own_rows(col, near).astype(F32)

        raw = sum(dot(rows, w) for rows, w in zip(input_rows, w_qkv))
        query_raw = raw[:, :head_cols]
        key_raw = raw[:, head_cols : 2 * head_cols]
        squares = jnp.stack(
            [jnp.sum(query_raw * query_raw, axis=1), jnp.sum(key_raw * key_raw, axis=1)]
        )
        squares, down_parts = lax.optimization_barrier((squares, down_parts))
        down_parts = assemble(col, down_parts, 1)
        w_gate, w_up = after((w_gate, w_up), down_parts)
        gate_up_parts = exchange(col, gate_up_block)
        gains = jnp.stack([gain_attn, gain_ffn])
        squares, gains = sum_all(row, col, squares, lambda index: gains)
        squares, w_out_all, gate_up_parts[1::2] = lax.optimization_barrier(
            (squares, w_out_all, gate_up_parts[1::2])
        )
        w_down_all = gather_dp(down_parts)
        gains = assemble(col, gains, 1)
        gain_attn_all, gain_ffn_all = gains[0:1], gains[1:2]

        scales = lax.rsqrt(squares / width + EPSILON)
        query_scale, key_scale = scales[0][:, None], scales[1][:, None]
        head_gains = (gain_query[None, :], gain_key[None, :])
        marks = jnp.stack([turned_docs, slots]).astype(F32)
        lines = jnp.concatenate([scales, marks, jnp.zeros((4, length), F32)], axis=0)
        *saved, mixture = attend_forward(row, col, raw, lines, head_gains, tables)
        attended = []
        for k in range(n_col):
            total, *others = (
                dot(block_at(mixture, k * n_row + j, own_tokens, 0), w_out_all)
                for j in range(n_row)
            )
            for j, other in enumerate(others):
                total = total + row.give(other.astype(BF), j + 1).astype(F32)
            attended.append(total)
        gate_up_parts, attended = lax.optimization_barrier((gate_up_parts, attended))
        gate_up_parts = assemble(
            col, [part[:, None] for part in after(gate_up_parts, w_down_all)], 1
        )
        gate_up_parts, attended = lax.optimization_barrier((gate_up_parts, attended))
        attended, _, _ = reduce_near(col, attended)
        w_gate_up = lax.all_gather(gate_up_parts[:, :, None], "dp", axis=2, tiled=True)
        w_gate_up = w_gate_up.reshape(2, width, hidden_cols)
        attn_scale = rms_scale(attended)
        hidden_state = own_input + attended * attn_scale * gain_attn_all

        state_low, grad_output = lax.optimization_barrier((hidden_state.astype(BF), grad_output))
        cotangent = exchange(
            col, lambda index: block_at(grad_output, index, own_tokens, 0)
        )
        state_rows, _, (w_gate_up, cotangent) = gather_tokens(
            row, col, state_low, (), (w_gate_up, cotangent)
        )
        cotangent = assemble(col, cotangent, 1).astype(F32)
        w_gate, w_up = w_gate_up[0], w_gate_up[1]
        kept, activated = [], []
        for block in state_rows:
            pair = lax.optimization_barrier((dot(block, w_gate), dot(block, w_up)))
            gate_values, up_values = pair
            kept.append(pair)
            activated.append((gate_values * jax.nn.sigmoid(gate_values) * up_values).astype(BF))
        lowered = [sum_rows(row, dot(block, w_down_all)) for block in activated]
        lowered, _, _ = reduce_near(col, lowered)
        ffn_scale = rms_scale(lowered)
        own_output = (hidden_state + lowered * ffn_scale * gain_ffn_all).astype(BF)

        grad_lowered, grad_gain_ffn = rms_back(cotangent, lowered, ffn_scale, gain_ffn_all)
        lowered_rows, _, _ = gather_tokens(row, col, grad_lowered.astype(BF))
        gate_grads, up_grads, state_part = [], [], []
        for block, (gate_values, up_values) in zip(lowered_rows, kept):
            sigmoid_gate = jax.nn.sigmoid(gate_values)
            grad_activated = dot_nt(block, w_down_all)
            grad_gate = (
                grad_activated
                * up_values
                * (sigmoid_gate * (1.0 + gate_values * (1.0 - sigmoid_gate)))
            )
            grad_up = grad_activated * (gate_values * sigmoid_gate)
            pair = lax.optimization_barrier((grad_gate.astype(BF), grad_up.astype(BF)))
            gate_grads.append(pair[0])
            up_grads.append(pair[1])
            state_part.append(sum_rows(row, dot_nt(pair[0], w_gate) + dot_nt(pair[1], w_up)))
        wide = (
            jnp.concatenate(activated),
            jnp.concatenate(lowered_rows),
            jnp.concatenate(state_rows),
            jnp.concatenate(gate_grads),
            jnp.concatenate(up_grads),
        )
        activated, lowered_rows, state_rows, gate_grads, up_grads = after(wide, state_part)
        grad_w_down = dot_tn(activated, lowered_rows).astype(BF)
        down_sum = GroupSum(
            lambda index: halves_of(block_at(grad_w_down, index, down_rows, 0))
        )
        gate_up_grads = [
            dot_tn(after(state_rows, grad_w_down), grads)
            .astype(BF)
            .reshape(n_col, n_dp, in_rows, hidden_cols)
            for grads in (gate_grads, up_grads)
        ]
        state_part, _, gate_up_grads = reduce_near(
            col, state_part, grad_w_down, gate_up_grads
        )
        gate_up_sum = GroupSum(
            lambda index: [
                lax.dynamic_index_in_dim(grads, index, 1, False) for grads in gate_up_grads
            ]
        )
        state_part = down_sum.land(state_part)
        grad_state = cotangent + state_part
        grad_attended, grad_gain_attn = rms_back(
            grad_state, attended, attn_scale, gain_attn_all
        )
        attended_rows, gate_up_sum.came, _ = gather_tokens(
            row, col, grad_attended.astype(BF), gate_up_sum.came
        )
        gate_up_sum.land(())
        down_parts, attended_rows = down_sum.finish(attended_rows)
        down_parts = jnp.concatenate(down_parts, axis=1)
        down_parts = exchange(
            col, lambda index, whole=down_parts: block_at(whole, index, features, 1)
        )

        grad_mixture = [dot_nt(block, w_out_all).astype(BF) for block in attended_rows]
        attended_rows = jnp.concatenate(attended_rows)
        grad_mixture = jnp.concatenate(grad_mixture)
        (
            query_weighted,
            key_weighted,
            grad_value,
            inner,
            grad_gain_query,
            grad_gain_key,
        ) = attend_backward(row, col, raw, lines, head_gains, tables, saved, grad_mixture)
        gate_up_sum.came, down_parts, inner, mixture = lax.optimization_barrier(
            (gate_up_sum.came, down_parts, inner, mixture)
        )
        out_grads = dot_tn(mixture, attended_rows).astype(BF)
        out_grads = out_grads.reshape(n_dp, out_rows, n_col, n_out, -1)
        out_grads = out_grads.transpose(2, 0, 3, 1, 4).reshape(n_col, n_dp, in_rows, -1)
        out_grads = from_here(col, out_grads, 1, 0)
        down_back = assemble(col, [part[None] for part in down_parts], 0)
        down_all = gather_dp(down_back[None])
        small = jnp.stack([grad_gain_attn, grad_gain_ffn])
        inner, small = sum_all(row, col, inner[:2], lambda index: block_at(small, index, features, 1))
        inner, out_grads = lax.optimization_barrier((inner, out_grads))
        inner = inner / width
        gate_up_sum.came, inner = lax.optimization_barrier((gate_up_sum.came, inner))
        gate_up_sum, _ = gate_up_sum.finish(())
        gate_up_whole = jnp.stack(gate_up_sum)
        gate_up_parts = exchange(
            col, lambda index: lax.dynamic_index_in_dim(gate_up_whole, index, 1, False)
        )
        small = sum(small[1:], small[0])
        head_gain_grads = [grad_gain_query.reshape(-1), grad_gain_key.reshape(-1)]
        small = sum((row.fetch(small, j) for j in range(1, n_row)), small)
        small = jnp.concatenate([small, jnp.stack(head_gain_grads)], axis=1)
        grad_query = (
            query_scale * query_weighted
            - query_raw * (query_scale * query_scale * query_scale) * inner[0][:, None]
        )
        grad_key = (
            key_scale * key_weighted
            - key_raw * (key_scale * key_scale * key_scale) * inner[1][:, None]
        )
        grad_qkv = jnp.concatenate(
            [grad_query.astype(BF), grad_key.astype(BF), grad_value], axis=1
        )
        small, grad_qkv = lax.optimization_barrier((small, grad_qkv))
        grad_w_qkv = [dot_tn(rows, grad_qkv).astype(BF) for rows in input_rows]
        for step in steps:
            came = partner(small, step)
            if step == steps[0]:
                came, grad_w_qkv[0] = lax.optimization_barrier((came, grad_w_qkv[0]))
            small = small + came
        grad_w_qkv = jnp.stack(grad_w_qkv)
        qkv_grads = grad_w_qkv.reshape(n_col, n_dp, in_rows, 3 * head_cols)
        def last_block(index):
            return halves_of(
                jnp.concatenate(
                    [
                        lax.dynamic_index_in_dim(grads, index, 1, False)
                        for grads in (qkv_grads, out_grads)
                    ],
                    axis=-1,
                )
            )

        qkv_grads, out_grads, small, grad_qkv = lax.optimization_barrier(
            (qkv_grads, out_grads, small, grad_qkv)
        )
        last_sum = GroupSum(last_block)
        input_part = [dot_nt(grad_qkv, w) for w in w_qkv]
        gate_up_parts, last_sum.came, input_part = lax.optimization_barrier(
            (gate_up_parts, last_sum.came, input_part)
        )
        last_sum.land(())
        gate_up_back = assemble(
            col, [part[None] for part in after(gate_up_parts, down_back)], 0
        )
        gate_up_all = gather_dp(gate_up_back[None])
        input_part = [sum_rows(row, partial) for partial in input_part]
        gate_up_back, input_part = lax.optimization_barrier((gate_up_back, input_part))
        last_sum, _ = last_sum.finish(())
        last_sum = jnp.concatenate(last_sum, axis=-1)
        last_parts = [col.fetch(last_sum[-k % n_col], k) for k in range(n_col)]
        grad_w_down = down_gradients(down_all)
        grad_input, (last_parts, grad_w_down), _ = reduce_near(
            col, by_arrival(col, input_part), (last_parts, grad_w_down)
        )
        own_output, grad_state = after((own_output, grad_state), last_parts)
        own_state = grad_state.astype(BF)
        output_parts = exchange(col, lambda index: block_at(own_output, index, features, 1))
        state_parts = exchange(col, lambda index: block_at(own_state, index, features, 1))
        grad_w_wide = (
            *pair_gradients(gate_up_all),
            grad_w_down,
        )
        if n_dp == 4:
            pieces, (output_parts, state_parts) = gather_four(
                jnp.stack(last_parts), (output_parts, state_parts)
            )
            pieces, grad_w_wide = lax.optimization_barrier((pieces, grad_w_wide))
            (grad_w_query, grad_w_key, grad_w_value), grad_w_out = last_gradients(
                dp, col.here, sum(pieces, []), head_cols, n_out
            )
        else:
            last_parts = assemble(col, [part[None] for part in last_parts], 0)
            last_all = gather_dp(after(last_parts, gate_up_all)[None])

            def columns_of(whole):
                return jnp.concatenate(
                    [whole[:, k].reshape(features, -1) for k in range(n_col)], axis=1
                ).astype(F32)

            grad_w_query, grad_w_key, grad_w_value = (
                columns_of(last_all[..., i * head_cols : (i + 1) * head_cols])
                for i in range(3)
            )
            out_all = last_all[..., 3 * head_cols :].reshape(
                n_dp, n_col, n_out, out_rows, -1
            )
            grad_w_out = out_all.transpose(1, 0, 3, 2, 4).reshape(w_out.shape).astype(F32)
        grad_w_gate, grad_w_up, grad_w_down = grad_w_wide
        layer_output = assemble(col, output_parts, 0)
        grad_input = grad_input + assemble(col, state_parts, 0).astype(F32)
        return (
            layer_output,
            grad_input,
            grad_w_query,
            grad_w_key,
            grad_w_value,
            grad_w_out,
            grad_w_gate,
            grad_w_up,
            grad_w_down,
            small[0, features:],
            small[1, features:],
            small[0, :features],
            small[1, :features],
        )

    return per_device


def solution(mesh):
    in_specs = (
        P(("dp", "row"), "col"),
        P("dp"),
        P("dp"),
        P("col", "row"),
        P("col", "row"),
        P("col", "row"),
        P("row", "col"),
        P("col", "row"),
        P("col", "row"),
        P("row", "col"),
        P(("row", "col")),
        P(("row", "col")),
        P("col"),
        P("col"),
        P(("dp", "row"), "col"),
    )
    out_specs = (
        P(("dp", "row"), "col"),
        P(("dp", "row"), "col"),
        P("col", "row"),
        P("col", "row"),
        P("col", "row"),
        P("row", "col"),
        P("col", "row"),
        P("col", "row"),
        P("row", "col"),
        P(("row", "col")),
        P(("row", "col")),
        P("col"),
        P("col"),
    )
    return jax.shard_map(
        device_program(dict(mesh.shape)),
        mesh=mesh,
        in_specs=in_specs,
        out_specs=out_specs,
        check_vma=False,
    )
```
